32 devices in a mesh: dp: 4 (over y, x), index: 8 (over z, core).
Axes of the slice: x: 2, y: 2, z: 4, core: 2. Of those that a mesh axis runs over, the one named last changes fastest.
Arguments:
- tokens: bfloat16 [16384, 768], P(('dp', 'index')), may hold values from -6 to 6
- upstream: bfloat16 [16384, 768], P(('dp', 'index')), may hold values from -0.119628906 to 0.119628906
- w_query: bfloat16 [768, 768], replicated, may hold values from -0.21875 to 0.21875
- w_key: bfloat16 [768, 768], replicated, may hold values from -0.21875 to 0.21875
- w_value: bfloat16 [768, 768], replicated, may hold values from -0.21875 to 0.21875
- w_out: bfloat16 [768, 768], replicated, may hold values from -1.75 to 1.75
- w_in: bfloat16 [768, 3072], replicated, may hold values from -0.21875 to 0.21875
- w_hid: bfloat16 [3072, 768], replicated, may hold values from -0.109375 to 0.109375
- b_query: float32 [768], replicated, may hold values from -3 to 3
- b_value: float32 [768], replicated, may hold values from -3 to 3
- b_out: float32 [768], replicated, may hold values from -3 to 3
- b_in: float32 [3072], replicated, may hold values from -3 to 3
- b_hid: float32 [768], replicated, may hold values from -3 to 3
- gain_one: float32 [768], replicated, may hold values from 0.5 to 1.5
- shift_one: float32 [768], replicated, may hold values from -2 to 2
- gain_two: float32 [768], replicated, may hold values from 0.5 to 1.5
- shift_two: float32 [768], replicated, may hold values from -2 to 2
- passages: bfloat16 [16384, 768], P('index'), may hold values from -0.59765625 to 0.59765625
- slots: int32 [128, 10], P('dp'), may hold values from 0 to 16383
- counts: int32 [128], P('dp'), may hold values from 2 to 10
- gen_loglik: float32 [128, 10], P('dp'), may hold values from -18 to -1
Outputs:
- encoded: bfloat16 [16384, 768], P(('dp', 'index'))
- input_grad: bfloat16 [16384, 768], P(('dp', 'index'))
- loss: float32 [], replicated
- entropy: float32 [], replicated
- grad_w_query: float32 [768, 768], P('index')
- grad_w_key: float32 [768, 768], P('index')
- grad_w_value: float32 [768, 768], P('index')
- grad_w_out: float32 [768, 768], P('index')
- grad_w_in: float32 [768, 3072], P('index')
- grad_w_hid: float32 [3072, 768], P('index')
- grad_b_query: float32 [768], P('index')
- grad_b_value: float32 [768], P('index')
- grad_b_out: float32 [768], P('index')
- grad_b_in: float32 [3072], P('index')
- grad_b_hid: float32 [768], P('index')
- grad_gain_one: float32 [768], P('index')
- grad_shift_one: float32 [768], P('index')
- grad_gain_two: float32 [768], P('index')
- grad_shift_two: float32 [768], P('index')
The draws below stay inside these ranges and needn't reach their ends.
Inputs may be any that keep to these rules, and one draw needn't show every extreme that they name: Slot ids name rows of the whole index; slots past a question's count are ignored.
All inputs are finite; a program needn't handle non-finite values.
Results may differ from the reference program's by a relative error of at most 0.018.
Values may be sent and summed in bfloat16 or wider, within the bound.
No kernel may reach another device: no remote copies, remote signals or barrier semaphores. Data moves between devices by JAX's collectives and lax.ppermute only.
A program may use at most 128 MiB of HBM per device.

```python
import math
import jax
import jax.numpy as jnp
from jax import lax

D = 768
HEADS = 12
HDIM = 64
FF = 3072
SEQ = 128
SLOTS = 10
TOKENS = 16384
QUESTIONS = 128
PASSAGES = 16384
N_DP = 4


def draw_gen_loglik(key, part):
    key = jax.random.fold_in(key, 7)
    uniform_part = jax.random.uniform(key, (QUESTIONS, SLOTS), jnp.float32)
    base = 1.0 + 5.0 * uniform_part
    group = (jnp.arange(QUESTIONS) // (QUESTIONS // N_DP)).astype(jnp.float32)
    factor = 1.0 + 2.0 * group / max(N_DP - 1, 1)
    return (-base * factor[:, None]).astype(jnp.float32)


def touch_ends(entries, stream_key, smallest, largest):
    spot = [jax.random.randint(jax.random.fold_in(stream_key, axis), (), 0, length) for axis, length in enumerate(entries.shape)]
    main_axis = entries.shape.index(max(entries.shape))
    next_to = spot[:main_axis] + [(spot[main_axis] + 1) % entries.shape[main_axis]] + spot[main_axis + 1:]
    return entries.at[tuple(spot)].set(smallest).at[tuple(next_to)].set(largest)


def block_levels(rng, dims, shards, smallest, high):
    gain = 1.0
    for position, blocks in shards:
        draws = jax.random.uniform(jax.random.fold_in(jax.random.fold_in(rng, 6), position), (blocks,), jnp.float32, smallest / len(shards), high / len(shards))
        gain = gain * jnp.repeat(jnp.exp(draws), dims[position] // blocks).reshape((-1,) + (1,) * (len(dims) - 1 - position))
    return gain


def centred(rng, extent, deviation, limit, shards=(), held_as=jnp.bfloat16):
    result = jax.random.normal(rng, extent, jnp.float32) * deviation
    if len(shards) > 0:
        result = block_levels(rng, extent, shards, -0.22, 0.18) * result
    return jnp.clip(result, min=-limit, max=limit).astype(held_as)


def setup_inputs(seed: int = 0) -> dict:
    key_list = jax.random.split(jax.random.key(seed), 22)
    tokens = centred(key_list[0], (TOKENS, D), 1.0, 6.0, ((0, 32),))
    upstream = centred(key_list[1], (TOKENS, D), 0.02, 0.119628906, ((0, 32),))
    w_query = centred(key_list[2], (D, D), D ** -0.5, 0.21875)
    w_key = centred(key_list[3], (D, D), D ** -0.5, 0.21875)
    w_value = centred(key_list[4], (D, D), D ** -0.5, 0.21875)
    w_out = centred(key_list[5], (D, D), (D // 64) ** -0.5, 1.75)
    w_in = centred(key_list[6], (D, FF), D ** -0.5, 0.21875)
    w_hid = centred(key_list[7], (FF, D), FF ** -0.5, 0.109375)
    b_query = centred(key_list[8], (D,), 0.5, 3.0, (), jnp.float32)
    b_value = centred(key_list[9], (D,), 0.5, 3.0, (), jnp.float32)
    b_out = centred(key_list[10], (D,), 0.5, 3.0, (), jnp.float32)
    b_in = centred(key_list[11], (FF,), 0.5, 3.0, (), jnp.float32)
    b_hid = centred(key_list[12], (D,), 0.5, 3.0, (), jnp.float32)
    gain_one = jnp.clip(1.0 + 0.1 * jax.random.normal(key_list[13], (D,), jnp.float32), 0.5, 1.5)
    shift_one = centred(key_list[14], (D,), 0.3, 2.0, (), jnp.float32)
    gain_two = jnp.clip(1.0 + 0.1 * jax.random.normal(key_list[15], (D,), jnp.float32), 0.5, 1.5)
    shift_two = centred(key_list[16], (D,), 0.3, 2.0, (), jnp.float32)
    passages = centred(key_list[17], (PASSAGES, D), 0.1, 0.59765625, ((0, 8),))
    slots = touch_ends(jax.random.randint(key_list[18], (QUESTIONS, SLOTS), 0, PASSAGES), jax.random.fold_in(key_list[18], 1), 0, PASSAGES - 1).astype(jnp.int32)
    counts = touch_ends(jax.random.randint(key_list[19], (QUESTIONS,), 2, SLOTS + 1), jax.random.fold_in(key_list[19], 1), 2, SLOTS).astype(jnp.int32)
    gen_loglik = draw_gen_loglik(jax.random.fold_in(key_list[21], 71), 0)
    return dict(tokens=tokens, upstream=upstream, w_query=w_query, w_key=w_key, w_value=w_value, w_out=w_out, w_in=w_in, w_hid=w_hid, b_query=b_query, b_value=b_value, b_out=b_out, b_in=b_in, b_hid=b_hid, gain_one=gain_one, shift_one=shift_one, gain_two=gain_two, shift_two=shift_two, passages=passages, slots=slots, counts=counts, gen_loglik=gen_loglik)


@jax.custom_vjp
def low(v):
    return lax.optimization_barrier(v.astype(jnp.bfloat16)).astype(jnp.float32)

@jax.custom_vjp
def low_back(v):
    return v

def low_keep(v):
    return (low(v), None)

def low_pass(kept, grad):
    return (grad,)

def back_keep(v):
    return (v, None)

def back_low(kept, grad):
    return (low(grad),)
low.defvjp(low_keep, low_pass)
low_back.defvjp(back_keep, back_low)
PRECISE = lax.Precision.HIGHEST
NORM_EPSILON = 1e-06
ENTROPY_WEIGHT = 0.5

def product(left_side, right_side):
    return jnp.dot(left_side, right_side, precision=PRECISE, preferred_element_type=jnp.float32)

def layer_norm(values, gain_vector, offset):
    center = values - lax.optimization_barrier(jnp.mean(values, axis=-1, keepdims=True))
    return center * lax.rsqrt(lax.optimization_barrier(jnp.mean(center * center, axis=-1, keepdims=True)) + NORM_EPSILON) * gain_vector + offset

def gelu_exact(values):
    return 0.5 * values * (1.0 + jax.scipy.special.erf(values * 0.7071067811865476))

def encoder(inputs, params):
    w_query, w_key, w_value, w_out, w_in, w_hid, b_query, b_value, b_out, b_in, b_hid, gain_one, shift_one, gain_two, shift_two = params
    seq_count = inputs.shape[0] // SEQ
    heads_shape = (seq_count, SEQ, HEADS, HDIM)
    queries = low(low_back(product(inputs, w_query) + b_query)).reshape(heads_shape)
    keys_all = low(low_back(product(inputs, w_key))).reshape(heads_shape)
    values_all = low(low_back(product(inputs, w_value) + b_value)).reshape(heads_shape)
    scores = low_back(jnp.einsum('bqhd,bkhd->bhqk', queries, keys_all, precision=PRECISE) * 0.125)
    weights = low(jax.nn.softmax(scores, axis=-1))
    context = jnp.einsum('bhqk,bkhd->bqhd', weights, values_all, precision=PRECISE).reshape(inputs.shape)
    context = low(low_back(context))
    attended = low_back(product(context, w_out) + b_out)
    hidden_one = layer_norm(inputs + attended, gain_one, shift_one)
    pre_act = low_back(product(low(hidden_one), w_in) + b_in)
    branch = low_back(product(low(gelu_exact(pre_act)), w_hid) + b_hid)
    return layer_norm(hidden_one + branch, gain_two, shift_two)

def retrieve(cls_rows, slot_rows, count_rows, gen_rows, index_rows):
    scores = low_back(jnp.dot(low(cls_rows), index_rows.T, precision=PRECISE, preferred_element_type=jnp.float32))
    peak = lax.optimization_barrier(jnp.max(scores, axis=1, keepdims=True))
    log_total = peak[:, 0] + jnp.log(lax.optimization_barrier(jnp.sum(jnp.exp(scores - peak), axis=1)))
    picked = jnp.take_along_axis(scores, slot_rows, axis=1)
    valid = jnp.arange(SLOTS)[None, :] < count_rows[:, None]
    joint = picked - log_total[:, None] + gen_rows
    masked = jnp.where(valid, joint, -1e+30)
    best = lax.optimization_barrier(jnp.max(masked, axis=1, keepdims=True))
    marginal = best[:, 0] + jnp.log(lax.optimization_barrier(jnp.sum(jnp.exp(masked - best), axis=1)))
    centered = jnp.where(valid, joint - marginal[:, None], 0.0)
    posterior = jnp.where(valid, jnp.exp(masked - marginal[:, None]), 0.0)
    entropy_rows = -lax.optimization_barrier(jnp.sum(posterior * centered, axis=1))
    return (jnp.sum(-marginal), jnp.sum(entropy_rows))

def reference(tokens, upstream, w_query, w_key, w_value, w_out, w_in, w_hid, b_query, b_value, b_out, b_in, b_hid, gain_one, shift_one, gain_two, shift_two, passages, slots, counts, gen_loglik):
    params = tuple((member.astype(jnp.float32) for member in (w_query, w_key, w_value, w_out, w_in, w_hid, b_query, b_value, b_out, b_in, b_hid, gain_one, shift_one, gain_two, shift_two)))
    inputs = tokens.astype(jnp.float32)
    cotangent = upstream.astype(jnp.float32)
    index_rows = passages.astype(jnp.float32)
    group_tokens = math.gcd(TOKENS, 4096)
    group_count = TOKENS // group_tokens
    per_group = QUESTIONS // N_DP

    def objective(inputs, params):
        layer = jax.checkpoint(lambda block_rows: encoder(block_rows, params))
        outputs = lax.map(layer, inputs.reshape(group_count, group_tokens, D)).reshape(TOKENS, D)
        cls_all = outputs[::SEQ]
        scorer = jax.checkpoint(lambda items: retrieve(items[0], items[1], items[2], items[3], index_rows))
        nll_parts, entropy_parts = lax.map(scorer, (cls_all.reshape(N_DP, per_group, D), slots.reshape(N_DP, per_group, SLOTS), counts.reshape(N_DP, per_group), gen_loglik.reshape(N_DP, per_group, SLOTS)))
        nll_total = jnp.sum(nll_parts)
        entropy_total = jnp.sum(entropy_parts)
        total = jnp.sum(outputs * cotangent) + nll_total + ENTROPY_WEIGHT * entropy_total
        return (total, (outputs, nll_total, entropy_total))
    total, pullback, extras = jax.vjp(objective, inputs, params, has_aux=True)
    outputs, nll_total, entropy_total = extras
    grad_inputs, grad_params = pullback(jnp.ones_like(total))
    loss = (nll_total + ENTROPY_WEIGHT * entropy_total) / QUESTIONS
    entropy = entropy_total / QUESTIONS
    return (outputs.astype(jnp.bfloat16), grad_inputs.astype(jnp.bfloat16), loss, entropy, grad_params[0], grad_params[1], grad_params[2], grad_params[3], grad_params[4], grad_params[5], grad_params[6], grad_params[7], grad_params[8], grad_params[9], grad_params[10], grad_params[11], grad_params[12], grad_params[13], grad_params[14])
```

```python
import functools
import math

import jax
import jax.numpy as jnp
from jax import lax
from jax.experimental import pallas as pl
from jax.experimental.pallas import tpu as pltpu
from jax.sharding import PartitionSpec as P

HEADS = 12
FEED_PART = 256
SLOT_RECORDS = 13
RECORD_ROWS = 64
HDIM = 64
SEQ = 128
NORM_EPSILON = 1e-06
ENTROPY_WEIGHT = 0.5
BF = jnp.bfloat16
F32 = jnp.float32
MIB = 1 << 20
NEGATIVE = -1e30


def dot(left, right):
    return jnp.dot(left, right, preferred_element_type=F32)


def dot_nt(left, right):
    return lax.dot_general(left, right, (((1,), (1,)), ((), ())), preferred_element_type=F32)


def dot_tn(left, right):
    return lax.dot_general(left, right, (((0,), (0,)), ((), ())), preferred_element_type=F32)


B_QUERY, B_VALUE, B_OUT, GAIN_ONE, SHIFT_ONE, B_HID, GAIN_TWO, SHIFT_TWO, B_IN = range(9)


def line(ref, n):
    return ref[n : n + 1, :]


def norm_forward(values):
    center = values - jnp.mean(values, axis=-1, keepdims=True)
    inverse = lax.rsqrt(jnp.mean(center * center, axis=-1, keepdims=True) + NORM_EPSILON)
    return center * inverse, inverse


def norm_backward(scaled, normed, inverse):
    return inverse * (
        scaled
        - jnp.mean(scaled, axis=-1, keepdims=True)
        - normed * jnp.mean(scaled * normed, axis=-1, keepdims=True)
    )


def gelu_and_slope(values):
    cumulative = 0.5 * (1.0 + lax.erf(values * 0.7071067811865476))
    bell = jnp.exp(-0.5 * values * values)
    return values * cumulative, cumulative + values * bell * 0.3989422804014327


def whole(memory=pltpu.VMEM):
    return pl.BlockSpec(memory_space=memory)


def params(limit):
    return pltpu.CompilerParams(vmem_limit_bytes=limit * MIB)


def cost(flops, moved):
    return pl.CostEstimate(flops=int(flops), bytes_accessed=int(moved), transcendentals=0)


def shape(dims, dtype):
    return jax.ShapeDtypeStruct(dims, dtype)


class Given:
    def __init__(self, held, ref, sems=None, parts=0):
        self.ref, self.sems, self.parts = ref, sems, parts
        self.waiting = []
        if parts:
            size = ref.shape[0] // parts
            for n in range(parts):
                cut = pl.ds(n * size, size)
                source, target = (held, ref) if parts == 1 else (held.at[cut], ref.at[cut])
                self.waiting.append(pltpu.make_async_copy(source, target, sems.at[n]))

    def start(self):
        for copy in self.waiting:
            copy.start()

    def get(self, part=None):
        for n in range(self.parts) if part is None else (part,):
            if self.parts and self.waiting[n] is not None:
                self.waiting[n].wait()
                self.waiting[n] = None
        return self.ref


class Made:
    def __init__(self, ref, far=None, sems=None, parts=0):
        self.ref, self.far, self.sems, self.parts = ref, far, sems, parts
        self.running = []

    def put(self, part=None):
        if not self.parts:
            return
        for n in range(self.parts) if part is None else (part,):
            size = self.ref.shape[0] // self.parts
            cut = pl.ds(n * size, size)
            source, target = (self.ref, self.far) if self.parts == 1 else (self.ref.at[cut], self.far.at[cut])
            copy = pltpu.make_async_copy(source, target, self.sems.at[n])
            copy.start()
            self.running.append(copy)


def kernel(body, name, ins, outs, scratch=(), flops=0, moved=MIB):
    operands = [pltpu.with_memory_space_constraint(a, pltpu.HBM) if parts else a for a, parts in ins]
    in_specs = [whole(pl.ANY if parts else pltpu.VMEM) for _, parts in ins]
    near = [(shape if not kind else pltpu.VMEM)(dims, dtype) for dims, dtype, kind, _ in outs if kind != "far"]
    far = [pltpu.HBM(dims, dtype) for dims, dtype, kind, _ in outs if kind in ("far", "both")]
    extra = [pltpu.VMEM(a.shape, a.dtype) for a, parts in ins if parts]
    extra += [pltpu.SemaphoreType.DMA((parts,)) for _, parts in ins if parts]
    extra += [pltpu.VMEM(dims, dtype) for dims, dtype, kind, _ in outs if kind == "far"]
    extra += [pltpu.SemaphoreType.DMA((parts,)) for _, _, _, parts in outs if parts]
    buffers = [part for part in extra + list(scratch) if hasattr(part, "shape") and part.memory_space == pltpu.VMEM]
    limit = sum(math.prod(part.shape) * jnp.dtype(part.dtype).itemsize for part in buffers) // MIB + 8

    def run(*refs):
        refs = list(refs)

        def take(count):
            taken, refs[:] = refs[:count], refs[count:]
            return taken

        given, near_refs, far_refs = take(len(ins)), take(len(near)), take(len(far))
        copied = [n for n, (_, parts) in enumerate(ins) if parts]
        buffers, in_sems = take(len(copied)), take(len(copied))
        results, out_sems = take(sum(kind == "far" for _, _, kind, _ in outs)), take(len(far))
        arguments = []
        for n, (_, parts) in enumerate(ins):
            if parts:
                at = copied.index(n)
                arguments.append(Given(given[n], buffers[at], in_sems[at], parts))
            else:
                arguments.append(Given(None, given[n]))
        for argument in arguments:
            argument.start()
        made = []
        for _, _, kind, parts in outs:
            ref = results.pop(0) if kind == "far" else near_refs.pop(0)
            made.append(Made(ref, far_refs.pop(0), out_sems.pop(0), parts) if parts else Made(ref))
        body(arguments, made, *refs)
        for argument in arguments:
            argument.get()
        for result in made:
            for copy in result.running:
                copy.wait()

    return pl.pallas_call(
        run,
        out_shape=near + far,
        in_specs=in_specs,
        out_specs=[whole()] * len(near) + [whole(pl.ANY)] * len(far),
        scratch_shapes=extra + list(scratch),
        compiler_params=params(limit),
        cost_estimate=cost(flops, moved),
        name=name,
    )(*operands)


def place():
    dp, index = lax.axis_index("dp"), lax.axis_index("index")
    return dp % 2, dp // 2, index // 2, index % 2


def exchange(array, move):
    pairs = []
    for dp in range(4):
        for index in range(8):
            y, x, z, core = move(dp // 2, dp % 2, index // 2, index % 2)
            pairs.append((dp * 8 + index, (y * 2 + x) * 8 + z * 2 + core))
    return lax.ppermute(array, ("dp", "index"), pairs)


def over_core(y, x, z, core):
    return y, x, z, 1 - core


def over_x(y, x, z, core):
    return y, 1 - x, z, core


def over_y(y, x, z, core):
    return 1 - y, x, z, core


def over_both(y, x, z, core):
    return 1 - y, 1 - x, z, core


def over_z(step):
    return lambda y, x, z, core: (y, x, z ^ step, core)


def project_kernel(ins, outs):
    tok, wk, wv, wq, bv, bq, wo, bo, g1, s1, wi, bi, wh, bh, g2, s2 = ins
    q_out, k_out, v_out, cls_out, vec_out = outs
    row = lambda given: given.get()[...].reshape(1, -1)
    tokens = tok.get()
    k_out.ref[...] = dot(tokens[...], wk.get()[...]).astype(BF)
    k_out.put()
    v_out.ref[...] = (dot(tokens[...], wv.get()[...]) + row(bv)).astype(BF)
    v_out.put()
    q_out.ref[...] = (dot(tokens[...], wq.get()[...]) + row(bq)).astype(BF)
    q_out.put()
    rows, width = tokens.shape
    count = rows // SEQ
    head_rows = 16
    owned = lax.broadcasted_iota(jnp.int32, (head_rows, width), 1) // HDIM == lax.broadcasted_iota(
        jnp.int32, (head_rows, width), 0
    )
    contexts, firsts = [], []
    for b in range(count):
        query = q_out.ref[b * SEQ : b * SEQ + 16, :][:1].astype(F32)
        spread = jnp.where(owned, query, 0.0).astype(BF)
        scores = dot_nt(spread, k_out.ref[b * SEQ : (b + 1) * SEQ, :]) * 0.125
        raised = jnp.exp(scores - jnp.max(scores, axis=1, keepdims=True))
        weights = (raised / jnp.sum(raised, axis=1, keepdims=True)).astype(BF)
        mixed = dot(weights, v_out.ref[b * SEQ : (b + 1) * SEQ, :])
        contexts.append(jnp.sum(jnp.where(owned, mixed, 0.0), axis=0, keepdims=True))
        firsts.append(tokens[b * SEQ : b * SEQ + 16, :][:1].astype(F32))
    context = jnp.concatenate(contexts + contexts, axis=0).astype(BF)
    first = jnp.concatenate(firsts + firsts, axis=0)
    attended = dot(context, wo.get()[...]) + row(bo)
    normed, _ = norm_forward(first + attended)
    hidden = normed * row(g1) + row(s1)
    flat = row(bi)
    act, _ = gelu_and_slope(dot(hidden.astype(BF), wi.get()[...]) + flat)
    branch = dot(act.astype(BF), wh.get()[...]) + row(bh)
    normed, _ = norm_forward(hidden + branch)
    lines = lax.broadcasted_iota(jnp.int32, (2 * count, width), 0)
    mine = lines // count == lax.axis_index("index") % 2
    cls_out.ref[...] = jnp.where(mine, normed * row(g2) + row(s2), 0.0).astype(BF)
    cls_out.put()
    for n, vector in enumerate((bq, bv, bo, g1, s1, bh, g2, s2)):
        vec_out.ref[n : n + 1, :] = row(vector)
    for n in range(flat.shape[1] // width):
        vec_out.ref[B_IN + n : B_IN + n + 1, :] = flat[:, n * width : (n + 1) * width]
    vec_out.ref[B_IN + flat.shape[1] // width :, :] = jnp.zeros((16 - B_IN - flat.shape[1] // width, width), F32)
    vec_out.put()


def project(sources):
    rows, width = sources[0].shape
    outs = [((rows, width), BF, "both", 1)] * 3 + [((2 * (rows // SEQ), width), BF, "", 0), ((16, width), F32, "", 0)]
    return kernel(
        project_kernel, "project", [(part, 1) for part in sources], outs, flops=8 * rows * width * width, moved=20 * MIB
    )


def stacked(pair):
    lane = lax.broadcasted_iota(jnp.int32, pair.shape, 1)
    zero = jnp.zeros_like(pair)
    return jnp.concatenate(
        [jnp.where(lane < HDIM, pair, zero), jnp.where(lane < HDIM, zero, pair)], axis=0
    )


def unstacked(tall):
    half = tall.shape[0] // 2
    lane = lax.broadcasted_iota(jnp.int32, (half, tall.shape[1]), 1)
    return jnp.where(lane < HDIM, tall[:half], tall[half:])


def attend_kernel(ins, outs):
    q, k, v, tok, wo, vec = ins
    p_out, ctx_out, n1_out, i1_out, low_out = outs
    rows, width = q.ref.shape
    pair = 2 * HDIM
    for b in range(rows // SEQ):
        here = pl.ds(b * SEQ, SEQ)
        for h in range(width // pair):
            lanes = pl.ds(h * pair, pair)
            scores = dot_nt(q.ref[here, lanes], stacked(k.ref[here, lanes])) * 0.125
            parts = []
            for part in (scores[:, :SEQ], scores[:, SEQ:]):
                raised = jnp.exp(part - jnp.max(part, axis=1, keepdims=True))
                parts.append(raised * (1.0 / jnp.sum(raised, axis=1, keepdims=True)))
            weights = jnp.concatenate(parts, axis=1).astype(BF)
            p_out.ref[here, pl.ds(h * 2 * SEQ, 2 * SEQ)] = weights
            ctx_out.ref[here, lanes] = dot(weights, stacked(v.ref[here, lanes])).astype(BF)
        p_out.put(b)
    ctx_out.put()
    vectors = vec.get()
    attended = dot(ctx_out.ref[...], wo.get()[...]) + line(vectors, B_OUT)
    normed, inverse = norm_forward(tok.get()[...].astype(F32) + attended)
    low_out.ref[...] = (normed * line(vectors, GAIN_ONE) + line(vectors, SHIFT_ONE)).astype(BF)
    low_out.put()
    n1_out.ref[...] = normed
    n1_out.put()
    i1_out.ref[...] = jnp.broadcast_to(inverse, i1_out.ref.shape)
    i1_out.put()


def attend(q, k, v, tokens, wo, vec):
    rows, width = q.shape
    outs = [
        ((rows, HEADS * SEQ), BF, "far", rows // SEQ),
        ((rows, width), BF, "far", 1),
        ((rows, width), F32, "both", 1),
        ((rows, 128), F32, "far", 1),
        ((rows, width), BF, "both", 1),
    ]
    ins = [(q, 0), (k, 0), (v, 0), (tokens, 0), (wo, 0), (vec, 0)]
    n1_near, low_near, p, ctx, n1, i1, low = kernel(attend_kernel, "attend", ins, outs, flops=4 * rows * width * width)
    return p, ctx, n1, i1, low, n1_near, low_near


def gelu_part(low, wi, vectors, column, act, slope, count):
    width = low.shape[1]
    bias = vectors[B_IN + column // width : B_IN + column // width + 1, :][:, column % width : column % width + FEED_PART]
    value, steep = gelu_and_slope(dot(low[...], wi[:, pl.ds(column, FEED_PART)]) + bias)
    act[:, pl.ds(count * FEED_PART, FEED_PART)] = value.astype(BF)
    slope[count] = steep.astype(BF)


def feed_kernel(ins, outs):
    low, vec, wi = ins
    act_out, slope_out = outs
    vectors = vec.get()
    weights = wi.get()
    for n in range(slope_out.ref.shape[0]):
        gelu_part(low.ref, weights, vectors, n * FEED_PART, act_out.ref, slope_out.ref, n)
        slope_out.put(n)
    act_out.put()


def feed(low, wi, vec):
    rows, width = low.shape
    deep = wi.shape[1] // 2
    parts = deep // FEED_PART
    outs = [((rows, deep), BF, "both", 1), ((parts, rows, FEED_PART), BF, "far", parts)]
    return kernel(
        feed_kernel, "feed", [(low, 0), (vec, 0), (wi, 0)], outs, flops=2 * rows * width * deep
    )


def second_kernel(ins, outs):
    low, vec, wi, act0, n1, wh = ins
    act_out, slope_out, enc_out, n2_out, i2_out = outs
    vectors = vec.get()
    weights = wi.get()
    parts = slope_out.ref.shape[0]
    for n in range(parts):
        gelu_part(low.ref, weights, vectors, (parts + n) * FEED_PART, act_out.ref, slope_out.ref, n)
        slope_out.put(n)
    act_out.put()
    deep = act_out.ref.shape[1]
    weights = wh.get()
    branch = dot(act0.get()[...], weights[:deep, :]) + dot(act_out.ref[...], weights[deep:, :]) + line(vectors, B_HID)
    hidden = n1.get()[...] * line(vectors, GAIN_ONE) + line(vectors, SHIFT_ONE)
    normed, inverse = norm_forward(hidden + branch)
    enc_out.ref[...] = (normed * line(vectors, GAIN_TWO) + line(vectors, SHIFT_TWO)).astype(BF)
    enc_out.put()
    n2_out.ref[...] = normed
    i2_out.ref[...] = jnp.broadcast_to(inverse, i2_out.ref.shape)


def second(low, vec, wi, act0, n1, wh):
    rows, width = n1.shape
    deep = act0.shape[1]
    parts = deep // FEED_PART
    outs = [
        ((rows, deep), BF, "both", 1),
        ((parts, rows, FEED_PART), BF, "far", parts),
        ((rows, width), BF, "far", 1),
        ((rows, width), F32, "near", 0),
        ((rows, 128), F32, "near", 0),
    ]
    ins = [(low, 0), (vec, 0), (wi, 0), (act0, 0), (n1, 0), (wh, 0)]
    return kernel(second_kernel, "second", ins, outs, flops=6 * rows * width * deep)


def split(value, pieces):
    found = []
    for _ in range(pieces):
        piece = value.astype(BF).astype(F32)
        found.append(piece)
        value = value - piece
    return found


def packed_numbers(peak, total, width):
    lane = lax.broadcasted_iota(jnp.int32, (peak.shape[0], width), 1)
    packed = jnp.zeros((peak.shape[0], width), F32)
    for n, piece in enumerate(split(peak, 3) + split(total, 3)):
        packed = jnp.where(lane == n, piece, packed)
    return packed


def unpacked_numbers(packed):
    return (
        packed[:, 0:1] + packed[:, 1:2] + packed[:, 2:3],
        packed[:, 3:4] + packed[:, 4:5] + packed[:, 5:6],
    )


def search_kernel(ins, outs):
    _, _, z, core = place()
    passages, slots = ins[8].get(), ins[9].get()
    (out,) = outs
    each = slots.shape[0] // 4
    ids = jnp.concatenate(
        [slots[pl.ds(pl.multiple_of((z ^ n) * each, each), each), :] for n in range(4)], axis=0
    ) - (2 * z + core) * passages.shape[0]
    count, many = ids.shape
    lane = lax.broadcasted_iota(jnp.int32, (count, passages.shape[0]), 1)
    marks = jnp.concatenate(
        [jnp.where(lane == ids[:, j : j + 1], 1.0, 0.0).astype(BF) for j in range(many)], axis=0
    )
    found = dot(marks, passages[...]).astype(BF)
    for j in range(many):
        out.ref[j] = found[j * count : (j + 1) * count, :]
    pairs = zip([given.get() for given in ins[:4]], [given.get() for given in ins[4:8]])
    cls = jnp.concatenate([a[...].astype(F32) + b[...].astype(F32) for a, b in pairs], axis=0).astype(BF)
    scores = dot_nt(cls, passages[...])
    width = passages.shape[1]
    peak = jnp.max(scores, axis=1, keepdims=True)
    raised = jnp.exp(scores - peak)
    total = jnp.sum(raised, axis=1, keepdims=True)
    mixed = dot(raised.astype(BF), passages[...])
    for n, piece in enumerate(split(mixed, 2)):
        out.ref[many + n] = piece.astype(BF)
    out.ref[many + 2] = packed_numbers(peak, total, width).astype(BF)
    out.put()


def search(own, other, passages, slots):
    local, width = passages.shape
    count = slots.shape[0]
    outs = [((slots.shape[1] + 3, count, width), BF, "", 0)]
    ins = [(part, 0) for part in (*own, *other, passages, slots)]
    return kernel(search_kernel, "search", ins, outs, flops=24 * count * local * width)[0]


def joined(records):
    peak = functools.reduce(jnp.maximum, [r[2] for r in records])
    scales = [jnp.exp(r[2] - peak) for r in records]
    rows = functools.reduce(jnp.add, [r[0] for r in records])
    mixed = functools.reduce(jnp.add, [r[1] * s for r, s in zip(records, scales)])
    total = functools.reduce(jnp.add, [r[3] * s for r, s in zip(records, scales)])
    return rows, mixed, peak, total


def meet_kernel(ins, outs):
    records = []
    for given in ins:
        array = given.get()[...].astype(F32)
        many = array.shape[0] - 3
        records.append((array[:many], array[many] + array[many + 1], *unpacked_numbers(array[many + 2])))
    rows, mixed, peak, total = joined(records)
    width = mixed.shape[1]
    lines = [rows[j] for j in range(rows.shape[0])] + split(mixed, 2) + [packed_numbers(peak, total, width)]
    each = mixed.shape[0] // 4
    half = each // 2
    first = lax.axis_index("index") % 2 == 0
    fill = [jnp.zeros((outs[0].ref.shape[0] - len(lines) * half, width), F32)]
    for n, out in enumerate(outs):
        cut = [part[n * each : (n + 1) * each] for part in lines]
        cut = [jnp.where(first, part[:half], part[half:]) for part in cut]
        out.ref[...] = jnp.concatenate(cut + fill, axis=0).astype(BF)
        out.put()


def meet(mine, theirs):
    outs = [((RECORD_ROWS, mine.shape[2]), BF, "", 0)] * 4
    return kernel(meet_kernel, "meet", [(mine, 0), (theirs, 0)], outs)


def question_grad(records, cls, counts, loglik):
    many = loglik.shape[1]
    asked = cls.shape[0] // 2
    parted = []
    for record in records:
        array = record[...].astype(F32)
        lines = [array[n * asked : (n + 1) * asked] for n in range(many + 3)]
        parted.append((jnp.stack(lines[:many]), lines[many] + lines[many + 1], *unpacked_numbers(lines[many + 2])))
    found, mixed, peak, total = joined(parted)
    lse = peak + jnp.log(total)
    index = lax.axis_index("index")
    both = cls[...].astype(F32)
    question = both[:asked] + both[asked:]
    lane = lax.broadcasted_iota(jnp.int32, (asked, many), 1)
    picked = jnp.zeros((asked, many), F32)
    for j in range(many):
        picked = jnp.where(lane == j, jnp.sum(question * found[j], axis=1, keepdims=True), picked)
    each = 2 * asked
    first = index % 2 == 0
    block = pl.ds(pl.multiple_of((index // 2) * each, each), each)
    near = loglik[block, :]
    limits = counts[block, :]
    near = jnp.where(first, near[:asked], near[asked:])
    limits = jnp.where(first, limits[:asked], limits[asked:])
    valid = lane < limits
    joint = picked - lse + near
    masked = jnp.where(valid, joint, NEGATIVE)
    best = jnp.max(masked, axis=1, keepdims=True)
    marginal = best + jnp.log(jnp.sum(jnp.exp(masked - best), axis=1, keepdims=True))
    centered = jnp.where(valid, joint - marginal, 0.0)
    posterior = jnp.where(valid, jnp.exp(masked - marginal), 0.0)
    entropy = -jnp.sum(posterior * centered, axis=1, keepdims=True)
    picked_grad = jnp.where(valid, -posterior * (1.0 + ENTROPY_WEIGHT * (centered + entropy)), 0.0)
    grad = mixed * (1.0 / total)
    for j in range(many):
        grad = grad + picked_grad[:, j : j + 1] * found[j]
    return grad, jnp.sum(-marginal), jnp.sum(entropy)


def lead_kernel(ins, outs, full):
    r0, r1, r2, r3, cls, counts, loglik, up, vec, n2, i2, act0, act1 = ins
    back_out, sum_out, vec_out, send_out = outs
    records = [given.get() for given in (r0, r1, r2, r3)]
    grad, nll, entropy = question_grad(records, cls.get(), counts.get(), loglik.get())
    rows, width = n2.ref.shape
    spot = lax.broadcasted_iota(jnp.int32, (rows, 1), 0)
    incoming = up.get()[...].astype(F32)
    for b in range(rows // SEQ):
        incoming = incoming + jnp.where(spot == b * SEQ, grad[b : b + 1], 0.0)
    normed = n2.ref[...]
    back = norm_backward(incoming * line(vec.get(), GAIN_TWO), normed, i2.ref[:, :1])
    low = back.astype(BF)
    back_out.ref[...] = low
    back_out.put()
    sum_out.ref[...] = back
    sum_out.put()
    spread = lax.broadcasted_iota(jnp.int32, (1, width), 1)
    numbers = jnp.where(spread == 0, nll, jnp.where(spread == 1, entropy, 0.0))
    vec_out.ref[...] = jnp.concatenate(
        [
            jnp.sum(low.astype(F32), axis=0, keepdims=True),
            jnp.sum(incoming * normed, axis=0, keepdims=True),
            jnp.sum(incoming, axis=0, keepdims=True),
            numbers,
            jnp.zeros((4, width), F32),
        ],
        axis=0,
    )
    vec_out.put()
    _, _, _, core = place()
    hid_product(1 - core, back_out.ref, act0.get(), act1.get(), full)
    hid_send(send_out, full)


def lead(records, cls, counts, loglik, up, vec, n2, i2, act0, act1):
    rows, width = n2.shape
    outs = [
        ((rows, width), BF, "both", 1),
        ((rows, width), F32, "near", 0),
        ((8, width), F32, "", 0),
        ((2, 2, 2) + PIECE, BF, "", 0),
    ]
    ins = [(part, 0) for part in (*records, cls, counts, loglik, up, vec)] + [(n2, 0), (i2, 0), (act0, 0), (act1, 0)]
    return kernel(
        lead_kernel, "lead", ins, outs, scratch=[pltpu.VMEM((width, act0.shape[1]), F32)],
        flops=2 * rows * width * act0.shape[1],
    )


def descend_kernel(ins, outs):
    low, wh, slope0, slope1, wi, sum_two, n1, i1, vec, wo = ins
    pre_out, attend_out, one_out, grad_out, vec_out = outs
    parts = slope0.ref.shape[0]
    width = low.ref.shape[1]
    biases = []
    for n in range(2 * parts):
        steep = slope0.get(n)[n] if n < parts else slope1.get(n - parts)[n - parts]
        here = pl.ds(n * FEED_PART, FEED_PART)
        pre = (dot_nt(low.ref[...], wh.get(n)[here, :]) * steep.astype(F32)).astype(BF)
        pre_out.ref[:, here] = pre
        biases.append(jnp.sum(pre.astype(F32), axis=0, keepdims=True))
    pre_out.put()
    incoming = sum_two.get()[...] + dot_nt(pre_out.ref[...], wi.get()[...])
    normed = n1.get()[...]
    one = norm_backward(incoming * line(vec.get(), GAIN_ONE), normed, i1.get()[:, :1])
    one_out.ref[...] = one
    one_out.put()
    attend_low = one.astype(BF)
    attend_out.ref[...] = attend_low
    attend_out.put()
    grad_out.ref[...] = dot_nt(attend_low, wo.get()[...]).astype(BF)
    grad_out.put()
    flat = jnp.concatenate(biases, axis=1)
    vec_out.ref[...] = jnp.concatenate(
        [
            jnp.sum(attend_low.astype(F32), axis=0, keepdims=True),
            jnp.sum(incoming * normed, axis=0, keepdims=True),
            jnp.sum(incoming, axis=0, keepdims=True),
            jnp.zeros((1, width), F32),
        ]
        + [flat[:, n * width : (n + 1) * width] for n in range(flat.shape[1] // width)],
        axis=0,
    )
    vec_out.put()


def descend(low, wh, slope0, slope1, wi, sum_two, n1, i1, vec, wo):
    rows, width = low.shape
    deep = wi.shape[1]
    parts = deep // FEED_PART
    outs = [
        ((rows, deep), BF, "both", 1),
        ((rows, width), BF, "far", 1),
        ((rows, width), F32, "near", 0),
        ((rows, width), BF, "near", 0),
        ((8, width), F32, "", 0),
    ]
    ins = [
        (low, 0), (wh, 0), (slope0, 0), (slope1, 0), (wi, 0), (sum_two, 0), (n1, 0), (i1, 0), (vec, 0),
        (wo, 0),
    ]
    return kernel(descend_kernel, "descend", ins, outs, flops=4 * rows * width * deep)


def unattend_kernel(ins, outs):
    grad, p, q, k, v, one, wq, wk, wv = ins
    dq_out, dk_out, dv_out, input_out, vec_out = outs
    rows, width = q.ref.shape
    pair = 2 * HDIM
    for b in range(rows // SEQ):
        here = pl.ds(b * SEQ, SEQ)
        for given in (grad, p, q, k, v):
            given.get(b)
        for h in range(width // pair):
            lanes = pl.ds(h * pair, pair)
            weights = p.ref[here, pl.ds(h * 2 * SEQ, 2 * SEQ)]
            incoming = grad.ref[here, lanes]
            dv_out.ref[here, lanes] = unstacked(dot_tn(weights, incoming)).astype(BF)
            sloped = dot_nt(incoming, stacked(v.ref[here, lanes]))
            parts = []
            for n in range(2):
                exact = weights[:, n * SEQ : (n + 1) * SEQ].astype(F32)
                steep = sloped[:, n * SEQ : (n + 1) * SEQ]
                parts.append(
                    exact * (steep - jnp.sum(steep * exact, axis=1, keepdims=True))
                )
            low = jnp.concatenate(parts, axis=1).astype(BF)
            dq_out.ref[here, lanes] = (dot(low, stacked(k.ref[here, lanes])) * 0.125).astype(BF)
            dk_out.ref[here, lanes] = (unstacked(dot_tn(low, q.ref[here, lanes])) * 0.125).astype(BF)
    for out in (dq_out, dk_out, dv_out):
        out.put()
    input_out.ref[...] = (
        one.get()[...]
        + dot_nt(dq_out.ref[...], wq.get()[...])
        + dot_nt(dk_out.ref[...], wk.get()[...])
        + dot_nt(dv_out.ref[...], wv.get()[...])
    ).astype(BF)
    input_out.put()
    vec_out.ref[...] = jnp.concatenate(
        [
            jnp.sum(dq_out.ref[...].astype(F32), axis=0, keepdims=True),
            jnp.sum(dv_out.ref[...].astype(F32), axis=0, keepdims=True),
            jnp.zeros((6, width), F32),
        ],
        axis=0,
    )
    vec_out.put()


def unattend(grad, p, q, k, v, one, wq, wk, wv):
    rows, width = q.shape
    many = rows // SEQ
    outs = [((rows, width), BF, "near", 0)] * 3 + [((rows, width), BF, "far", 1), ((8, width), F32, "", 0)]
    ins = [(part, 0) for part in (grad, p, q, k, v)] + [(part, 0) for part in (one, wq, wk, wv)]
    return kernel(unattend_kernel, "unattend", ins, outs, flops=8 * rows * width * width)


PIECE = (4, 96, 384)


def spots():
    x, y, _, _ = place()
    return ((x, y), (y, x))


def hid_product(core, low, act0, act1, full):
    each = act0.shape[1] // 4
    parts = []
    for z in range(4):
        ref = act0 if z < 2 else act1
        parts.append(ref[:, pl.ds(pl.multiple_of((2 * (z % 2) + core) * each, 128), each)])
    full[...] = dot_tn(low[...], jnp.concatenate(parts, axis=1))


def hid_piece(full, half, first, second):
    size = full.shape[0] // 8
    each = full.shape[1] // 4
    value = full[pl.ds(pl.multiple_of((half * 4 + first * 2 + second) * size, 16), size), :]
    return [value[:, z * each : (z + 1) * each] for z in range(4)]


def hid_send(out, full):
    for half, (mine, _) in enumerate(spots()):
        for role in range(2):
            first = mine if role else 1 - mine
            for second in range(2):
                for z, value in enumerate(hid_piece(full, half, first, second)):
                    out.ref[half, role, second, z] = value.astype(BF)
        out.put(half)


def hid_keep_kernel(ins, outs, full):
    low, act0, act1, came = ins
    _, _, _, core = place()
    hid_product(core, low.get(), act0.get(), act1.get(), full)
    for half, (mine, _) in enumerate(spots()):
        for role in range(2):
            first = mine if role else 1 - mine
            out = outs[2 * half + role]
            for second in range(2):
                for z, value in enumerate(hid_piece(full, half, first, second)):
                    out.ref[second, z] = (value + came.get(half)[half, role, second, z].astype(F32)).astype(BF)
            out.put()


def turned_rows(turned, core):
    size = turned.shape[0] // 8
    return jnp.concatenate(
        [turned[pl.ds(pl.multiple_of((2 * z + core) * size, 16), size), :] for z in range(4)], axis=0
    )


def wide_products(lefts, rights, half, first):
    if len(rights) == 1:
        width = rights[0].shape[1] // 4
        right = rights[0][:, pl.ds(pl.multiple_of((half * 2 + first) * width, 128), width)]
        return dot(lefts[0], right)
    low = half * 2
    right = jnp.where(first == 0, rights[low][...], rights[low + 1][...])
    left = lefts[low] if lefts[low] is lefts[low + 1] else jnp.where(first == 0, lefts[low], lefts[low + 1])
    return dot(left, right)


def wide_send(lefts, rights, out):
    for half, (mine, _) in enumerate(spots()):
        for role in range(2):
            value = wide_products(lefts, rights, half, mine if role else 1 - mine)
            for second in range(2):
                for z in range(4):
                    out.ref[half, role, second, z] = value[
                        z * PIECE[1] : (z + 1) * PIECE[1], second * PIECE[2] : (second + 1) * PIECE[2]
                    ].astype(BF)
        out.put(half)


def wide_keep(lefts, rights, came, outs):
    for half, (mine, _) in enumerate(spots()):
        for role in range(2):
            value = wide_products(lefts, rights, half, mine if role else 1 - mine)
            out = outs[2 * half + role]
            for second in range(2):
                for z in range(4):
                    part = value[z * PIECE[1] : (z + 1) * PIECE[1], second * PIECE[2] : (second + 1) * PIECE[2]]
                    out.ref[second, z] = (part + came.get(half)[half, role, second, z].astype(F32)).astype(BF)
            out.put()


def in_send_kernel(ins, outs, turned):
    low, pre = ins
    _, _, _, core = place()
    turned[...] = low.get()[...].T
    wide_send([turned_rows(turned, 1 - core)], [pre.get()], outs[0])


def in_keep_kernel(ins, outs, turned):
    low, pre, came = ins
    _, _, _, core = place()
    turned[...] = low.get()[...].T
    wide_keep([turned_rows(turned, core)], [pre.get()], came, outs)


def rest_lefts(tok, ctx, turned, core):
    turned[0] = tok.get()[...].T
    turned[1] = ctx.get()[...].T
    left, last = turned_rows(turned.at[0], core), turned_rows(turned.at[1], core)
    return [left, left, left, last]


def rest_send_kernel(ins, outs, turned):
    tok, ctx, dq, dk, dv, al = ins
    _, _, _, core = place()
    lefts = rest_lefts(tok, ctx, turned, 1 - core)
    wide_send(lefts, [given.get() for given in (dq, dk, dv, al)], outs[0])


def rest_keep_kernel(ins, outs, turned):
    tok, ctx, dq, dk, dv, al, came = ins
    _, _, _, core = place()
    lefts = rest_lefts(tok, ctx, turned, core)
    wide_keep(lefts, [given.get() for given in (dq, dk, dv, al)], came, outs)


def cut_for_partner(body, name, operands, scratch, flops):
    outs = [((2, 2, 2) + PIECE, BF, "", 0)]
    return kernel(body, name, [(part, 0) for part in operands], outs, scratch=scratch, flops=flops)[0]


def cut_for_chips(body, name, operands, came, scratch, flops):
    outs = [((2,) + PIECE, BF, "", 0)] * 4
    return kernel(body, name, [(part, 0) for part in operands] + [(came, 0)], outs, scratch=scratch, flops=flops)


def halve_kernel(ins, outs):
    for n, (_, mine) in enumerate(spots()):
        kept, came = ins[2 * n].get(), ins[2 * n + 1].get()
        for out, second in ((outs[2 * n], 1 - mine), (outs[2 * n + 1], mine)):
            out.ref[...] = (kept[second].astype(F32) + came[second].astype(F32)).astype(BF)
            out.put()


def deal_kernel(ins, outs):
    _, _, z, _ = place()
    k0, r0, k1, r1 = [given.get() for given in ins]
    for n, out in enumerate(outs):
        for half, (kept, came) in enumerate(((k0, r0), (k1, r1))):
            out.ref[half] = (kept[z ^ n].astype(F32) + came[z ^ n].astype(F32)).astype(BF)
        out.put()


def total_kernel(ins, outs):
    a, b, c, d = [given.get()[...].astype(F32) for given in ins]
    outs[0].ref[...] = ((a + b) + (c + d)).astype(BF)
    outs[0].put()


def combine(body, name, operands, outs):
    return kernel(body, name, [(part, 0) for part in operands], outs)


def dp_sources(ins):
    x, y, _, _ = place()
    own, from_x, from_y, from_both = [given.get() for given in ins[:4]]
    return ((own, x, y), (from_x, 1 - x, y), (from_y, x, 1 - y), (from_both, 1 - x, 1 - y))


def hid_final_kernel(ins, outs, full):
    size = PIECE[1]
    for ref, x, y in dp_sources(ins):
        for half, number in enumerate((2 * x + y, 2 * y + x)):
            full[pl.ds(pl.multiple_of((4 * half + number) * size, 16), size), :] = ref[half].astype(F32)
    outs[0].ref[...] = full[...].T
    outs[0].put()


def fill_wide(ins, full):
    for ref, x, y in dp_sources(ins):
        for half, number in enumerate((2 * x + y, 2 * y + x)):
            full[:, pl.ds(pl.multiple_of((4 * half + number) * PIECE[2], 128), PIECE[2])] = ref[half].astype(F32)


def in_final_kernel(ins, outs):
    fill_wide(ins, outs[0].ref)
    outs[0].put()


def rest_final_kernel(ins, outs, full):
    fill_wide(ins, full)
    width = outs[0].ref.shape[1]
    for n, out in enumerate(outs):
        out.ref[...] = full[:, n * width : (n + 1) * width]
        out.put()


def numbers_kernel(questions, vec, bq, bv, bo, bi, bh, g1, s1, g2, s2, loss, entropy):
    index = lax.axis_index("index")
    value = vec[...]
    nll, ent = jnp.sum(value[11:12, 0:1]), jnp.sum(value[11:12, 1:2])
    loss[0, 0] = (nll + ENTROPY_WEIGHT * ent) / questions
    entropy[0, 0] = ent / questions
    size = bq.shape[0]
    deep = bi.shape[0]
    per = value.shape[1] // deep
    for n in range(8):

        @pl.when(index == n)
        def _():
            for at, out in ((0, bq), (1, bv), (4, bo), (5, g1), (6, s1), (8, bh), (9, g2), (10, s2)):
                out[...] = value[at, n * size : (n + 1) * size]
            bi[...] = value[12 + n // per, (n % per) * deep : (n % per + 1) * deep]


def numbers(vec, questions):
    width = vec.shape[1]
    part, deep = width // 8, width // 2
    vectors = [shape((size,), F32) for size in (part, part, part, deep, part, part, part, part, part)]
    return pl.pallas_call(
        functools.partial(numbers_kernel, questions),
        out_shape=vectors + [shape((1, 1), F32)] * 2,
        in_specs=[whole()],
        out_specs=[whole()] * 9 + [whole(pltpu.SMEM)] * 2,
        compiler_params=params(56),
        cost_estimate=cost(0, MIB),
        name="numbers",
    )(vec)


def gather_kernel(ins, outs):
    lead_vec, descend_vec, unattend_vec = [given.get() for given in ins]
    outs[0].ref[...] = jnp.concatenate(
        [unattend_vec[0:4, :], descend_vec[0:4, :], lead_vec[0:4, :], descend_vec[4:8, :]], axis=0
    )
    outs[0].put()


def on_this_slice(
    tokens, upstream, w_query, w_key, w_value, w_out, w_in, w_hid, b_query, b_value, b_out, b_in, b_hid,
    gain_one, shift_one, gain_two, shift_two, passages, slots, counts, gen_loglik,
):
    rows, width = tokens.shape
    deep = w_in.shape[1]
    questions = slots.shape[0] * lax.axis_size("dp")
    q_near, k_near, v_near, cls, vec, q, k, v = project(
        (
            tokens, w_key, w_value, w_query, b_value, b_query, w_out, b_out, gain_one, shift_one, w_in, b_in, w_hid, b_hid,
            gain_two, shift_two,
        )
    )
    own = [cls] + [exchange(cls, over_z(n)) for n in (1, 2, 3)]
    p, ctx, n1, i1, low, n1_near, low_near = attend(q_near, k_near, v_near, tokens, w_out, vec)
    other = [exchange(part, over_core) for part in own]
    record = search(own, other, passages, slots)
    partner = exchange(record, over_core)
    act0_near, act0, slope0 = feed(low_near, w_in, vec)
    cuts = meet(record, partner)
    records = [cuts[0]] + [exchange(cuts[n], over_z(n)) for n in (1, 2, 3)]
    act1_near, n2, i2, act1, slope1, encoded = second(low_near, vec, w_in, act0_near, n1_near, w_hid)
    back_near, sum_two, lead_vec, hid_cut, back = lead(
        records, cls, counts.reshape(-1, 1), gen_loglik, upstream, vec, n2, i2, act0_near, act1_near
    )
    flops = rows * width * deep
    hid_came = exchange(hid_cut, over_core)
    pre_near, one, grad, descend_vec, pre, attend_low = descend(back_near, w_hid, slope0, slope1, w_in, sum_two, n1, i1, vec, w_out)
    hid = cut_for_chips(
        hid_keep_kernel, "hid_keep", (back, act0, act1), hid_came, [pltpu.VMEM((width, deep // 2), F32)], flops
    )
    turned = [pltpu.VMEM((width, rows), BF)]
    in_came = exchange(cut_for_partner(in_send_kernel, "in_send", (low, pre_near), turned, flops), over_core)
    dq, dk, dv, unattend_vec, input_grad = unattend(grad, p, q, k, v, one, w_query, w_key, w_value)
    into = cut_for_chips(in_keep_kernel, "in_keep", (low, pre), in_came, turned, flops)
    turned = [pltpu.VMEM((2, width, rows), BF)]
    operands = (tokens, ctx, dq, dk, dv, attend_low)
    rest_came = exchange(cut_for_partner(rest_send_kernel, "rest_send", operands, turned, flops), over_core)
    rest = cut_for_chips(rest_keep_kernel, "rest_keep", operands, rest_came, turned, flops)
    finished = []
    small = ((2,) + PIECE[1:], BF, "", 0)
    for s0, k0, s1, k1 in (hid, into, rest):
        r0, r1 = exchange(s0, over_x), exchange(s1, over_y)
        t0, u0, t1, u1 = combine(halve_kernel, "halve", (k0, r0, k1, r1), [(PIECE, BF, "", 0)] * 4)
        r0, r1 = exchange(t0, over_y), exchange(t1, over_x)
        parts = combine(deal_kernel, "deal", (u0, r0, u1, r1), [small] * 4)
        came = [exchange(parts[n], over_z(n)) for n in (1, 2, 3)]
        mine = combine(total_kernel, "total", (parts[0], *came), [small])[0]
        finished.append((mine, exchange(mine, over_x), exchange(mine, over_y), exchange(mine, over_both)))
    vec = combine(gather_kernel, "gather", (lead_vec, descend_vec, unattend_vec), [((16, width), F32, "", 0)])[0]
    for move in (over_core, over_x, over_y, over_z(1), over_z(2)):
        vec = vec + exchange(vec, move)
    part = width // 8
    operands = [[(piece, 0) for piece in pieces] for pieces in finished]
    grad_hid = kernel(
        hid_final_kernel, "hid_final", operands[0], [((deep // 8, width), F32, "", 0)],
        scratch=[pltpu.VMEM((width, deep // 8), F32)],
    )[0]
    grad_in = kernel(in_final_kernel, "in_final", operands[1], [((part, deep), F32, "", 0)])[0]
    grads = kernel(
        rest_final_kernel, "rest_final", operands[2], [((part, width), F32, "", 0)] * 4,
        scratch=[pltpu.VMEM((part, deep), F32)],
    )
    *vectors, loss, entropy = numbers(vec, questions)
    return (
        encoded, input_grad, loss.reshape(()), entropy.reshape(()), *grads, grad_in, grad_hid, *vectors,
    )


PRECISE = lax.Precision.HIGHEST


def shortened(array):

    def short(part):
        return part.astype(jnp.bfloat16) if part.dtype == jnp.float32 else part

    return jax.tree.map(short, array)


def product(left_side, right_side):
    return jnp.dot(left_side, right_side, preferred_element_type=jnp.float32)


def times_transpose(left_side, right_side):
    return lax.dot_general(
        left_side, right_side, (((1,), (1,)), ((), ())), preferred_element_type=jnp.float32
    )


def transpose_times(left_side, right_side):
    return lax.dot_general(
        left_side, right_side, (((0,), (0,)), ((), ())), preferred_element_type=jnp.float32
    )


def plain_norm_forward(values, gain_vector, offset):
    center = values - jnp.mean(values, axis=-1, keepdims=True)
    inverse = lax.rsqrt(jnp.mean(center * center, axis=-1, keepdims=True) + NORM_EPSILON)
    normed = center * inverse
    return (normed * gain_vector + offset, normed, inverse)


def plain_norm_backward(incoming, normed, inverse, gain_vector):
    scaled = incoming * gain_vector
    inner = (
        scaled
        - jnp.mean(scaled, axis=-1, keepdims=True)
        - normed * jnp.mean(scaled * normed, axis=-1, keepdims=True)
    )
    return (inverse * inner, jnp.sum(incoming * normed, axis=0), jnp.sum(incoming, axis=0))


def gelu_slope(values):
    cumulative = 0.5 * (1.0 + jax.scipy.special.erf(values * 0.7071067811865476))
    return (
        values * cumulative,
        cumulative + values * jnp.exp(-0.5 * values * values) * 0.3989422804014327,
    )


def on_any_slice(
    tokens,
    upstream,
    w_query,
    w_key,
    w_value,
    w_out,
    w_in,
    w_hid,
    b_query,
    b_value,
    b_out,
    b_in,
    b_hid,
    gain_one,
    shift_one,
    gain_two,
    shift_two,
    passages,
    slots,
    counts,
    gen_loglik,
):
    tok_rows, model_width = tokens.shape
    seq_count = tok_rows // SEQ
    heads_shape = (seq_count, SEQ, HEADS, HDIM)
    inputs = tokens.astype(jnp.float32)
    queries = (product(tokens, w_query) + b_query).astype(jnp.bfloat16).reshape(heads_shape)
    keys_all = product(tokens, w_key).astype(jnp.bfloat16).reshape(heads_shape)
    values_all = (product(tokens, w_value) + b_value).astype(jnp.bfloat16).reshape(heads_shape)
    scores = (
        jnp.einsum("bqhd,bkhd->bhqk", queries, keys_all, preferred_element_type=jnp.float32) * 0.125
    )
    peak = jnp.max(scores, axis=-1, keepdims=True)
    log_total = peak + jnp.log(jnp.sum(jnp.exp(scores - peak), axis=-1, keepdims=True))
    weights_low = jnp.exp(scores - log_total).astype(jnp.bfloat16)
    context = jnp.einsum(
        "bhqk,bkhd->bqhd", weights_low, values_all, preferred_element_type=jnp.float32
    )
    context = context.reshape(tok_rows, model_width).astype(jnp.bfloat16)
    attended = product(context, w_out) + b_out
    hidden_one, normed_one, inverse_one = plain_norm_forward(inputs + attended, gain_one, shift_one)
    hidden_low = hidden_one.astype(jnp.bfloat16)
    pre_act = product(hidden_low, w_in) + b_in
    activated, slope = gelu_slope(pre_act)
    act_low = activated.astype(jnp.bfloat16)
    branch = product(act_low, w_hid) + b_hid
    outputs, normed_two, inverse_two = plain_norm_forward(hidden_one + branch, gain_two, shift_two)
    cls_low = outputs[::SEQ].astype(jnp.bfloat16)
    index_scores = times_transpose(lax.all_gather(cls_low, "index", axis=0, tiled=True), passages)
    group_rows, local_rows = index_scores.shape
    first_row = lax.axis_index("index") * local_rows
    local_slots = slots - first_row
    onehot = (
        lax.broadcasted_iota(jnp.int32, (1, 1, local_rows), 2) == local_slots[:, :, None]
    ).astype(jnp.float32)
    picked_part = jnp.einsum("qr,qsr->qs", index_scores, onehot, precision=PRECISE)
    row_peak = jnp.max(index_scores, axis=1)
    peak_all = lax.pmax(row_peak, "index")
    total_part = jnp.sum(jnp.exp(index_scores - peak_all[:, None]), axis=1)
    total_all, picked = lax.psum((total_part, picked_part), "index")
    index_lse = peak_all + jnp.log(total_all)
    valid = lax.broadcasted_iota(jnp.int32, picked.shape, 1) < counts[:, None]
    joint = picked - index_lse[:, None] + gen_loglik
    masked = jnp.where(valid, joint, -1e30)
    best = jnp.max(masked, axis=1, keepdims=True)
    marginal = best[:, 0] + jnp.log(jnp.sum(jnp.exp(masked - best), axis=1))
    centered = jnp.where(valid, joint - marginal[:, None], 0.0)
    posterior = jnp.where(valid, jnp.exp(masked - marginal[:, None]), 0.0)
    entropy_rows = -jnp.sum(posterior * centered, axis=1)
    nll_total, entropy_total = lax.psum((jnp.sum(-marginal), jnp.sum(entropy_rows)), "dp")
    questions = group_rows * lax.axis_size("dp")
    loss = (nll_total + ENTROPY_WEIGHT * entropy_total) / questions
    entropy = entropy_total / questions
    picked_grad = jnp.where(
        valid, -posterior * (1.0 + ENTROPY_WEIGHT * (centered + entropy_rows[:, None])), 0.0
    )
    score_grad = jnp.exp(index_scores - index_lse[:, None]) + jnp.einsum(
        "qs,qsr->qr", picked_grad, onehot, precision=PRECISE
    )
    score_low = score_grad.astype(jnp.bfloat16)
    cls_grad = lax.psum_scatter(
        product(score_low, passages), "index", scatter_dimension=0, tiled=True
    )
    out_grad = (
        upstream.astype(jnp.float32).reshape(seq_count, SEQ, model_width).at[:, 0].add(cls_grad)
    )
    out_grad = out_grad.reshape(tok_rows, model_width)
    sum_two, grad_gain_two, grad_shift_two = plain_norm_backward(
        out_grad, normed_two, inverse_two, gain_two
    )
    branch_low = sum_two.astype(jnp.bfloat16)
    grad_b_hid = jnp.sum(branch_low.astype(jnp.float32), axis=0)
    grad_w_hid = transpose_times(act_low, branch_low)
    pre_low = (times_transpose(branch_low, w_hid) * slope).astype(jnp.bfloat16)
    grad_b_in = jnp.sum(pre_low.astype(jnp.float32), axis=0)
    grad_w_in = transpose_times(hidden_low, pre_low)
    sum_one, grad_gain_one, grad_shift_one = plain_norm_backward(
        sum_two + times_transpose(pre_low, w_in), normed_one, inverse_one, gain_one
    )
    attend_low = sum_one.astype(jnp.bfloat16)
    grad_b_out = jnp.sum(attend_low.astype(jnp.float32), axis=0)
    grad_w_out = transpose_times(context, attend_low)
    context_grad = times_transpose(attend_low, w_out).astype(jnp.bfloat16).reshape(heads_shape)
    scores_again = (
        jnp.einsum("bqhd,bkhd->bhqk", queries, keys_all, preferred_element_type=jnp.float32) * 0.125
    )
    weights_again = jnp.exp(scores_again - log_total)
    again_low = weights_again.astype(jnp.bfloat16)
    weight_grad = jnp.einsum(
        "bqhd,bkhd->bhqk", context_grad, values_all, preferred_element_type=jnp.float32
    )
    value_grad = jnp.einsum(
        "bhqk,bqhd->bkhd", again_low, context_grad, preferred_element_type=jnp.float32
    )
    value_grad = value_grad.reshape(tok_rows, model_width).astype(jnp.bfloat16)
    logit_grad = weights_again * (
        weight_grad - jnp.sum(weight_grad * weights_again, axis=-1, keepdims=True)
    )
    logit_low = logit_grad.astype(jnp.bfloat16)
    query_grad = (
        jnp.einsum("bhqk,bkhd->bqhd", logit_low, keys_all, preferred_element_type=jnp.float32)
        * 0.125
    )
    query_grad = query_grad.reshape(tok_rows, model_width).astype(jnp.bfloat16)
    key_grad = (
        jnp.einsum("bhqk,bqhd->bkhd", logit_low, queries, preferred_element_type=jnp.float32)
        * 0.125
    )
    key_grad = key_grad.reshape(tok_rows, model_width).astype(jnp.bfloat16)
    input_grad = (
        sum_one
        + times_transpose(query_grad, w_query)
        + times_transpose(key_grad, w_key)
        + times_transpose(value_grad, w_value)
    ).astype(jnp.bfloat16)
    grad_w_query = transpose_times(tokens, query_grad)
    grad_w_key = transpose_times(tokens, key_grad)
    grad_w_value = transpose_times(tokens, value_grad)
    grad_b_query = jnp.sum(query_grad.astype(jnp.float32), axis=0)
    grad_b_value = jnp.sum(value_grad.astype(jnp.float32), axis=0)
    shares = (
        lax.psum_scatter(grad_w_query, "index", scatter_dimension=0, tiled=True),
        lax.psum_scatter(grad_w_key, "index", scatter_dimension=0, tiled=True),
        lax.psum_scatter(grad_w_value, "index", scatter_dimension=0, tiled=True),
        lax.psum_scatter(grad_w_out, "index", scatter_dimension=0, tiled=True),
        lax.psum_scatter(grad_w_in, "index", scatter_dimension=0, tiled=True),
        lax.psum_scatter(grad_w_hid, "index", scatter_dimension=0, tiled=True),
        lax.psum_scatter(grad_b_query, "index", scatter_dimension=0, tiled=True),
        lax.psum_scatter(grad_b_value, "index", scatter_dimension=0, tiled=True),
        lax.psum_scatter(grad_b_out, "index", scatter_dimension=0, tiled=True),
        lax.psum_scatter(grad_b_in, "index", scatter_dimension=0, tiled=True),
        lax.psum_scatter(grad_b_hid, "index", scatter_dimension=0, tiled=True),
        lax.psum_scatter(grad_gain_one, "index", scatter_dimension=0, tiled=True),
        lax.psum_scatter(grad_shift_one, "index", scatter_dimension=0, tiled=True),
        lax.psum_scatter(grad_gain_two, "index", scatter_dimension=0, tiled=True),
        lax.psum_scatter(grad_shift_two, "index", scatter_dimension=0, tiled=True),
    )
    summed = jax.tree.map(
        lambda part: part.astype(jnp.float32), lax.psum(shortened(tuple(shares)), "dp")
    )
    return (outputs.astype(jnp.bfloat16), input_grad, loss, entropy) + tuple(summed)


def solution(mesh):
    here = (mesh.shape["dp"], mesh.shape["index"]) == (4, 8)
    return jax.shard_map(
        on_this_slice if here else on_any_slice,
        mesh=mesh,
        in_specs=(
            P(("dp", "index"), None),
            P(("dp", "index"), None),
            P(),
            P(),
            P(),
            P(),
            P(),
            P(),
            P(),
            P(),
            P(),
            P(),
            P(),
            P(),
            P(),
            P(),
            P(),
            P("index", None),
            P("dp", None),
            P("dp"),
            P("dp", None),
        ),
        out_specs=(
            P(("dp", "index"), None),
            P(("dp", "index"), None),
            P(),
            P(),
            P("index", None),
            P("index", None),
            P("index", None),
            P("index", None),
            P("index", None),
            P("index", None),
            P("index"),
            P("index"),
            P("index"),
            P("index"),
            P("index"),
            P("index"),
            P("index"),
            P("index"),
            P("index"),
        ),
        check_vma=False,
    )
```

```python
import functools
import math

import jax
import jax.numpy as jnp
from jax import lax
from jax.experimental import pallas as pl
from jax.experimental.pallas import tpu as pltpu
from jax.sharding import PartitionSpec as P

HEADS = 12
FEED_PART = 256
SLOT_RECORDS = 13
RECORD_ROWS = 64
HDIM = 64
SEQ = 128
NORM_EPSILON = 1e-06
ENTROPY_WEIGHT = 0.5
BF = jnp.bfloat16
F32 = jnp.float32
MIB = 1 << 20
NEGATIVE = -1e30
WORK = {"in_deal": 5e9, "rest_deal": 1, "hid_deal": 1, "hid_pair": 1}


def dot(left, right):
    return jnp.dot(left, right, preferred_element_type=F32)


def dot_nt(left, right):
    return lax.dot_general(left, right, (((1,), (1,)), ((), ())), preferred_element_type=F32)


def dot_tn(left, right):
    return lax.dot_general(left, right, (((0,), (0,)), ((), ())), preferred_element_type=F32)


B_QUERY, B_VALUE, B_OUT, GAIN_ONE, SHIFT_ONE, B_HID, GAIN_TWO, SHIFT_TWO, B_IN = range(9)


def line(ref, n):
    return ref[n : n + 1, :]


def norm_forward(values):
    center = values - jnp.mean(values, axis=-1, keepdims=True)
    inverse = lax.rsqrt(jnp.mean(center * center, axis=-1, keepdims=True) + NORM_EPSILON)
    return center * inverse, inverse


def norm_backward(scaled, normed, inverse):
    return inverse * (
        scaled
        - jnp.mean(scaled, axis=-1, keepdims=True)
        - normed * jnp.mean(scaled * normed, axis=-1, keepdims=True)
    )


def gelu_and_slope(values):
    cumulative = 0.5 * (1.0 + lax.erf(values * 0.7071067811865476))
    bell = jnp.exp(-0.5 * values * values)
    return values * cumulative, cumulative + values * bell * 0.3989422804014327


def whole(memory=pltpu.VMEM):
    return pl.BlockSpec(memory_space=memory)


def params(limit):
    return pltpu.CompilerParams(vmem_limit_bytes=limit * MIB)


def cost(flops, moved):
    return pl.CostEstimate(flops=int(flops), bytes_accessed=int(moved), transcendentals=0)


def shape(dims, dtype):
    return jax.ShapeDtypeStruct(dims, dtype)


class Given:
    def __init__(self, held, ref, sems=None, parts=0, axis=0):
        self.ref, self.sems, self.parts = ref, sems, parts
        self.waiting = []
        if parts:
            size = ref.shape[axis] // parts
            for n in range(parts):
                cut = (slice(None),) * axis + (pl.ds(n * size, size),)
                source, target = (held, ref) if parts == 1 else (held.at[cut], ref.at[cut])
                self.waiting.append(pltpu.make_async_copy(source, target, sems.at[n]))

    def start(self):
        for copy in self.waiting:
            copy.start()

    def get(self, part=None):
        for n in range(self.parts) if part is None else (part,):
            if self.parts and self.waiting[n] is not None:
                self.waiting[n].wait()
                self.waiting[n] = None
        return self.ref


class Made:
    def __init__(self, ref, far=None, sems=None, parts=0):
        self.ref, self.far, self.sems, self.parts = ref, far, sems, parts
        self.running = []

    def put(self, part=None):
        if not self.parts:
            return
        for n in range(self.parts) if part is None else (part,):
            size = self.ref.shape[0] // self.parts
            cut = pl.ds(n * size, size)
            source, target = (self.ref, self.far) if self.parts == 1 else (self.ref.at[cut], self.far.at[cut])
            copy = pltpu.make_async_copy(source, target, self.sems.at[n])
            copy.start()
            self.running.append(copy)


def kernel(body, name, ins, outs, scratch=(), flops=0, moved=MIB, after=()):
    ins, axes = [part[:2] for part in ins], [(*part, 0)[2] for part in ins]
    operands = [pltpu.with_memory_space_constraint(a, pltpu.HBM) if parts else a for a, parts in ins]
    in_specs = [whole(pl.ANY if parts else pltpu.VMEM) for _, parts in ins]
    operands += after
    in_specs += [whole(pl.ANY)] * len(after)
    near = [(shape if not kind else pltpu.VMEM)(dims, dtype) for dims, dtype, kind, _ in outs if kind != "far"]
    far = [pltpu.HBM(dims, dtype) for dims, dtype, kind, _ in outs if kind in ("far", "both")]
    extra = [pltpu.VMEM(a.shape, a.dtype) for a, parts in ins if parts]
    extra += [pltpu.SemaphoreType.DMA((parts,)) for _, parts in ins if parts]
    extra += [pltpu.VMEM(dims, dtype) for dims, dtype, kind, _ in outs if kind == "far"]
    extra += [pltpu.SemaphoreType.DMA((parts,)) for _, _, _, parts in outs if parts]
    buffers = [part for part in extra + list(scratch) if hasattr(part, "shape") and part.memory_space == pltpu.VMEM]
    limit = sum(math.prod(part.shape) * jnp.dtype(part.dtype).itemsize for part in buffers) // MIB + 8

    def run(*refs):
        refs = list(refs)

        def take(count):
            taken, refs[:] = refs[:count], refs[count:]
            return taken

        given, _, near_refs, far_refs = take(len(ins)), take(len(after)), take(len(near)), take(len(far))
        copied = [n for n, (_, parts) in enumerate(ins) if parts]
        buffers, in_sems = take(len(copied)), take(len(copied))
        results, out_sems = take(sum(kind == "far" for _, _, kind, _ in outs)), take(len(far))
        arguments = []
        for n, (_, parts) in enumerate(ins):
            if parts:
                at = copied.index(n)
                arguments.append(Given(given[n], buffers[at], in_sems[at], parts, axes[n]))
            else:
                arguments.append(Given(None, given[n]))
        for argument in arguments:
            argument.start()
        made = []
        for _, _, kind, parts in outs:
            ref = results.pop(0) if kind == "far" else near_refs.pop(0)
            made.append(Made(ref, far_refs.pop(0), out_sems.pop(0), parts) if parts else Made(ref))
        body(arguments, made, *refs)
        for argument in arguments:
            argument.get()
        for result in made:
            for copy in result.running:
                copy.wait()

    call = functools.partial(
        pl.pallas_call,
        run,
        out_shape=near + far,
        in_specs=in_specs,
        out_specs=[whole()] * len(near) + [whole(pl.ANY)] * len(far),
        scratch_shapes=extra + list(scratch),
        compiler_params=params(limit),
        cost_estimate=cost(WORK.get(name, 1), 1),
        name=name,
    )
    if name == "project":
        return call()(*operands)
    if name == "attend":
        return call()(*operands)
    if name == "forward":
        return call()(*operands)
    if name == "lead":
        return call()(*operands)
    if name == "slope":
        return call()(*operands)
    if name == "descend":
        return call()(*operands)
    if name == "unattend":
        return call()(*operands)
    if name == "hid_keep":
        return call()(*operands)
    return call()(*operands)


def place():
    dp, index = lax.axis_index("dp"), lax.axis_index("index")
    return dp % 2, dp // 2, index // 2, index % 2


def exchange(array, move):
    pairs = []
    for dp in range(4):
        for index in range(8):
            y, x, z, core = move(dp // 2, dp % 2, index // 2, index % 2)
            pairs.append((dp * 8 + index, (y * 2 + x) * 8 + z * 2 + core))
    return lax.ppermute(array, ("dp", "index"), pairs)


def over_core(y, x, z, core):
    return y, x, z, 1 - core


def over_x(y, x, z, core):
    return y, 1 - x, z, core


def over_y(y, x, z, core):
    return 1 - y, x, z, core


def over_both(y, x, z, core):
    return 1 - y, 1 - x, z, core


def over_z_by_core(turn):
    return lambda y, x, z, core: (y, x, z ^ (1 + (core + turn) % 2), core)


def over_z(step):
    return lambda y, x, z, core: (y, x, z ^ step, core)


def project_kernel(ins, outs):
    tok, wk, wv, wq, bv, bq, wo, bo, g1, s1, wi, bi, wh, bh, g2, s2 = ins
    q_out, k_out, v_out, cls_out, vec_out = outs
    row = lambda given: given.get()[...].reshape(1, -1)
    tokens = tok.get()
    k_out.ref[...] = dot(tokens[...], wk.get()[...]).astype(BF)
    k_out.put()
    v_out.ref[...] = (dot(tokens[...], wv.get()[...]) + row(bv)).astype(BF)
    v_out.put()
    q_out.ref[...] = (dot(tokens[...], wq.get()[...]) + row(bq)).astype(BF)
    q_out.put()
    rows, width = tokens.shape
    count = rows // SEQ
    head_rows = 16
    owned = lax.broadcasted_iota(jnp.int32, (head_rows, width), 1) // HDIM == lax.broadcasted_iota(
        jnp.int32, (head_rows, width), 0
    )
    contexts, firsts = [], []
    for b in range(count):
        query = q_out.ref[b * SEQ : b * SEQ + 16, :][:1].astype(F32)
        spread = jnp.where(owned, query, 0.0).astype(BF)
        scores = dot_nt(spread, k_out.ref[b * SEQ : (b + 1) * SEQ, :]) * 0.125
        raised = jnp.exp(scores - jnp.max(scores, axis=1, keepdims=True))
        weights = (raised / jnp.sum(raised, axis=1, keepdims=True)).astype(BF)
        mixed = dot(weights, v_out.ref[b * SEQ : (b + 1) * SEQ, :])
        contexts.append(jnp.sum(jnp.where(owned, mixed, 0.0), axis=0, keepdims=True))
        firsts.append(tokens[b * SEQ : b * SEQ + 16, :][:1].astype(F32))
    context = jnp.concatenate(contexts + contexts, axis=0).astype(BF)
    first = jnp.concatenate(firsts + firsts, axis=0)
    attended = dot(context, wo.get()[...]) + row(bo)
    normed, _ = norm_forward(first + attended)
    hidden = normed * row(g1) + row(s1)
    flat = row(bi)
    act, _ = gelu_and_slope(dot(hidden.astype(BF), wi.get()[...]) + flat)
    branch = dot(act.astype(BF), wh.get()[...]) + row(bh)
    normed, _ = norm_forward(hidden + branch)
    lines = lax.broadcasted_iota(jnp.int32, (2 * count, width), 0)
    mine = lines // count == lax.axis_index("index") % 2
    cls_out.ref[...] = jnp.where(mine, normed * row(g2) + row(s2), 0.0).astype(BF)
    cls_out.put()
    for n, vector in enumerate((bq, bv, bo, g1, s1, bh, g2, s2)):
        vec_out.ref[n : n + 1, :] = row(vector)
    for n in range(flat.shape[1] // width):
        vec_out.ref[B_IN + n : B_IN + n + 1, :] = flat[:, n * width : (n + 1) * width]
    vec_out.ref[B_IN + flat.shape[1] // width :, :] = jnp.zeros((16 - B_IN - flat.shape[1] // width, width), F32)
    vec_out.put()


def project(sources):
    rows, width = sources[0].shape
    outs = [((rows, width), BF, "far", 1)] * 3 + [((2 * (rows // SEQ), width), BF, "", 0), ((16, width), F32, "far", 1)]
    return kernel(
        project_kernel, "project", [(part, 1) for part in sources], outs, flops=8 * rows * width * width, moved=20 * MIB
    )


def stacked(pair):
    lane = lax.broadcasted_iota(jnp.int32, pair.shape, 1)
    zero = jnp.zeros_like(pair)
    return jnp.concatenate(
        [jnp.where(lane < HDIM, pair, zero), jnp.where(lane < HDIM, zero, pair)], axis=0
    )


def unstacked(tall):
    half = tall.shape[0] // 2
    lane = lax.broadcasted_iota(jnp.int32, (half, tall.shape[1]), 1)
    return jnp.where(lane < HDIM, tall[:half], tall[half:])


def attend_kernel(ins, outs):
    q, k, v, tok, wo, vec = ins
    p_out, ctx_out, n1_out, i1_out, low_out = outs
    rows, width = q.ref.shape
    pair = 2 * HDIM
    many = rows // SEQ
    for b in range(many):
        here = pl.ds(b * SEQ, SEQ)
        for h in range(width // pair):
            lanes = pl.ds(h * pair, pair)
            scores = dot_nt(q.ref[here, lanes], stacked(k.ref[here, lanes])) * 0.125
            parts = []
            for part in (scores[:, :SEQ], scores[:, SEQ:]):
                raised = jnp.exp(part - jnp.max(part, axis=1, keepdims=True))
                parts.append(raised * (1.0 / jnp.sum(raised, axis=1, keepdims=True)))
            weights = jnp.concatenate(parts, axis=1).astype(BF)
            p_out.ref[here, pl.ds(h * 2 * SEQ, 2 * SEQ)] = weights
            ctx_out.ref[here, lanes] = dot(weights, stacked(v.ref[here, lanes])).astype(BF)
        p_out.put(b)
    ctx_out.put()
    vectors, tokens, weights = vec.get(), tok.get(), wo.get()
    attended = dot(ctx_out.ref[...], weights[...]) + line(vectors, B_OUT)
    normed, inverse = norm_forward(tokens[...].astype(F32) + attended)
    n1_out.ref[...] = normed
    low_out.ref[...] = (normed * line(vectors, GAIN_ONE) + line(vectors, SHIFT_ONE)).astype(BF)
    i1_out.ref[...] = jnp.broadcast_to(inverse, i1_out.ref.shape)
    for out in (low_out, n1_out, i1_out):
        out.put()


def attend(q, k, v, tokens, wo, vec, after=()):
    rows, width = q.shape
    many = rows // SEQ
    outs = [
        ((rows, HEADS * SEQ), BF, "far", many),
        ((rows, width), BF, "far", 1),
        ((rows, width), F32, "both", 1),
        ((rows, 128), F32, "far", 1),
        ((rows, width), BF, "both", 1),
    ]
    ins = plain((q, k, v, tokens, wo, vec))
    n1_near, low_near, p, ctx, n1, i1, low = kernel(attend_kernel, "attend", ins, outs, after=after)
    return p, ctx, n1, i1, low, n1_near, low_near


def forward_kernel(ins, outs):
    low, n1, vec, wi, wh, up = ins
    act_out, slope_out, enc_out, back_out, sum_out, first_out, vec_out = outs
    rows, width = low.ref.shape
    vectors, weights = vec.get(), wi.get()
    for n in range(slope_out.ref.shape[0]):
        column = n * FEED_PART
        bias = vectors[B_IN + column // width : B_IN + column // width + 1, :][:, column % width : column % width + FEED_PART]
        value, steep = gelu_and_slope(dot(low.ref[...], weights[:, pl.ds(column, FEED_PART)]) + bias)
        act_out.ref[:, pl.ds(column, FEED_PART)] = value.astype(BF)
        slope_out.ref[n] = steep.astype(BF)
        slope_out.put(n)
    act_out.put()
    weights = wh.get()
    firsts, sums = [], []
    for n in range(enc_out.parts):
        size = rows // enc_out.parts
        here = pl.ds(n * size, size)
        branch = dot(act_out.ref[here, :], weights[...]) + line(vectors, B_HID)
        hidden = n1.ref[here, :] * line(vectors, GAIN_ONE) + line(vectors, SHIFT_ONE)
        normed, inverse = norm_forward(hidden + branch)
        enc_out.ref[here, :] = (normed * line(vectors, GAIN_TWO) + line(vectors, SHIFT_TWO)).astype(BF)
        enc_out.put(n)
        incoming = up.ref[here, :].astype(F32)
        back = norm_backward(incoming * line(vectors, GAIN_TWO), normed, inverse)
        sum_out.ref[here, :] = back
        sum_out.put(n)
        short = back.astype(BF)
        back_out.ref[here, :] = short
        wide = jnp.broadcast_to(inverse, normed.shape)
        firsts.append([[value[b : b + 1] for b in range(0, size, SEQ)] for value in (normed, incoming, wide)])
        sums.append(
            [
                jnp.sum(short.astype(F32), axis=0, keepdims=True),
                jnp.sum(incoming * normed, axis=0, keepdims=True),
                jnp.sum(incoming, axis=0, keepdims=True),
            ]
        )
    lines = [part for n in range(3) for block in firsts for part in block[n]]
    first_out.ref[...] = jnp.concatenate(lines + [jnp.zeros((16 - len(lines), width), F32)], axis=0)
    vec_out.ref[...] = jnp.concatenate(
        [functools.reduce(jnp.add, [block[n] for block in sums]) for n in range(3)] + [jnp.zeros((5, width), F32)], axis=0
    )


def forward(low, n1, vec, wi, wh, up):
    rows, width = low.shape
    deep = wi.shape[1]
    outs = [
        ((rows, deep), BF, "far", 1),
        ((deep // FEED_PART, rows, FEED_PART), BF, "far", deep // FEED_PART),
        ((rows, width), BF, "far", 2),
        ((rows, width), BF, "near", 0),
        ((rows, width), F32, "far", 2),
        ((16, width), F32, "", 0),
        ((8, width), F32, "", 0),
    ]
    ins = plain((low, n1, vec, wi, wh, up))
    back, first, sums, act, slope, encoded, sum_two = kernel(forward_kernel, "forward", ins, outs)
    return act, slope, encoded, sum_two, back, first, sums


def split(value, pieces):
    found = []
    for _ in range(pieces):
        piece = value.astype(BF).astype(F32)
        found.append(piece)
        value = value - piece
    return found


def packed_numbers(peak, total, width):
    lane = lax.broadcasted_iota(jnp.int32, (peak.shape[0], width), 1)
    packed = jnp.zeros((peak.shape[0], width), F32)
    for n, piece in enumerate(split(peak, 3) + split(total, 3)):
        packed = jnp.where(lane == n, piece, packed)
    return packed


def unpacked_numbers(packed):
    return (
        packed[:, 0:1] + packed[:, 1:2] + packed[:, 2:3],
        packed[:, 3:4] + packed[:, 4:5] + packed[:, 5:6],
    )


def mark_kernel(far_passages, far_slots, passages, found, slots, sems):
    copies = [
        pltpu.make_async_copy(far_slots, slots, sems.at[0]),
        pltpu.make_async_copy(far_passages, passages, sems.at[1]),
    ]
    for copy in copies:
        copy.start()
    copies[0].wait()
    _, _, z, core = place()
    many, count = slots.shape
    each = count // 4
    spot = lax.broadcasted_iota(jnp.int32, (count, count), 0)
    question = ((spot // each) ^ z) * each + spot % each
    chosen = lax.broadcasted_iota(jnp.int32, (count, count), 1) == question
    local = passages.shape[0]
    lane = lax.broadcasted_iota(jnp.int32, (count, local), 1)
    marks = []
    for j in range(many):
        ids = jnp.sum(jnp.where(chosen, slots[j : j + 1, :].astype(F32), 0.0), axis=1, keepdims=True)
        ids = ids.astype(jnp.int32) - (2 * z + core) * local
        marks.append(jnp.where(lane == ids, 1.0, 0.0).astype(BF))
    marks = jnp.concatenate(marks, axis=0)
    copies[1].wait()
    rows = dot(marks, passages[...]).astype(BF)
    for j in range(many):
        found[j] = rows[j * count : (j + 1) * count, :]


def mark(passages, slots):
    many, count = slots.shape
    local, width = passages.shape
    return pl.pallas_call(
        mark_kernel,
        out_shape=[pltpu.VMEM(passages.shape, BF), pltpu.VMEM((many, count, width), BF)],
        in_specs=[whole(pl.ANY)] * 2,
        out_specs=[whole()] * 2,
        scratch_shapes=[pltpu.VMEM(slots.shape, slots.dtype), pltpu.SemaphoreType.DMA((2,))],
        compiler_params=params(8),
        cost_estimate=cost(2 * many * count * local * width, 4 * MIB),
        name="mark",
    )(*[pltpu.with_memory_space_constraint(part, pltpu.HBM) for part in (passages, slots)])


def collect_kernel(ins, outs):
    outs[0].ref[...] = jnp.concatenate([given.ref[...].astype(F32) for given in ins], axis=0).astype(BF)


def search_kernel(ins, outs):
    mine, theirs, passages, found = [given.ref for given in ins]
    (out,) = outs
    many = found.shape[0]
    cls = (mine[...].astype(F32) + theirs[...].astype(F32)).astype(BF)
    out.ref[:many] = found[...]
    scores = dot_nt(cls, passages[...])
    width = passages.shape[1]
    peak = jnp.max(scores, axis=1, keepdims=True)
    raised = jnp.exp(scores - peak)
    total = jnp.sum(raised, axis=1, keepdims=True)
    mixed = dot(raised.astype(BF), passages[...])
    for n, piece in enumerate(split(mixed, 2)):
        out.ref[many + n] = piece.astype(BF)
    out.ref[many + 2] = packed_numbers(peak, total, width).astype(BF)


def search(mine, theirs, passages, found):
    local, width = passages.shape
    many, count, _ = found.shape
    outs = [((many + 3, count, width), BF, "", 0)]
    ins = [(part, 0) for part in (mine, theirs, passages, found)]
    return kernel(search_kernel, "search", ins, outs, flops=4 * count * local * width)[0]


def joined(records):
    peak = functools.reduce(jnp.maximum, [r[2] for r in records])
    scales = [jnp.exp(r[2] - peak) for r in records]
    rows = functools.reduce(jnp.add, [r[0] for r in records])
    mixed = functools.reduce(jnp.add, [r[1] * s for r, s in zip(records, scales)])
    total = functools.reduce(jnp.add, [r[3] * s for r, s in zip(records, scales)])
    return rows, mixed, peak, total


def meet_kernel(ins, outs):
    records = []
    for given in ins:
        array = given.get()[...].astype(F32)
        many = array.shape[0] - 3
        records.append((array[:many], array[many] + array[many + 1], *unpacked_numbers(array[many + 2])))
    rows, mixed, peak, total = joined(records)
    width = mixed.shape[1]
    lines = [rows[j] for j in range(rows.shape[0])] + split(mixed, 2) + [packed_numbers(peak, total, width)]
    each = mixed.shape[0] // 4
    half = each // 2
    first = lax.axis_index("index") % 2 == 0
    fill = [jnp.zeros((outs[0].ref.shape[0] - len(lines) * half, width), F32)]
    for n, out in enumerate(outs):
        cut = [part[n * each : (n + 1) * each] for part in lines]
        cut = [jnp.where(first, part[:half], part[half:]) for part in cut]
        out.ref[...] = jnp.concatenate(cut + fill, axis=0).astype(BF)
        out.put()


def meet(mine, theirs):
    outs = [((RECORD_ROWS, mine.shape[2]), BF, "", 0)] * 4
    return kernel(meet_kernel, "meet", [(mine, 0), (theirs, 0)], outs)


def question_grad(records, cls, counts, loglik):
    many = loglik.shape[0]
    asked = cls.shape[0] // 2
    parted = []
    for record in records:
        array = record[...].astype(F32)
        lines = [array[n * asked : (n + 1) * asked] for n in range(many + 3)]
        parted.append((jnp.stack(lines[:many]), lines[many] + lines[many + 1], *unpacked_numbers(lines[many + 2])))
    found, mixed, peak, total = joined(parted)
    lse = peak + jnp.log(total)
    index = lax.axis_index("index")
    both = cls[...].astype(F32)
    question = both[:asked] + both[asked:]
    lane = lax.broadcasted_iota(jnp.int32, (asked, many), 1)
    picked = jnp.zeros((asked, many), F32)
    for j in range(many):
        picked = jnp.where(lane == j, jnp.sum(question * found[j], axis=1, keepdims=True), picked)
    questions = loglik.shape[1]
    spot = lax.broadcasted_iota(jnp.int32, (asked, questions), 0) + index * asked
    chosen = lax.broadcasted_iota(jnp.int32, (asked, questions), 1) == spot
    near = jnp.zeros((asked, many), F32)
    for j in range(many):
        value = jnp.sum(jnp.where(chosen, loglik[j : j + 1, :], 0.0), axis=1, keepdims=True)
        near = jnp.where(lane == j, value, near)
    limits = counts[...].reshape(1, questions).astype(F32)
    limits = jnp.sum(jnp.where(chosen, limits, 0.0), axis=1, keepdims=True).astype(jnp.int32)
    valid = lane < limits
    joint = picked - lse + near
    masked = jnp.where(valid, joint, NEGATIVE)
    best = jnp.max(masked, axis=1, keepdims=True)
    marginal = best + jnp.log(jnp.sum(jnp.exp(masked - best), axis=1, keepdims=True))
    centered = jnp.where(valid, joint - marginal, 0.0)
    posterior = jnp.where(valid, jnp.exp(masked - marginal), 0.0)
    entropy = -jnp.sum(posterior * centered, axis=1, keepdims=True)
    picked_grad = jnp.where(valid, -posterior * (1.0 + ENTROPY_WEIGHT * (centered + entropy)), 0.0)
    grad = mixed * (1.0 / total)
    for j in range(many):
        grad = grad + picked_grad[:, j : j + 1] * found[j]
    return grad, jnp.sum(-marginal), jnp.sum(entropy)


def lead_kernel(ins, outs, full):
    r0, r1, r2, r3, cls, counts, loglik, first, sums, vec, back, act = ins
    back_out, fix_out, vec_out, send_out = outs
    records = [given.get() for given in (r0, r1, r2, r3)]
    grad, nll, entropy = question_grad(records, cls.get(), counts.get(), loglik.get())
    many, width = grad.shape
    normed, incoming, inverse = [first.ref[...][n * many : (n + 1) * many] for n in range(3)]
    gain = line(vec.get(), GAIN_TWO)
    old = norm_backward(incoming * gain, normed, inverse[:, :1])
    new = norm_backward((incoming + grad) * gain, normed, inverse[:, :1])
    low = new.astype(BF).astype(F32)
    fix_out.ref[...] = jnp.concatenate([new, jnp.zeros((8 - many, width), F32)], axis=0)
    back_out.ref[...] = back.get()[...]
    top = lax.broadcasted_iota(jnp.int32, (16, width), 0) == 0
    for b in range(many):
        here = pl.ds(b * SEQ, 16)
        rows = back_out.ref[here, :].astype(F32)
        back_out.ref[here, :] = jnp.where(top, low[b : b + 1], rows).astype(BF)
    back_out.put()
    spread = lax.broadcasted_iota(jnp.int32, (1, width), 1)
    numbers = jnp.where(spread == 0, nll, jnp.where(spread == 1, entropy, 0.0))
    old_sums = sums.ref[...]
    change = low - old.astype(BF).astype(F32)
    vec_out.ref[...] = jnp.concatenate(
        [
            old_sums[0:1] + jnp.sum(change, axis=0, keepdims=True),
            old_sums[1:2] + jnp.sum(grad * normed, axis=0, keepdims=True),
            old_sums[2:3] + jnp.sum(grad, axis=0, keepdims=True),
            numbers,
            jnp.zeros((4, width), F32),
        ],
        axis=0,
    )
    _, _, _, core = place()
    hid_product(1 - core, back_out.ref, act.get(), full)
    hid_send(send_out, full)


def lead(records, cls, counts, loglik, first, sums, vec, back, act):
    rows, width = back.shape
    deep = act.shape[1]
    outs = [
        ((rows, width), BF, "both", 1),
        ((8, width), F32, "", 0),
        ((8, width), F32, "", 0),
        ((4, width, deep // 8), BF, "", 0),
    ]
    ins = [(part, 0) for part in (*records, cls)] + [(counts, 1), (loglik, 1), (first, 0), (sums, 0), (vec, 1), (back, 0), (act, 1)]
    return kernel(
        lead_kernel, "lead", ins, outs, scratch=[pltpu.VMEM((width, deep // 2), F32)], flops=rows * width * deep
    )


def slope_kernel(ins, outs):
    low, wh, slope = ins
    pre_out, vec_out = outs
    parts = slope.ref.shape[0]
    width = low.ref.shape[1]
    biases = []
    for n in range(parts):
        here = pl.ds(n * FEED_PART, FEED_PART)
        pre = (dot_nt(low.ref[...], wh.ref[here, :]) * slope.ref[n].astype(F32)).astype(BF)
        pre_out.ref[:, here] = pre
        biases.append(jnp.sum(pre.astype(F32), axis=0, keepdims=True))
    pre_out.put()
    flat = jnp.concatenate(biases, axis=1)
    vec_out.ref[...] = jnp.concatenate(
        [flat[:, n * width : (n + 1) * width] for n in range(flat.shape[1] // width)] + [jnp.zeros((4, width), F32)], axis=0
    )


def descend_kernel(ins, outs):
    pre, wi, fix, sum_two, n1, i1, vec, wo = ins
    attend_out, one_out, grad_out, vec_out = outs
    rows, width = n1.ref.shape
    back = dot_nt(pre.ref[...], wi.ref[...])
    before = sum_two.get()[...]
    spot = lax.broadcasted_iota(jnp.int32, (rows, 1), 0)
    for b in range(rows // SEQ):
        before = jnp.where(spot == b * SEQ, fix.ref[b : b + 1, :], before)
    incoming = before + back
    normed = n1.get()[...]
    one = norm_backward(incoming * line(vec.get(), GAIN_ONE), normed, i1.get()[:, :1])
    one_out.ref[...] = one
    one_out.put()
    attend_low = one.astype(BF)
    attend_out.ref[...] = attend_low
    grad_out.ref[...] = dot_nt(attend_low, wo.ref[...]).astype(BF)
    grad_out.put()
    vec_out.ref[...] = jnp.concatenate(
        [
            jnp.sum(attend_low.astype(F32), axis=0, keepdims=True),
            jnp.sum(incoming * normed, axis=0, keepdims=True),
            jnp.sum(incoming, axis=0, keepdims=True),
            jnp.zeros((5, width), F32),
        ],
        axis=0,
    )


def slope_part(low, wh, slope):
    rows, width = low.shape
    outs = [((rows, wh.shape[0]), BF, "both", 1), ((8, width), F32, "", 0)]
    return kernel(slope_kernel, "slope", plain((low, wh, slope)), outs)


def descend(pre, wi, fix, sum_two, n1, i1, vec, wo, after=()):
    rows, width = n1.shape
    outs = [
        ((rows, width), BF, "near", 0),
        ((rows, width), F32, "far", 1),
        ((rows, width), BF, "far", 1),
        ((8, width), F32, "", 0),
    ]
    ins = [(pre, 0), (wi, 0), (fix, 0), (sum_two, 1), (n1, 1), (i1, 1), (vec, 1), (wo, 0)]
    return kernel(descend_kernel, "descend", ins, outs, after=after)


def unattend_kernel(ins, outs):
    grad, p, q, k, v, one, wq, wk, wv = ins
    dq_out, dk_out, dv_out, input_out, vec_out = outs
    rows, width = q.ref.shape
    pair = 2 * HDIM
    pairs = range(width // pair)
    for b in range(rows // SEQ):
        here = pl.ds(b * SEQ, SEQ)
        lanes = [pl.ds(h * pair, pair) for h in pairs]
        weights = [p.ref[here, pl.ds(h * 2 * SEQ, 2 * SEQ)] for h in pairs]
        incoming = [grad.ref[here, at] for at in lanes]
        sloped = [dot_nt(incoming[h], stacked(v.ref[here, lanes[h]])) for h in pairs]
        values = [unstacked(dot_tn(weights[h], incoming[h])).astype(BF) for h in pairs]
        lows = []
        for h in pairs:
            parts = []
            for n in range(2):
                exact = weights[h][:, n * SEQ : (n + 1) * SEQ].astype(F32)
                steep = sloped[h][:, n * SEQ : (n + 1) * SEQ]
                parts.append(exact * (steep - jnp.sum(steep * exact, axis=1, keepdims=True)))
            lows.append(jnp.concatenate(parts, axis=1).astype(BF))
        queries = [(dot(lows[h], stacked(k.ref[here, lanes[h]])) * 0.125).astype(BF) for h in pairs]
        keys = [(unstacked(dot_tn(lows[h], q.ref[here, lanes[h]])) * 0.125).astype(BF) for h in pairs]
        for h in pairs:
            dv_out.ref[here, lanes[h]] = values[h]
            dq_out.ref[here, lanes[h]] = queries[h]
            dk_out.ref[here, lanes[h]] = keys[h]
    for out in (dq_out, dk_out, dv_out):
        out.put()
    input_out.ref[...] = (
        one.get()[...]
        + dot_nt(dq_out.ref[...], wq.get()[...])
        + dot_nt(dk_out.ref[...], wk.get()[...])
        + dot_nt(dv_out.ref[...], wv.get()[...])
    ).astype(BF)
    input_out.put()
    vec_out.ref[...] = jnp.concatenate(
        [
            jnp.sum(dq_out.ref[...].astype(F32), axis=0, keepdims=True),
            jnp.sum(dv_out.ref[...].astype(F32), axis=0, keepdims=True),
            jnp.zeros((6, width), F32),
        ],
        axis=0,
    )
    vec_out.put()


def unattend(grad, p, q, k, v, one, wq, wk, wv, after=()):
    rows, width = q.shape
    many = rows // SEQ
    outs = [((rows, width), BF, "near", 0)] * 3 + [((rows, width), BF, "far", 1), ((8, width), F32, "", 0)]
    ins = [(part, 0) for part in (grad, p, q, k, v, one, wq, wk, wv)]
    return kernel(unattend_kernel, "unattend", ins, outs, flops=8 * rows * width * width, after=after)


LINES = 96
LANES = 384
MORE = 16


def hid_product(core, low, act, full):
    each = act.shape[1] // 8
    parts = [act[:, pl.ds(pl.multiple_of((2 * z + core) * each, 128), each)] for z in range(4)]
    full[...] = dot_tn(low[...], jnp.concatenate(parts, axis=1))


def hid_send(out, full):
    each = full.shape[1] // 4
    for z in range(4):
        out.ref[z] = full[:, z * each : (z + 1) * each].astype(BF)


def hid_keep_kernel(ins, outs, full):
    low, act, came = [given.get() for given in ins]
    _, _, z, core = place()
    hid_product(core, low, act, full)
    each = full.shape[1] // 4
    for n, far in enumerate((3, 1 + core, 2 - core, 0)):
        lanes = pl.ds(pl.multiple_of((z ^ far) * each, 128), each)
        outs[n // 2].ref[n % 2] = (full[:, lanes] + came[z ^ far].astype(F32)).astype(BF)


def sum_kernel(ins, outs):
    outs[0].ref[...] = functools.reduce(jnp.add, [given.get()[...].astype(F32) for given in ins]).astype(BF)


def hid_pair_kernel(ins, outs):
    kept, came = [given.ref for given in ins]
    outs[0].ref[...] = (kept[0].astype(F32) + came[0].astype(F32)).astype(BF)


def hid_deal_kernel(ins, outs):
    x, y, _, _ = place()
    kept, came, last = [given.ref for given in ins]
    size = outs[0].ref.shape[0]
    for out, number in zip(outs, (2 * x + y, 2 * (1 - x) + y, 2 * x + 1 - y, 2 * (1 - x) + 1 - y)):
        cut = pl.ds(pl.multiple_of(number * size, 16), size)
        out.ref[...] = (kept[1, cut, :].astype(F32) + came[1, cut, :].astype(F32) + last[cut, :].astype(F32)).astype(BF)


def spots():
    x, y, _, _ = place()
    return ((x, y), (y, x))


def turned_rows(turned, core):
    size = turned.shape[0] // 8
    return jnp.concatenate(
        [turned[pl.ds(pl.multiple_of((2 * z + core) * size, 16), size), :] for z in range(4)], axis=0
    )


def vector_lines(vectors, core):
    lead_vec, slope_vec, descend_vec, unattend_vec = [given.get() for given in vectors]
    eight = jnp.concatenate(
        [unattend_vec[0:2, :], descend_vec[0:1, :], lead_vec[0:1, :], descend_vec[1:3, :], lead_vec[1:3, :]], axis=0
    )
    deep = slope_vec[0:4, :]
    device = lax.axis_index("dp") * 8 + lax.axis_index("index")
    lane = lax.broadcasted_iota(jnp.int32, (1, LANES), 1)
    terms = jnp.zeros((1, LANES), F32)
    for n, piece in enumerate(split(lead_vec[3:4, 0:1], 3) + split(lead_vec[3:4, 1:2], 3)):
        terms = jnp.where(lane == 32 * n + device, piece, terms)
    found = []
    for z in range(4):
        both = []
        for index in (2 * z, 2 * z + 1):
            at = (index % 2) * LANES
            cuts = [eight[:, index * LINES : (index + 1) * LINES]]
            cuts += [deep[index // 2 : index // 2 + 1, at + n * LINES : at + (n + 1) * LINES] for n in range(4)]
            both.append(jnp.concatenate(cuts, axis=0))
        part = jnp.where(core == 0, both[0], both[1])
        part = jnp.concatenate([part, jnp.zeros((part.shape[0], LANES - LINES), F32)], axis=1)
        found.append(jnp.concatenate([part, terms, jnp.zeros((MORE - part.shape[0] - 1, LANES), F32)], axis=0))
    return found


def cut(full, wide, narrow, vectors, came, target):
    few = LINES // 4
    for half, (mine, _) in enumerate(spots()):
        for role in range(2):
            first = mine if role else 1 - mine
            for second in range(2):
                ref = target(half, role, second)
                for z in range(4):
                    parts = []
                    if wide:
                        lanes = pl.ds(pl.multiple_of(first * 2 * LANES, 128) + (half * 4 + second) * LANES, LANES)
                        parts.append(full[z * LINES : (z + 1) * LINES, lanes])
                    rows = pl.ds(pl.multiple_of(first * 2 * few, 8) + z * LINES + second * few, few)
                    for n in range(narrow):
                        column = wide + (2 * n + half) * LANES
                        parts.append(full[rows, column : column + LANES])
                    if half == 0 and vectors is not None:
                        parts.append(jnp.where(first == 0, vectors[z], 0.0) if second == 0 else jnp.zeros((MORE, LANES), F32))
                    part = jnp.concatenate(parts, axis=0)
                    if came is not None:
                        part = part + came[4 * half + 2 * role + second][z].astype(F32)
                    ref[z] = part.astype(BF)


def in_product(ins, core, full, turned):
    low, pre, ctx, al = ins
    turned[...] = low.get()[...].T
    wide = pre.ref.shape[1]
    full[:, :wide] = dot(turned_rows(turned, core), pre.get()[...])
    turned[...] = ctx.get()[...].T
    full[:, wide:] = dot(turned_rows(turned, core), al.get()[...])
    return wide


def in_send_kernel(ins, outs, full, turned):
    _, _, _, core = place()
    wide = in_product(ins, 1 - core, full, turned)
    cut(full, wide, 1, None, None, lambda half, role, second: outs[4 * half + 2 * role + second].ref)


def in_keep_kernel(ins, outs, full, turned):
    _, _, _, core = place()
    wide = in_product(ins[:4], core, full, turned)
    came = [given.get() for given in ins[4:]]
    cut(full, wide, 1, None, came, lambda half, role, second: outs[2 * half + role].ref.at[second])


def rest_product(ins, core, full, turned):
    tok, *grads = ins
    turned[...] = tok.get()[...].T
    left = turned_rows(turned, core)
    for n, grad in enumerate(grads):
        width = grad.ref.shape[1]
        full[:, n * width : (n + 1) * width] = dot(left, grad.get()[...])


def rest_send_kernel(ins, outs, full, turned):
    _, _, _, core = place()
    rest_product(ins[:4], 1 - core, full, turned)
    cut(full, 0, 3, vector_lines(ins[4:8], 1 - core), None, lambda half, role, second: outs[4 * half + 2 * role + second].ref)


def rest_keep_kernel(ins, outs, full, turned):
    _, _, _, core = place()
    rest_product(ins[:4], core, full, turned)
    came = [given.get() for given in ins[8:]]
    cut(full, 0, 3, vector_lines(ins[4:8], core), came, lambda half, role, second: outs[2 * half + role].ref.at[second])


def plain(operands):
    return [(part, 0) for part in operands]


def cut_for_partner(body, name, ins, lines, scratch, after=()):
    outs = [((4, count, LANES), BF, "", 0) for count in lines for _ in range(4)]
    return kernel(body, name, ins, outs, scratch=scratch, after=after)


def cut_for_chips(body, name, ins, came, lines, scratch, after=()):
    outs = [((2, 4, count, LANES), BF, "", 0) for count in lines for _ in range(2)]
    return kernel(body, name, [*ins, *plain(came)], outs, scratch=scratch, after=after)


def halve_kernel(ins, outs):
    for n, (_, mine) in enumerate(spots()):
        kept, came = ins[2 * n].get(), ins[2 * n + 1].get()
        for out, second in ((outs[2 * n], 1 - mine), (outs[2 * n + 1], mine)):
            out.ref[...] = (kept[second].astype(F32) + came[second].astype(F32)).astype(BF)


def deal_kernel(ins, outs):
    _, _, z, _ = place()
    k0, r0, k1, r1 = [given.get() for given in ins[:4]]
    for n, out in enumerate(outs):
        sums = [kept[z ^ n].astype(F32) + came[z ^ n].astype(F32) for kept, came in ((k0, r0), (k1, r1))]
        out.ref[...] = jnp.concatenate(sums, axis=0).astype(BF)


def combine(body, name, operands, outs, after=(), scratch=()):
    return kernel(body, name, plain(operands), [(*out, "", 0) for out in outs], after=after, scratch=scratch)


def dp_sources(ins):
    x, y, _, _ = place()
    own, from_x, from_y, from_both = [given.get() for given in ins[:4]]
    return ((own, x, y), (from_x, 1 - x, y), (from_y, x, 1 - y), (from_both, 1 - x, 1 - y))


def hid_final_kernel(ins, outs, full):
    for ref, x, y in dp_sources(ins):
        size = ref.shape[0]
        full[pl.ds(pl.multiple_of((2 * x + y) * size, 16), size), :] = ref[...].astype(F32)
    outs[0].ref[...] = full[...].T


def fill(ins, wide, narrow, skipped):
    few = LINES // 4
    left = []
    for ref, x, y in dp_sources(ins):
        value = ref[...].astype(F32)
        size = (value.shape[0] - skipped) // 2
        left.append((value[size : size + skipped], 2 * x + y))
        for half, number in enumerate((2 * x + y, 2 * y + x)):
            part = value[half * (size + skipped) :][:size]
            if wide is not None:
                lanes = pl.ds(pl.multiple_of(number * LANES, 128) + half * 4 * LANES, LANES)
                wide[:, lanes] = part[:LINES]
                part = part[LINES:]
            rows = pl.ds(pl.multiple_of(number * few, 8), few)
            for n, out in enumerate(narrow):
                out[rows, half * LANES : (half + 1) * LANES] = part[n * few : (n + 1) * few]
    return left


def in_final_kernel(ins, outs):
    fill(ins, outs[0].ref, [outs[1].ref], 0)


def rest_final_kernel(questions, a, b, c, d, q, k, v, bq, bv, bo, bi, bh, g1, s1, g2, s2, loss, entropy):
    lines = jnp.zeros((MORE, LANES), F32)
    for value, number in fill([Given(None, ref) for ref in (a, b, c, d)], None, (q, k, v), MORE):
        lines = lines + jnp.where(number == 0, value, 0.0)
    for n, out in enumerate((bq, bv, bo, bh, g1, s1, g2, s2)):
        out[...] = lines[n, :LINES]
    bi[...] = jnp.concatenate([lines[8 + n : 9 + n, :LINES] for n in range(4)], axis=1).reshape(4 * LINES)
    nll, ent = jnp.sum(lines[12:13, :96]), jnp.sum(lines[12:13, 96:192])
    loss[0, 0] = (nll + ENTROPY_WEIGHT * ent) / questions
    entropy[0, 0] = ent / questions


def rest_final(pieces, questions, width):
    part, deep = width // 8, width // 2
    vectors = [shape((size,), F32) for size in (part, part, part, deep, part, part, part, part, part)]
    return pl.pallas_call(
        functools.partial(rest_final_kernel, questions),
        out_shape=[shape((part, width), F32)] * 3 + vectors + [shape((1, 1), F32)] * 2,
        in_specs=[whole()] * 4,
        out_specs=[whole()] * 12 + [whole(pltpu.SMEM)] * 2,
        compiler_params=params(12),
        cost_estimate=cost(0, MIB),
        name="rest_final",
    )(*pieces)


def halve(name, operands, lines, after=()):
    outs = [((4, count, LANES), BF) for count in lines for _ in range(2)]
    return combine(halve_kernel, name, operands, outs, after=after)


def deal(name, halves, lines, after=()):
    send0, kept0, send1, kept1 = halves
    operands = (kept0, exchange(send0, over_y), kept1, exchange(send1, over_x))
    return combine(deal_kernel, name, operands, [((sum(lines), LANES), BF)] * 4, after=after)


def total(name, parts, after=()):
    came = [exchange(parts[n], over_z(n)) for n in (1, 2, 3)]
    return combine(sum_kernel, name, (parts[0], *came), [(parts[0].shape, BF)], after=after)[0]


def on_this_slice(
    tokens, upstream, w_query, w_key, w_value, w_out, w_in, w_hid, b_query, b_value, b_out, b_in, b_hid,
    gain_one, shift_one, gain_two, shift_two, passages, slots, counts, gen_loglik,
):
    rows, width = tokens.shape
    deep = w_in.shape[1]
    questions = slots.shape[0] * lax.axis_size("dp")
    cls, q, k, v, vec = project(
        (
            tokens, w_key, w_value, w_query, b_value, b_query, w_out, b_out, gain_one, shift_one, w_in, b_in, w_hid, b_hid,
            gain_two, shift_two,
        )
    )
    own = [cls] + [exchange(cls, over_z(n)) for n in (1, 2, 3)]
    near_passages, found = mark(passages, slots.T)
    mine = kernel(collect_kernel, "collect", plain(own), [((4 * cls.shape[0], width), BF, "", 0)], after=(found,))[0]
    record = search(mine, exchange(mine, over_core), near_passages, found)
    cuts = meet(record, exchange(record, over_core))
    records = [cuts[0]] + [exchange(cuts[n], over_z(n)) for n in (1, 2, 3)]
    p, ctx, n1, i1, low, n1_near, low_near = attend(q, k, v, tokens, w_out, vec, after=(cuts[0],))
    act, slope, encoded, sum_two, back, first, sums = forward(low_near, n1_near, vec, w_in, w_hid, upstream)
    back_near, fix, lead_vec, hid_cut, back = lead(records, cls, counts, gen_loglik.T, first, sums, vec, back, act)
    hid_came = exchange(hid_cut, over_core)
    pre_near, slope_vec, pre = slope_part(back_near, w_hid, slope)
    attend_low, descend_vec, one, grad = descend(pre_near, w_in, fix, sum_two, n1, i1, vec, w_out)
    few = LINES // 4
    scratch = [pltpu.VMEM((4 * LINES, deep + width), F32), pltpu.VMEM((width, rows), BF)]
    lines = (LINES + few, LINES + few)
    in_cut = cut_for_partner(in_send_kernel, "in_send", plain((low, pre_near, ctx, attend_low)), lines, scratch)
    in_came = [exchange(part, over_core) for part in in_cut]
    block = (width, deep // 8)
    hid_sent, hid_kept = kernel(
        hid_keep_kernel, "hid_keep", plain((back, act, hid_came)), [((2, *block), BF, "", 0)] * 2,
        scratch=[pltpu.VMEM((width, deep // 2), F32)], after=(in_cut[0],),
    )
    hid_came = exchange(hid_sent, over_z_by_core(0))
    into = cut_for_chips(
        in_keep_kernel, "in_keep", plain((low, pre, ctx, attend_low)), in_came, lines, scratch, after=(hid_kept,)
    )
    first_x, first_y = exchange(into[0], over_x), exchange(into[2], over_y)
    dq, dk, dv, unattend_vec, input_grad = unattend(grad, p, q, k, v, one, w_query, w_key, w_value, after=(into[1],))
    operands = plain((tokens, dq, dk, dv, lead_vec, slope_vec, descend_vec, unattend_vec))
    scratch = [pltpu.VMEM((4 * LINES, 3 * width), F32), pltpu.VMEM((width, rows), BF)]
    more = (3 * few + MORE, 3 * few)
    rest_cut = cut_for_partner(rest_send_kernel, "rest_send", operands, more, scratch)
    rest_came = [exchange(part, over_core) for part in rest_cut]
    in_halves = halve("in_halve", (into[1], first_x, into[3], first_y), lines, after=(rest_cut[0],))
    rest = cut_for_chips(rest_keep_kernel, "rest_keep", operands, rest_came, more, scratch, after=(in_halves[0],))
    rest_first = exchange(rest[0], over_x), exchange(rest[2], over_y)
    hid_sum = combine(hid_pair_kernel, "hid_pair", (hid_kept, hid_came), [(block, BF)], after=(rest[1],))[0]
    hid_last = exchange(hid_sum, over_z_by_core(1))
    in_parts = deal("in_deal", in_halves, lines, after=(hid_sum,))
    rest_halves = halve("rest_halve", (rest[1], rest_first[0], rest[3], rest_first[1]), more, after=(in_parts[0],))
    small = ((width // 4, deep // 8), BF)
    hid_parts = combine(
        hid_deal_kernel, "hid_deal", (hid_kept, hid_came, hid_last), [small] * 4, after=(rest_halves[0],)
    )
    rest_parts = deal("rest_deal", rest_halves, more, after=(hid_parts[0],))
    in_total = total("in_total", in_parts, after=(rest_parts[0],))
    came = [exchange(hid_parts[n], move) for n, move in ((1, over_x), (2, over_y), (3, over_both))]
    hid_total = combine(sum_kernel, "hid_total", (hid_parts[0], *came), [small], after=(in_total,))[0]
    rest_total = total("rest_total", rest_parts, after=(hid_total,))
    in_pieces, hid_pieces, rest_pieces = [
        (mine, exchange(mine, over_x), exchange(mine, over_y), exchange(mine, over_both))
        for mine in (in_total, hid_total, rest_total)
    ]
    grad_hid = combine(
        hid_final_kernel, "hid_final", hid_pieces, [((deep // 8, width), F32)], scratch=[pltpu.VMEM((width, deep // 8), F32)],
        after=(rest_total,),
    )[0]
    grad_in, grad_out = combine(
        in_final_kernel, "in_final", in_pieces, [((LINES, deep), F32), ((LINES, width), F32)], after=(rest_total,)
    )
    *rest, loss, entropy = rest_final(rest_pieces, questions, width)
    return (
        encoded, input_grad, loss.reshape(()), entropy.reshape(()), *rest[:3], grad_out, grad_in, grad_hid, *rest[3:],
    )


PRECISE = lax.Precision.HIGHEST


def shortened(array):

    def short(part):
        return part.astype(jnp.bfloat16) if part.dtype == jnp.float32 else part

    return jax.tree.map(short, array)


def product(left_side, right_side):
    return jnp.dot(left_side, right_side, preferred_element_type=jnp.float32)


def times_transpose(left_side, right_side):
    return lax.dot_general(
        left_side, right_side, (((1,), (1,)), ((), ())), preferred_element_type=jnp.float32
    )


def transpose_times(left_side, right_side):
    return lax.dot_general(
        left_side, right_side, (((0,), (0,)), ((), ())), preferred_element_type=jnp.float32
    )


def plain_norm_forward(values, gain_vector, offset):
    center = values - jnp.mean(values, axis=-1, keepdims=True)
    inverse = lax.rsqrt(jnp.mean(center * center, axis=-1, keepdims=True) + NORM_EPSILON)
    normed = center * inverse
    return (normed * gain_vector + offset, normed, inverse)


def plain_norm_backward(incoming, normed, inverse, gain_vector):
    scaled = incoming * gain_vector
    inner = (
        scaled
        - jnp.mean(scaled, axis=-1, keepdims=True)
        - normed * jnp.mean(scaled * normed, axis=-1, keepdims=True)
    )
    return (inverse * inner, jnp.sum(incoming * normed, axis=0), jnp.sum(incoming, axis=0))


def gelu_slope(values):
    cumulative = 0.5 * (1.0 + jax.scipy.special.erf(values * 0.7071067811865476))
    return (
        values * cumulative,
        cumulative + values * jnp.exp(-0.5 * values * values) * 0.3989422804014327,
    )


def on_any_slice(
    tokens,
    upstream,
    w_query,
    w_key,
    w_value,
    w_out,
    w_in,
    w_hid,
    b_query,
    b_value,
    b_out,
    b_in,
    b_hid,
    gain_one,
    shift_one,
    gain_two,
    shift_two,
    passages,
    slots,
    counts,
    gen_loglik,
):
    tok_rows, model_width = tokens.shape
    seq_count = tok_rows // SEQ
    heads_shape = (seq_count, SEQ, HEADS, HDIM)
    inputs = tokens.astype(jnp.float32)
    queries = (product(tokens, w_query) + b_query).astype(jnp.bfloat16).reshape(heads_shape)
    keys_all = product(tokens, w_key).astype(jnp.bfloat16).reshape(heads_shape)
    values_all = (product(tokens, w_value) + b_value).astype(jnp.bfloat16).reshape(heads_shape)
    scores = (
        jnp.einsum("bqhd,bkhd->bhqk", queries, keys_all, preferred_element_type=jnp.float32) * 0.125
    )
    peak = jnp.max(scores, axis=-1, keepdims=True)
    log_total = peak + jnp.log(jnp.sum(jnp.exp(scores - peak), axis=-1, keepdims=True))
    weights_low = jnp.exp(scores - log_total).astype(jnp.bfloat16)
    context = jnp.einsum(
        "bhqk,bkhd->bqhd", weights_low, values_all, preferred_element_type=jnp.float32
    )
    context = context.reshape(tok_rows, model_width).astype(jnp.bfloat16)
    attended = product(context, w_out) + b_out
    hidden_one, normed_one, inverse_one = plain_norm_forward(inputs + attended, gain_one, shift_one)
    hidden_low = hidden_one.astype(jnp.bfloat16)
    pre_act = product(hidden_low, w_in) + b_in
    activated, slope = gelu_slope(pre_act)
    act_low = activated.astype(jnp.bfloat16)
    branch = product(act_low, w_hid) + b_hid
    outputs, normed_two, inverse_two = plain_norm_forward(hidden_one + branch, gain_two, shift_two)
    cls_low = outputs[::SEQ].astype(jnp.bfloat16)
    index_scores = times_transpose(lax.all_gather(cls_low, "index", axis=0, tiled=True), passages)
    group_rows, local_rows = index_scores.shape
    first_row = lax.axis_index("index") * local_rows
    local_slots = slots - first_row
    onehot = (
        lax.broadcasted_iota(jnp.int32, (1, 1, local_rows), 2) == local_slots[:, :, None]
    ).astype(jnp.float32)
    picked_part = jnp.einsum("qr,qsr->qs", index_scores, onehot, precision=PRECISE)
    row_peak = jnp.max(index_scores, axis=1)
    peak_all = lax.pmax(row_peak, "index")
    total_part = jnp.sum(jnp.exp(index_scores - peak_all[:, None]), axis=1)
    total_all, picked = lax.psum((total_part, picked_part), "index")
    index_lse = peak_all + jnp.log(total_all)
    valid = lax.broadcasted_iota(jnp.int32, picked.shape, 1) < counts[:, None]
    joint = picked - index_lse[:, None] + gen_loglik
    masked = jnp.where(valid, joint, -1e30)
    best = jnp.max(masked, axis=1, keepdims=True)
    marginal = best[:, 0] + jnp.log(jnp.sum(jnp.exp(masked - best), axis=1))
    centered = jnp.where(valid, joint - marginal[:, None], 0.0)
    posterior = jnp.where(valid, jnp.exp(masked - marginal[:, None]), 0.0)
    entropy_rows = -jnp.sum(posterior * centered, axis=1)
    nll_total, entropy_total = lax.psum((jnp.sum(-marginal), jnp.sum(entropy_rows)), "dp")
    questions = group_rows * lax.axis_size("dp")
    loss = (nll_total + ENTROPY_WEIGHT * entropy_total) / questions
    entropy = entropy_total / questions
    picked_grad = jnp.where(
        valid, -posterior * (1.0 + ENTROPY_WEIGHT * (centered + entropy_rows[:, None])), 0.0
    )
    score_grad = jnp.exp(index_scores - index_lse[:, None]) + jnp.einsum(
        "qs,qsr->qr", picked_grad, onehot, precision=PRECISE
    )
    score_low = score_grad.astype(jnp.bfloat16)
    cls_grad = lax.psum_scatter(
        product(score_low, passages), "index", scatter_dimension=0, tiled=True
    )
    out_grad = (
        upstream.astype(jnp.float32).reshape(seq_count, SEQ, model_width).at[:, 0].add(cls_grad)
    )
    out_grad = out_grad.reshape(tok_rows, model_width)
    sum_two, grad_gain_two, grad_shift_two = plain_norm_backward(
        out_grad, normed_two, inverse_two, gain_two
    )
    branch_low = sum_two.astype(jnp.bfloat16)
    grad_b_hid = jnp.sum(branch_low.astype(jnp.float32), axis=0)
    grad_w_hid = transpose_times(act_low, branch_low)
    pre_low = (times_transpose(branch_low, w_hid) * slope).astype(jnp.bfloat16)
    grad_b_in = jnp.sum(pre_low.astype(jnp.float32), axis=0)
    grad_w_in = transpose_times(hidden_low, pre_low)
    sum_one, grad_gain_one, grad_shift_one = plain_norm_backward(
        sum_two + times_transpose(pre_low, w_in), normed_one, inverse_one, gain_one
    )
    attend_low = sum_one.astype(jnp.bfloat16)
    grad_b_out = jnp.sum(attend_low.astype(jnp.float32), axis=0)
    grad_w_out = transpose_times(context, attend_low)
    context_grad = times_transpose(attend_low, w_out).astype(jnp.bfloat16).reshape(heads_shape)
    scores_again = (
        jnp.einsum("bqhd,bkhd->bhqk", queries, keys_all, preferred_element_type=jnp.float32) * 0.125
    )
    weights_again = jnp.exp(scores_again - log_total)
    again_low = weights_again.astype(jnp.bfloat16)
    weight_grad = jnp.einsum(
        "bqhd,bkhd->bhqk", context_grad, values_all, preferred_element_type=jnp.float32
    )
    value_grad = jnp.einsum(
        "bhqk,bqhd->bkhd", again_low, context_grad, preferred_element_type=jnp.float32
    )
    value_grad = value_grad.reshape(tok_rows, model_width).astype(jnp.bfloat16)
    logit_grad = weights_again * (
        weight_grad - jnp.sum(weight_grad * weights_again, axis=-1, keepdims=True)
    )
    logit_low = logit_grad.astype(jnp.bfloat16)
    query_grad = (
        jnp.einsum("bhqk,bkhd->bqhd", logit_low, keys_all, preferred_element_type=jnp.float32)
        * 0.125
    )
    query_grad = query_grad.reshape(tok_rows, model_width).astype(jnp.bfloat16)
    key_grad = (
        jnp.einsum("bhqk,bqhd->bkhd", logit_low, queries, preferred_element_type=jnp.float32)
        * 0.125
    )
    key_grad = key_grad.reshape(tok_rows, model_width).astype(jnp.bfloat16)
    input_grad = (
        sum_one
        + times_transpose(query_grad, w_query)
        + times_transpose(key_grad, w_key)
        + times_transpose(value_grad, w_value)
    ).astype(jnp.bfloat16)
    grad_w_query = transpose_times(tokens, query_grad)
    grad_w_key = transpose_times(tokens, key_grad)
    grad_w_value = transpose_times(tokens, value_grad)
    grad_b_query = jnp.sum(query_grad.astype(jnp.float32), axis=0)
    grad_b_value = jnp.sum(value_grad.astype(jnp.float32), axis=0)
    shares = (
        lax.psum_scatter(grad_w_query, "index", scatter_dimension=0, tiled=True),
        lax.psum_scatter(grad_w_key, "index", scatter_dimension=0, tiled=True),
        lax.psum_scatter(grad_w_value, "index", scatter_dimension=0, tiled=True),
        lax.psum_scatter(grad_w_out, "index", scatter_dimension=0, tiled=True),
        lax.psum_scatter(grad_w_in, "index", scatter_dimension=0, tiled=True),
        lax.psum_scatter(grad_w_hid, "index", scatter_dimension=0, tiled=True),
        lax.psum_scatter(grad_b_query, "index", scatter_dimension=0, tiled=True),
        lax.psum_scatter(grad_b_value, "index", scatter_dimension=0, tiled=True),
        lax.psum_scatter(grad_b_out, "index", scatter_dimension=0, tiled=True),
        lax.psum_scatter(grad_b_in, "index", scatter_dimension=0, tiled=True),
        lax.psum_scatter(grad_b_hid, "index", scatter_dimension=0, tiled=True),
        lax.psum_scatter(grad_gain_one, "index", scatter_dimension=0, tiled=True),
        lax.psum_scatter(grad_shift_one, "index", scatter_dimension=0, tiled=True),
        lax.psum_scatter(grad_gain_two, "index", scatter_dimension=0, tiled=True),
        lax.psum_scatter(grad_shift_two, "index", scatter_dimension=0, tiled=True),
    )
    summed = jax.tree.map(
        lambda part: part.astype(jnp.float32), lax.psum(shortened(tuple(shares)), "dp")
    )
    return (outputs.astype(jnp.bfloat16), input_grad, loss, entropy) + tuple(summed)


def solution(mesh):
    here = (mesh.shape["dp"], mesh.shape["index"]) == (4, 8)
    return jax.shard_map(
        on_this_slice if here else on_any_slice,
        mesh=mesh,
        in_specs=(
            P(("dp", "index"), None),
            P(("dp", "index"), None),
            P(),
            P(),
            P(),
            P(),
            P(),
            P(),
            P(),
            P(),
            P(),
            P(),
            P(),
            P(),
            P(),
            P(),
            P(),
            P("index", None),
            P("dp", None),
            P("dp"),
            P("dp", None),
        ),
        out_specs=(
            P(("dp", "index"), None),
            P(("dp", "index"), None),
            P(),
            P(),
            P("index", None),
            P("index", None),
            P("index", None),
            P("index", None),
            P("index", None),
            P("index", None),
            P("index"),
            P("index"),
            P("index"),
            P("index"),
            P("index"),
            P("index"),
            P("index"),
            P("index"),
            P("index"),
        ),
        check_vma=False,
    )
```

```python
import functools
import math

import jax
import jax.numpy as jnp
from jax import lax
from jax.experimental import pallas as pl
from jax.experimental.pallas import tpu as pltpu
from jax.sharding import PartitionSpec as P

HEADS = 12
FEED_PART = 256
SLOT_RECORDS = 13
RECORD_ROWS = 64
HDIM = 64
SEQ = 128
NORM_EPSILON = 1e-06
ENTROPY_WEIGHT = 0.5
BF = jnp.bfloat16
F32 = jnp.float32
MIB = 1 << 20
NEGATIVE = -1e30
WORK = {"in_deal": 5e9, "rest_deal": 1, "hid_deal": 1, "hid_pair": 1}


def dot(left, right):
    return jnp.dot(left, right, preferred_element_type=F32)


def dot_nt(left, right):
    return lax.dot_general(left, right, (((1,), (1,)), ((), ())), preferred_element_type=F32)


def dot_tn(left, right):
    return lax.dot_general(left, right, (((0,), (0,)), ((), ())), preferred_element_type=F32)


B_QUERY, B_VALUE, B_OUT, GAIN_ONE, SHIFT_ONE, B_HID, GAIN_TWO, SHIFT_TWO, B_IN = range(9)


def line(ref, n):
    return ref[n : n + 1, :]


def norm_forward(values):
    center = values - jnp.mean(values, axis=-1, keepdims=True)
    inverse = lax.rsqrt(jnp.mean(center * center, axis=-1, keepdims=True) + NORM_EPSILON)
    return center * inverse, inverse


def norm_backward(scaled, normed, inverse):
    return inverse * (
        scaled
        - jnp.mean(scaled, axis=-1, keepdims=True)
        - normed * jnp.mean(scaled * normed, axis=-1, keepdims=True)
    )


def gelu_and_slope(values):
    cumulative = 0.5 * (1.0 + lax.erf(values * 0.7071067811865476))
    bell = jnp.exp(-0.5 * values * values)
    return values * cumulative, cumulative + values * bell * 0.3989422804014327


def whole(memory=pltpu.VMEM):
    return pl.BlockSpec(memory_space=memory)


def params(limit):
    return pltpu.CompilerParams(vmem_limit_bytes=limit * MIB)


def cost(flops, moved):
    return pl.CostEstimate(flops=int(flops), bytes_accessed=int(moved), transcendentals=0)


def shape(dims, dtype):
    return jax.ShapeDtypeStruct(dims, dtype)


class Given:
    def __init__(self, held, ref, sems=None, parts=0, axis=0):
        self.ref, self.sems, self.parts = ref, sems, parts
        self.waiting = []
        if parts:
            size = ref.shape[axis] // parts
            for n in range(parts):
                cut = (slice(None),) * axis + (pl.ds(n * size, size),)
                source, target = (held, ref) if parts == 1 else (held.at[cut], ref.at[cut])
                self.waiting.append(pltpu.make_async_copy(source, target, sems.at[n]))

    def start(self):
        for copy in self.waiting:
            copy.start()

    def get(self, part=None):
        for n in range(self.parts) if part is None else (part,):
            if self.parts and self.waiting[n] is not None:
                self.waiting[n].wait()
                self.waiting[n] = None
        return self.ref


class Made:
    def __init__(self, ref, far=None, sems=None, parts=0):
        self.ref, self.far, self.sems, self.parts = ref, far, sems, parts
        self.running = []

    def put(self, part=None):
        if not self.parts:
            return
        for n in range(self.parts) if part is None else (part,):
            size = self.ref.shape[0] // self.parts
            cut = pl.ds(n * size, size)
            source, target = (self.ref, self.far) if self.parts == 1 else (self.ref.at[cut], self.far.at[cut])
            copy = pltpu.make_async_copy(source, target, self.sems.at[n])
            copy.start()
            self.running.append(copy)


def kernel(body, name, ins, outs, scratch=(), flops=0, moved=MIB, after=()):
    ins, axes = [part[:2] for part in ins], [(*part, 0)[2] for part in ins]
    operands = [pltpu.with_memory_space_constraint(a, pltpu.HBM) if parts else a for a, parts in ins]
    in_specs = [whole(pl.ANY if parts else pltpu.VMEM) for _, parts in ins]
    operands += after
    in_specs += [whole(pl.ANY)] * len(after)
    near = [(shape if not kind else pltpu.VMEM)(dims, dtype) for dims, dtype, kind, _ in outs if kind != "far"]
    far = [pltpu.HBM(dims, dtype) for dims, dtype, kind, _ in outs if kind in ("far", "both")]
    extra = [pltpu.VMEM(a.shape, a.dtype) for a, parts in ins if parts]
    extra += [pltpu.SemaphoreType.DMA((parts,)) for _, parts in ins if parts]
    extra += [pltpu.VMEM(dims, dtype) for dims, dtype, kind, _ in outs if kind == "far"]
    extra += [pltpu.SemaphoreType.DMA((parts,)) for _, _, _, parts in outs if parts]
    buffers = [part for part in extra + list(scratch) if hasattr(part, "shape") and part.memory_space == pltpu.VMEM]
    limit = sum(math.prod(part.shape) * jnp.dtype(part.dtype).itemsize for part in buffers) // MIB + 8

    def run(*refs):
        refs = list(refs)

        def take(count):
            taken, refs[:] = refs[:count], refs[count:]
            return taken

        given, _, near_refs, far_refs = take(len(ins)), take(len(after)), take(len(near)), take(len(far))
        copied = [n for n, (_, parts) in enumerate(ins) if parts]
        buffers, in_sems = take(len(copied)), take(len(copied))
        results, out_sems = take(sum(kind == "far" for _, _, kind, _ in outs)), take(len(far))
        arguments = []
        for n, (_, parts) in enumerate(ins):
            if parts:
                at = copied.index(n)
                arguments.append(Given(given[n], buffers[at], in_sems[at], parts, axes[n]))
            else:
                arguments.append(Given(None, given[n]))
        for argument in arguments:
            argument.start()
        made = []
        for _, _, kind, parts in outs:
            ref = results.pop(0) if kind == "far" else near_refs.pop(0)
            made.append(Made(ref, far_refs.pop(0), out_sems.pop(0), parts) if parts else Made(ref))
        body(arguments, made, *refs)
        for argument in arguments:
            argument.get()
        for result in made:
            for copy in result.running:
                copy.wait()

    return pl.pallas_call(
        run,
        out_shape=near + far,
        in_specs=in_specs,
        out_specs=[whole()] * len(near) + [whole(pl.ANY)] * len(far),
        scratch_shapes=extra + list(scratch),
        compiler_params=params(limit),
        cost_estimate=cost(WORK.get(name, 1), 1),
        name=name,
    )(*operands)


def place():
    dp, index = lax.axis_index("dp"), lax.axis_index("index")
    return dp % 2, dp // 2, index // 2, index % 2


def exchange(array, move):
    pairs = []
    for dp in range(4):
        for index in range(8):
            y, x, z, core = move(dp // 2, dp % 2, index // 2, index % 2)
            pairs.append((dp * 8 + index, (y * 2 + x) * 8 + z * 2 + core))
    return lax.ppermute(array, ("dp", "index"), pairs)


def over_core(y, x, z, core):
    return y, x, z, 1 - core


def over_plane(turn):
    return lambda y, x, z, core: (y ^ ((core + turn + 1) % 2 == 0), x ^ ((core + turn) % 2 == 0), z, core)


def over_both(y, x, z, core):
    return 1 - y, 1 - x, z, core


def over_z_by_core(turn):
    return lambda y, x, z, core: (y, x, z ^ (1 + (core + turn) % 2), core)


def over_z(step):
    return lambda y, x, z, core: (y, x, z ^ step, core)


def project_kernel(ins, outs):
    tok, wk, wv, wq, bv, bq, wo, bo, g1, s1, wi, bi, wh, bh, g2, s2 = ins
    q_out, k_out, v_out, cls_out, vec_out = outs
    row = lambda given: given.get()[...].reshape(1, -1)
    tokens = tok.get()
    k_out.ref[...] = dot(tokens[...], wk.get()[...]).astype(BF)
    k_out.put()
    v_out.ref[...] = (dot(tokens[...], wv.get()[...]) + row(bv)).astype(BF)
    v_out.put()
    q_out.ref[...] = (dot(tokens[...], wq.get()[...]) + row(bq)).astype(BF)
    q_out.put()
    rows, width = tokens.shape
    count = rows // SEQ
    head_rows = 16
    owned = lax.broadcasted_iota(jnp.int32, (head_rows, width), 1) // HDIM == lax.broadcasted_iota(
        jnp.int32, (head_rows, width), 0
    )
    contexts, firsts = [], []
    for b in range(count):
        query = q_out.ref[b * SEQ : b * SEQ + 16, :][:1].astype(F32)
        spread = jnp.where(owned, query, 0.0).astype(BF)
        scores = dot_nt(spread, k_out.ref[b * SEQ : (b + 1) * SEQ, :]) * 0.125
        raised = jnp.exp(scores - jnp.max(scores, axis=1, keepdims=True))
        weights = (raised / jnp.sum(raised, axis=1, keepdims=True)).astype(BF)
        mixed = dot(weights, v_out.ref[b * SEQ : (b + 1) * SEQ, :])
        contexts.append(jnp.sum(jnp.where(owned, mixed, 0.0), axis=0, keepdims=True))
        firsts.append(tokens[b * SEQ : b * SEQ + 16, :][:1].astype(F32))
    context = jnp.concatenate(contexts + contexts, axis=0).astype(BF)
    first = jnp.concatenate(firsts + firsts, axis=0)
    attended = dot(context, wo.get()[...]) + row(bo)
    normed, _ = norm_forward(first + attended)
    hidden = normed * row(g1) + row(s1)
    flat = row(bi)
    act, _ = gelu_and_slope(dot(hidden.astype(BF), wi.get()[...]) + flat)
    branch = dot(act.astype(BF), wh.get()[...]) + row(bh)
    normed, _ = norm_forward(hidden + branch)
    lines = lax.broadcasted_iota(jnp.int32, (2 * count, width), 0)
    mine = lines // count == lax.axis_index("index") % 2
    cls_out.ref[...] = jnp.where(mine, normed * row(g2) + row(s2), 0.0).astype(BF)
    cls_out.put()
    for n, vector in enumerate((bq, bv, bo, g1, s1, bh, g2, s2)):
        vec_out.ref[n : n + 1, :] = row(vector)
    for n in range(flat.shape[1] // width):
        vec_out.ref[B_IN + n : B_IN + n + 1, :] = flat[:, n * width : (n + 1) * width]
    vec_out.ref[B_IN + flat.shape[1] // width :, :] = jnp.zeros((16 - B_IN - flat.shape[1] // width, width), F32)
    vec_out.put()


def project(sources):
    rows, width = sources[0].shape
    outs = [((rows, width), BF, "both", 1)] * 3 + [((2 * (rows // SEQ), width), BF, "", 0), ((16, width), F32, "far", 1)]
    return kernel(
        project_kernel, "project", [(part, 1) for part in sources], outs, flops=8 * rows * width * width, moved=20 * MIB
    )


def stacked(pair):
    lane = lax.broadcasted_iota(jnp.int32, pair.shape, 1)
    zero = jnp.zeros_like(pair)
    return jnp.concatenate(
        [jnp.where(lane < HDIM, pair, zero), jnp.where(lane < HDIM, zero, pair)], axis=0
    )


def unstacked(tall):
    half = tall.shape[0] // 2
    lane = lax.broadcasted_iota(jnp.int32, (half, tall.shape[1]), 1)
    return jnp.where(lane < HDIM, tall[:half], tall[half:])


def attend_kernel(ins, outs):
    q, k, v, tok, wo, vec = ins
    p_out, ctx_out, n1_out, i1_out, low_out = outs
    rows, width = q.ref.shape
    pair = 2 * HDIM
    many = rows // SEQ
    for b in range(many):
        here = pl.ds(b * SEQ, SEQ)
        for given in (q, k, v):
            given.get(b)
        for h in range(width // pair):
            lanes = pl.ds(h * pair, pair)
            scores = dot_nt(q.ref[here, lanes], stacked(k.ref[here, lanes])) * 0.125
            parts = []
            for part in (scores[:, :SEQ], scores[:, SEQ:]):
                raised = jnp.exp(part - jnp.max(part, axis=1, keepdims=True))
                parts.append(raised * (1.0 / jnp.sum(raised, axis=1, keepdims=True)))
            weights = jnp.concatenate(parts, axis=1).astype(BF)
            p_out.ref[here, pl.ds(h * 2 * SEQ, 2 * SEQ)] = weights
            ctx_out.ref[here, lanes] = dot(weights, stacked(v.ref[here, lanes])).astype(BF)
        p_out.put(b)
    ctx_out.put()
    vectors, tokens, weights = vec.get(), tok.get(), wo.get()
    attended = dot(ctx_out.ref[...], weights[...]) + line(vectors, B_OUT)
    normed, inverse = norm_forward(tokens[...].astype(F32) + attended)
    n1_out.ref[...] = normed
    low_out.ref[...] = (normed * line(vectors, GAIN_ONE) + line(vectors, SHIFT_ONE)).astype(BF)
    i1_out.ref[...] = jnp.broadcast_to(inverse, i1_out.ref.shape)
    for out in (low_out, n1_out, i1_out):
        out.put()


def attend(q, k, v, tokens, wo, vec, after=()):
    rows, width = q.shape
    many = rows // SEQ
    outs = [
        ((rows, HEADS * SEQ), BF, "far", many),
        ((rows, width), BF, "far", 1),
        ((rows, width), F32, "both", 1),
        ((rows, 128), F32, "far", 1),
        ((rows, width), BF, "both", 1),
    ]
    ins = plain((q, k, v, tokens, wo, vec))
    n1_near, low_near, p, ctx, n1, i1, low = kernel(attend_kernel, "attend", ins, outs, after=after)
    return p, ctx, n1, i1, low, n1_near, low_near


def forward_kernel(ins, outs):
    low, n1, vec, wi, wh, up = ins
    act_out, slope_out, enc_out, back_out, sum_out, first_out, vec_out = outs
    rows, width = low.ref.shape
    vectors, weights = vec.get(), wi.get()
    for n in range(slope_out.ref.shape[0]):
        column = n * FEED_PART
        bias = vectors[B_IN + column // width : B_IN + column // width + 1, :][:, column % width : column % width + FEED_PART]
        value, steep = gelu_and_slope(dot(low.ref[...], weights[:, pl.ds(column, FEED_PART)]) + bias)
        act_out.ref[:, pl.ds(column, FEED_PART)] = value.astype(BF)
        slope_out.ref[n] = steep.astype(BF)
        slope_out.put(n)
    act_out.put()
    weights = wh.get()
    firsts, sums = [], []
    for n in range(enc_out.parts):
        size = rows // enc_out.parts
        here = pl.ds(n * size, size)
        branch = dot(act_out.ref[here, :], weights[...]) + line(vectors, B_HID)
        hidden = n1.ref[here, :] * line(vectors, GAIN_ONE) + line(vectors, SHIFT_ONE)
        normed, inverse = norm_forward(hidden + branch)
        enc_out.ref[here, :] = (normed * line(vectors, GAIN_TWO) + line(vectors, SHIFT_TWO)).astype(BF)
        enc_out.put(n)
        incoming = up.ref[here, :].astype(F32)
        back = norm_backward(incoming * line(vectors, GAIN_TWO), normed, inverse)
        sum_out.ref[here, :] = back
        sum_out.put(n)
        short = back.astype(BF)
        back_out.ref[here, :] = short
        wide = jnp.broadcast_to(inverse, normed.shape)
        firsts.append([[value[b : b + 1] for b in range(0, size, SEQ)] for value in (normed, incoming, wide)])
        sums.append(
            [
                jnp.sum(short.astype(F32), axis=0, keepdims=True),
                jnp.sum(incoming * normed, axis=0, keepdims=True),
                jnp.sum(incoming, axis=0, keepdims=True),
            ]
        )
    lines = [part for n in range(3) for block in firsts for part in block[n]]
    first_out.ref[...] = jnp.concatenate(lines + [jnp.zeros((16 - len(lines), width), F32)], axis=0)
    vec_out.ref[...] = jnp.concatenate(
        [functools.reduce(jnp.add, [block[n] for block in sums]) for n in range(3)] + [jnp.zeros((5, width), F32)], axis=0
    )


def forward(low, n1, vec, wi, wh, up, after=()):
    rows, width = low.shape
    deep = wi.shape[1]
    outs = [
        ((rows, deep), BF, "far", 1),
        ((deep // FEED_PART, rows, FEED_PART), BF, "far", deep // FEED_PART),
        ((rows, width), BF, "far", 2),
        ((rows, width), BF, "near", 0),
        ((rows, width), F32, "far", 2),
        ((16, width), F32, "", 0),
        ((8, width), F32, "", 0),
    ]
    ins = plain((low, n1, vec, wi, wh, up))
    back, first, sums, act, slope, encoded, sum_two = kernel(forward_kernel, "forward", ins, outs, after=after)
    return act, slope, encoded, sum_two, back, first, sums


def split(value, pieces):
    found = []
    for _ in range(pieces):
        piece = value.astype(BF).astype(F32)
        found.append(piece)
        value = value - piece
    return found


def packed_numbers(peak, total, width):
    lane = lax.broadcasted_iota(jnp.int32, (peak.shape[0], width), 1)
    packed = jnp.zeros((peak.shape[0], width), F32)
    for n, piece in enumerate(split(peak, 3) + split(total, 3)):
        packed = jnp.where(lane == n, piece, packed)
    return packed


def unpacked_numbers(packed):
    return (
        packed[:, 0:1] + packed[:, 1:2] + packed[:, 2:3],
        packed[:, 3:4] + packed[:, 4:5] + packed[:, 5:6],
    )


def mark_kernel(far_passages, far_slots, passages, found, slots, sems):
    copies = [
        pltpu.make_async_copy(far_slots, slots, sems.at[0]),
        pltpu.make_async_copy(far_passages, passages, sems.at[1]),
    ]
    for copy in copies:
        copy.start()
    copies[0].wait()
    _, _, z, core = place()
    many, count = slots.shape
    each = count // 4
    spot = lax.broadcasted_iota(jnp.int32, (count, count), 0)
    question = ((spot // each) ^ z) * each + spot % each
    chosen = lax.broadcasted_iota(jnp.int32, (count, count), 1) == question
    local = passages.shape[0]
    lane = lax.broadcasted_iota(jnp.int32, (count, local), 1)
    marks = []
    for j in range(many):
        ids = jnp.sum(jnp.where(chosen, slots[j : j + 1, :].astype(F32), 0.0), axis=1, keepdims=True)
        ids = ids.astype(jnp.int32) - (2 * z + core) * local
        marks.append(jnp.where(lane == ids, 1.0, 0.0).astype(BF))
    marks = jnp.concatenate(marks, axis=0)
    copies[1].wait()
    rows = dot(marks, passages[...]).astype(BF)
    for j in range(many):
        found[j] = rows[j * count : (j + 1) * count, :]


def mark(passages, slots):
    many, count = slots.shape
    local, width = passages.shape
    return pl.pallas_call(
        mark_kernel,
        out_shape=[pltpu.VMEM(passages.shape, BF), pltpu.VMEM((many, count, width), BF)],
        in_specs=[whole(pl.ANY)] * 2,
        out_specs=[whole()] * 2,
        scratch_shapes=[pltpu.VMEM(slots.shape, slots.dtype), pltpu.SemaphoreType.DMA((2,))],
        compiler_params=params(8),
        cost_estimate=cost(2 * many * count * local * width, 4 * MIB),
        name="mark",
    )(*[pltpu.with_memory_space_constraint(part, pltpu.HBM) for part in (passages, slots)])


def collect_kernel(ins, outs):
    outs[0].ref[...] = jnp.concatenate([given.ref[...].astype(F32) for given in ins], axis=0).astype(BF)


def search_kernel(ins, outs):
    mine, theirs, passages, found = [given.ref for given in ins]
    (out,) = outs
    many = found.shape[0]
    cls = (mine[...].astype(F32) + theirs[...].astype(F32)).astype(BF)
    out.ref[:many] = found[...]
    scores = dot_nt(cls, passages[...])
    width = passages.shape[1]
    peak = jnp.max(scores, axis=1, keepdims=True)
    raised = jnp.exp(scores - peak)
    total = jnp.sum(raised, axis=1, keepdims=True)
    mixed = dot(raised.astype(BF), passages[...])
    for n, piece in enumerate(split(mixed, 2)):
        out.ref[many + n] = piece.astype(BF)
    out.ref[many + 2] = packed_numbers(peak, total, width).astype(BF)


def search(mine, theirs, passages, found):
    local, width = passages.shape
    many, count, _ = found.shape
    outs = [((many + 3, count, width), BF, "", 0)]
    ins = [(part, 0) for part in (mine, theirs, passages, found)]
    return kernel(search_kernel, "search", ins, outs, flops=4 * count * local * width)[0]


def joined(records):
    peak = functools.reduce(jnp.maximum, [r[2] for r in records])
    scales = [jnp.exp(r[2] - peak) for r in records]
    rows = functools.reduce(jnp.add, [r[0] for r in records])
    mixed = functools.reduce(jnp.add, [r[1] * s for r, s in zip(records, scales)])
    total = functools.reduce(jnp.add, [r[3] * s for r, s in zip(records, scales)])
    return rows, mixed, peak, total


def meet_kernel(ins, outs):
    records = []
    for given in ins:
        array = given.get()[...].astype(F32)
        many = array.shape[0] - 3
        records.append((array[:many], array[many] + array[many + 1], *unpacked_numbers(array[many + 2])))
    rows, mixed, peak, total = joined(records)
    width = mixed.shape[1]
    lines = [rows[j] for j in range(rows.shape[0])] + split(mixed, 2) + [packed_numbers(peak, total, width)]
    each = mixed.shape[0] // 4
    half = each // 2
    first = lax.axis_index("index") % 2 == 0
    fill = [jnp.zeros((outs[0].ref.shape[0] - len(lines) * half, width), F32)]
    for n, out in enumerate(outs):
        cut = [part[n * each : (n + 1) * each] for part in lines]
        cut = [jnp.where(first, part[:half], part[half:]) for part in cut]
        out.ref[...] = jnp.concatenate(cut + fill, axis=0).astype(BF)
        out.put()


def meet(mine, theirs):
    outs = [((RECORD_ROWS, mine.shape[2]), BF, "", 0)] * 4
    return kernel(meet_kernel, "meet", [(mine, 0), (theirs, 0)], outs)


def question_grad(records, cls, counts, loglik):
    many = loglik.shape[0]
    asked = cls.shape[0] // 2
    parted = []
    for record in records:
        array = record[...].astype(F32)
        lines = [array[n * asked : (n + 1) * asked] for n in range(many + 3)]
        parted.append((jnp.stack(lines[:many]), lines[many] + lines[many + 1], *unpacked_numbers(lines[many + 2])))
    found, mixed, peak, total = joined(parted)
    lse = peak + jnp.log(total)
    index = lax.axis_index("index")
    both = cls[...].astype(F32)
    question = both[:asked] + both[asked:]
    lane = lax.broadcasted_iota(jnp.int32, (asked, many), 1)
    picked = jnp.zeros((asked, many), F32)
    for j in range(many):
        picked = jnp.where(lane == j, jnp.sum(question * found[j], axis=1, keepdims=True), picked)
    questions = loglik.shape[1]
    spot = lax.broadcasted_iota(jnp.int32, (asked, questions), 0) + index * asked
    chosen = lax.broadcasted_iota(jnp.int32, (asked, questions), 1) == spot
    near = jnp.zeros((asked, many), F32)
    for j in range(many):
        value = jnp.sum(jnp.where(chosen, loglik[j : j + 1, :], 0.0), axis=1, keepdims=True)
        near = jnp.where(lane == j, value, near)
    limits = counts[...].reshape(1, questions).astype(F32)
    limits = jnp.sum(jnp.where(chosen, limits, 0.0), axis=1, keepdims=True).astype(jnp.int32)
    valid = lane < limits
    joint = picked - lse + near
    masked = jnp.where(valid, joint, NEGATIVE)
    best = jnp.max(masked, axis=1, keepdims=True)
    marginal = best + jnp.log(jnp.sum(jnp.exp(masked - best), axis=1, keepdims=True))
    centered = jnp.where(valid, joint - marginal, 0.0)
    posterior = jnp.where(valid, jnp.exp(masked - marginal), 0.0)
    entropy = -jnp.sum(posterior * centered, axis=1, keepdims=True)
    picked_grad = jnp.where(valid, -posterior * (1.0 + ENTROPY_WEIGHT * (centered + entropy)), 0.0)
    grad = mixed * (1.0 / total)
    for j in range(many):
        grad = grad + picked_grad[:, j : j + 1] * found[j]
    return grad, jnp.sum(-marginal), jnp.sum(entropy)


def lead_kernel(ins, outs, full):
    r0, r1, r2, r3, cls, counts, loglik, first, sums, vec, back, act = ins
    back_out, fix_out, vec_out, send_out = outs
    records = [given.get() for given in (r0, r1, r2, r3)]
    grad, nll, entropy = question_grad(records, cls.get(), counts.get(), loglik.get())
    many, width = grad.shape
    normed, incoming, inverse = [first.ref[...][n * many : (n + 1) * many] for n in range(3)]
    gain = line(vec.get(), GAIN_TWO)
    old = norm_backward(incoming * gain, normed, inverse[:, :1])
    new = norm_backward((incoming + grad) * gain, normed, inverse[:, :1])
    low = new.astype(BF).astype(F32)
    fix_out.ref[...] = jnp.concatenate([new, jnp.zeros((8 - many, width), F32)], axis=0)
    back_out.ref[...] = back.get()[...]
    top = lax.broadcasted_iota(jnp.int32, (16, width), 0) == 0
    for b in range(many):
        here = pl.ds(b * SEQ, 16)
        rows = back_out.ref[here, :].astype(F32)
        back_out.ref[here, :] = jnp.where(top, low[b : b + 1], rows).astype(BF)
    back_out.put()
    spread = lax.broadcasted_iota(jnp.int32, (1, width), 1)
    numbers = jnp.where(spread == 0, nll, jnp.where(spread == 1, entropy, 0.0))
    old_sums = sums.ref[...]
    change = low - old.astype(BF).astype(F32)
    vec_out.ref[...] = jnp.concatenate(
        [
            old_sums[0:1] + jnp.sum(change, axis=0, keepdims=True),
            old_sums[1:2] + jnp.sum(grad * normed, axis=0, keepdims=True),
            old_sums[2:3] + jnp.sum(grad, axis=0, keepdims=True),
            numbers,
            jnp.zeros((4, width), F32),
        ],
        axis=0,
    )
    _, _, _, core = place()
    hid_product(1 - core, back_out.ref, act.get(), full)
    hid_send(send_out, full)


def lead(records, cls, counts, loglik, first, sums, vec, back, act):
    rows, width = back.shape
    deep = act.shape[1]
    outs = [
        ((rows, width), BF, "both", 1),
        ((8, width), F32, "", 0),
        ((8, width), F32, "", 0),
        ((4, width, deep // 8), BF, "", 0),
    ]
    ins = [(part, 0) for part in (*records, cls)] + [(counts, 1), (loglik, 1), (first, 0), (sums, 0), (vec, 1), (back, 0), (act, 1)]
    return kernel(
        lead_kernel, "lead", ins, outs, scratch=[pltpu.VMEM((width, deep // 2), F32)], flops=rows * width * deep
    )


def slope_kernel(ins, outs):
    low, wh, slope = ins
    pre_out, vec_out = outs
    parts = slope.ref.shape[0]
    width = low.ref.shape[1]
    biases = []
    for n in range(parts):
        here = pl.ds(n * FEED_PART, FEED_PART)
        pre = (dot_nt(low.ref[...], wh.ref[here, :]) * slope.ref[n].astype(F32)).astype(BF)
        pre_out.ref[:, here] = pre
        biases.append(jnp.sum(pre.astype(F32), axis=0, keepdims=True))
    pre_out.put()
    flat = jnp.concatenate(biases, axis=1)
    vec_out.ref[...] = jnp.concatenate(
        [flat[:, n * width : (n + 1) * width] for n in range(flat.shape[1] // width)] + [jnp.zeros((4, width), F32)], axis=0
    )


def descend_kernel(ins, outs):
    pre, wi, fix, sum_two, n1, i1, vec, wo = ins
    attend_out, one_out, grad_out, vec_out = outs
    rows, width = n1.ref.shape
    size = rows // one_out.parts
    gain = None
    sums = []
    spot = lax.broadcasted_iota(jnp.int32, (size, 1), 0)
    for n in range(one_out.parts):
        here = pl.ds(n * size, size)
        back = dot_nt(pre.ref[here, :], wi.ref[...])
        before = sum_two.get(n)[here, :]
        for b in range(size // SEQ):
            question = n * size // SEQ + b
            before = jnp.where(spot == b * SEQ, fix.ref[question : question + 1, :], before)
        incoming = before + back
        normed = n1.get(n)[here, :]
        gain = line(vec.get(), GAIN_ONE) if gain is None else gain
        one = norm_backward(incoming * gain, normed, i1.get()[here, :1])
        one_out.ref[here, :] = one
        one_out.put(n)
        attend_low = one.astype(BF)
        attend_out.ref[here, :] = attend_low
        grad_out.ref[here, :] = dot_nt(attend_low, wo.ref[...]).astype(BF)
        grad_out.put(n)
        sums.append(
            [
                jnp.sum(attend_low.astype(F32), axis=0, keepdims=True),
                jnp.sum(incoming * normed, axis=0, keepdims=True),
                jnp.sum(incoming, axis=0, keepdims=True),
            ]
        )
    vec_out.ref[...] = jnp.concatenate(
        [functools.reduce(jnp.add, [block[n] for block in sums]) for n in range(3)] + [jnp.zeros((5, width), F32)], axis=0
    )


def slope_part(low, wh, slope):
    rows, width = low.shape
    outs = [((rows, wh.shape[0]), BF, "both", 1), ((8, width), F32, "", 0)]
    return kernel(slope_kernel, "slope", plain((low, wh, slope)), outs)


def descend(pre, wi, fix, sum_two, n1, i1, vec, wo, after=()):
    rows, width = n1.shape
    outs = [
        ((rows, width), BF, "near", 0),
        ((rows, width), F32, "far", 2),
        ((rows, width), BF, "far", 2),
        ((8, width), F32, "", 0),
    ]
    ins = [(pre, 0), (wi, 0), (fix, 0), (sum_two, 2), (n1, 2), (i1, 1), (vec, 1), (wo, 0)]
    return kernel(descend_kernel, "descend", ins, outs, after=after)


def unattend_kernel(ins, outs):
    grad, p, q, k, v, one, wq, wk, wv = ins
    dq_out, dk_out, dv_out, input_out, vec_out = outs
    rows, width = q.ref.shape
    pair = 2 * HDIM
    pairs = range(width // pair)
    for b in range(rows // SEQ):
        here = pl.ds(b * SEQ, SEQ)
        lanes = [pl.ds(h * pair, pair) for h in pairs]
        weights = [p.ref[here, pl.ds(h * 2 * SEQ, 2 * SEQ)] for h in pairs]
        incoming = [grad.ref[here, at] for at in lanes]
        sloped = [dot_nt(incoming[h], stacked(v.ref[here, lanes[h]])) for h in pairs]
        values = [unstacked(dot_tn(weights[h], incoming[h])).astype(BF) for h in pairs]
        lows = []
        for h in pairs:
            parts = []
            for n in range(2):
                exact = weights[h][:, n * SEQ : (n + 1) * SEQ].astype(F32)
                steep = sloped[h][:, n * SEQ : (n + 1) * SEQ]
                parts.append(exact * (steep - jnp.sum(steep * exact, axis=1, keepdims=True)))
            lows.append(jnp.concatenate(parts, axis=1).astype(BF))
        queries = [(dot(lows[h], stacked(k.ref[here, lanes[h]])) * 0.125).astype(BF) for h in pairs]
        keys = [(unstacked(dot_tn(lows[h], q.ref[here, lanes[h]])) * 0.125).astype(BF) for h in pairs]
        for h in pairs:
            dv_out.ref[here, lanes[h]] = values[h]
            dq_out.ref[here, lanes[h]] = queries[h]
            dk_out.ref[here, lanes[h]] = keys[h]
    for out in (dq_out, dk_out, dv_out):
        out.put()
    input_out.ref[...] = (
        one.get()[...]
        + dot_nt(dq_out.ref[...], wq.get()[...])
        + dot_nt(dk_out.ref[...], wk.get()[...])
        + dot_nt(dv_out.ref[...], wv.get()[...])
    ).astype(BF)
    input_out.put()
    vec_out.ref[...] = jnp.concatenate(
        [
            jnp.sum(dq_out.ref[...].astype(F32), axis=0, keepdims=True),
            jnp.sum(dv_out.ref[...].astype(F32), axis=0, keepdims=True),
            jnp.zeros((6, width), F32),
        ],
        axis=0,
    )
    vec_out.put()


def unattend(grad, p, q, k, v, one, wq, wk, wv, after=()):
    rows, width = q.shape
    many = rows // SEQ
    outs = [((rows, width), BF, "near", 0)] * 3 + [((rows, width), BF, "far", 1), ((8, width), F32, "", 0)]
    ins = [(part, 0) for part in (grad, p, q, k, v, one, wq, wk, wv)]
    return kernel(unattend_kernel, "unattend", ins, outs, flops=8 * rows * width * width, after=after)


LINES = 96
LANES = 384
WIDTH = 768
MORE = 16


def hid_product(core, low, act, full):
    each = act.shape[1] // 8
    parts = [act[:, pl.ds(pl.multiple_of((2 * z + core) * each, 128), each)] for z in range(4)]
    full[...] = dot_tn(low[...], jnp.concatenate(parts, axis=1))


def hid_send(out, full):
    each = full.shape[1] // 4
    for z in range(4):
        out.ref[z] = full[:, z * each : (z + 1) * each].astype(BF)


def hid_keep_kernel(ins, outs, full):
    low, act, came = [given.get() for given in ins]
    _, _, z, core = place()
    hid_product(core, low, act, full)
    each = full.shape[1] // 4
    for n, far in enumerate((3, 1 + core, 2 - core, 0)):
        lanes = pl.ds(pl.multiple_of((z ^ far) * each, 128), each)
        outs[n // 2].ref[n % 2] = (full[:, lanes] + came[z ^ far].astype(F32)).astype(BF)


def sum_kernel(ins, outs):
    outs[0].ref[...] = functools.reduce(jnp.add, [given.get()[...].astype(F32) for given in ins]).astype(BF)


def pair_kernel(ins, outs):
    kept, came = [given.ref for given in ins]
    outs[0].ref[...] = (kept[0].astype(F32) + came[0].astype(F32)).astype(BF)


def hid_deal_kernel(ins, outs):
    first, _ = spots()
    kept, came, last = [given.ref for given in ins]
    size = outs[0].ref.shape[0]
    for out, number in zip(outs, (1 - first, first)):
        cut = pl.ds(pl.multiple_of(number * size, 16), size)
        out.ref[...] = (kept[1, cut, :].astype(F32) + came[1, cut, :].astype(F32) + last[cut, :].astype(F32)).astype(BF)


def hid_halve_kernel(ins, outs):
    _, second = spots()
    kept, came = [given.ref for given in ins]
    size = outs[0].ref.shape[0]
    for out, number in zip(outs, (1 - second, second)):
        cut = pl.ds(pl.multiple_of(number * size, 16), size)
        out.ref[...] = (kept[cut, :].astype(F32) + came[cut, :].astype(F32)).astype(BF)


def spots(other=0):
    x, y, _, core = place()
    core = core ^ other
    return jnp.where(core == 0, x, y), jnp.where(core == 0, y, x)


def turned_rows(turned, core):
    size = turned.shape[0] // 8
    return jnp.concatenate(
        [turned[pl.ds(pl.multiple_of((2 * z + core) * size, 16), size), :] for z in range(4)], axis=0
    )


def vector_lines(vectors, core):
    lead_vec, slope_vec, descend_vec, unattend_vec = [given.get() for given in vectors]
    eight = jnp.concatenate(
        [unattend_vec[0:2, :], descend_vec[0:1, :], lead_vec[0:1, :], descend_vec[1:3, :], lead_vec[1:3, :]], axis=0
    )
    deep = slope_vec[0:4, :]
    device = lax.axis_index("dp") * 8 + lax.axis_index("index")
    lane = lax.broadcasted_iota(jnp.int32, (1, LANES), 1)
    terms = jnp.zeros((1, LANES), F32)
    for n, piece in enumerate(split(lead_vec[3:4, 0:1], 3) + split(lead_vec[3:4, 1:2], 3)):
        terms = jnp.where(lane == 32 * n + device, piece, terms)
    found = []
    for z in range(4):
        both = []
        for index in (2 * z, 2 * z + 1):
            at = (index % 2) * LANES
            cuts = [eight[:, index * LINES : (index + 1) * LINES]]
            cuts += [deep[index // 2 : index // 2 + 1, at + n * LINES : at + (n + 1) * LINES] for n in range(4)]
            both.append(jnp.concatenate(cuts, axis=0))
        part = jnp.where(core == 0, both[0], both[1])
        part = jnp.concatenate([part, jnp.zeros((part.shape[0], LANES - LINES), F32)], axis=1)
        part = jnp.concatenate([part, terms, jnp.zeros((MORE - part.shape[0] - 1, LANES), F32)], axis=0)
        found.append(jnp.concatenate([part, jnp.zeros((MORE, WIDTH - LANES), F32)], axis=1))
    return found


def cut(full, wide, narrow, vectors, came, target, other=0):
    few = LINES // 4
    mine, _ = spots(other)
    for role in range(2):
        first = mine if role else 1 - mine
        for second in range(2):
            for z in range(4):
                parts = []
                if wide:
                    lanes = pl.ds(pl.multiple_of((first * 2 + second) * WIDTH, 128), WIDTH)
                    parts.append(full[z * LINES : (z + 1) * LINES, lanes])
                rows = pl.ds(pl.multiple_of(first * 2 * few, 8) + z * LINES + second * few, few)
                for n in range(narrow):
                    parts.append(full[rows, n * WIDTH : (n + 1) * WIDTH])
                if vectors is not None:
                    parts.append(jnp.where(first == 0, vectors[z], 0.0) if second == 0 else jnp.zeros((MORE, WIDTH), F32))
                part = jnp.concatenate(parts, axis=0)
                if came is not None:
                    part = part + came(role, second, z).astype(F32)
                target(role, second, z)[...] = part.astype(BF)


def in_product(ins, core, full, turned):
    low, pre = ins
    turned[...] = low.ref[...].T
    full[...] = dot(turned_rows(turned, core), pre.ref[...])
    return full.shape[1]


def in_send_kernel(ins, outs, full, turned):
    _, _, _, core = place()
    wide = in_product(ins, 1 - core, full, turned)
    cut(full, wide, 0, None, None, lambda role, second, z: outs[role].ref.at[second, z], 1)


def in_keep_kernel(ins, outs, full, turned):
    _, _, _, core = place()
    wide = in_product(ins[:2], core, full, turned)
    came = lambda role, second, z: ins[2 + role].ref[second, z]
    cut(full, wide, 0, None, came, lambda role, second, z: outs[role].ref.at[second, z])


def rest_product(ins, core, full, turned):
    tok, ctx, *grads = ins
    turned[...] = tok.ref[...].T
    left = turned_rows(turned, core)
    for n, grad in enumerate(grads):
        width = grad.ref.shape[1]
        if n == len(grads) - 1:
            turned[...] = ctx.ref[...].T
            left = turned_rows(turned, core)
        full[:, n * width : (n + 1) * width] = dot(left, grad.ref[...])


def rest_send_kernel(ins, outs, full, turned):
    _, _, _, core = place()
    rest_product(ins[:6], 1 - core, full, turned)
    vectors = vector_lines(ins[6:10], 1 - core)
    def target(role, second, z):
        array, at = unit(role, second, z)
        return outs[array].ref.at[at]

    cut(full, 0, 4, vectors, None, target, 1)


def rest_keep_kernel(ins, outs, full, turned):
    _, _, _, core = place()
    rest_product(ins[:6], core, full, turned)
    def came(role, second, z):
        array, at = unit(role, second, z)
        return ins[10 + array].ref[at]

    vectors = vector_lines(ins[6:10], core)
    cut(full, 0, 4, vectors, came, lambda role, second, z: (outs[2].ref.at[second] if role else outs[second].ref).at[z])


def plain(operands):
    return [(part, 0) for part in operands]


def unit(role, second, z):
    n = role * 8 + second * 4 + z
    return (0, n) if n < 6 else ((n - 1) // 5, (n - 1) % 5)


def cut_for_partner(body, name, ins, lines, scratch, cuts, after=()):
    dims = [(2, 4)] * 2 if cuts == 2 else [(6,), (5,), (5,)]
    return kernel(body, name, ins, [((*part, lines, WIDTH), BF, "", 0) for part in dims], scratch=scratch, after=after)


def cut_for_chips(body, name, ins, came, lines, scratch, cuts, after=()):
    outs = [((2, 4, lines, WIDTH), BF, "", 0)]
    outs = (outs if cuts == 1 else [((4, lines, WIDTH), BF, "", 0)] * 2) + outs
    return kernel(body, name, [*ins, *plain(came)], outs, scratch=scratch, after=after)


def halve_kernel(ins, outs):
    _, mine = spots()
    kept = ins[0].ref
    for n, second in enumerate((1 - mine, mine)):
        if len(ins) == 2:
            came = ins[1].ref[second]
        else:
            came = jnp.where(second == 0, ins[1].ref[...], ins[2].ref[...])
        value = (kept[second].astype(F32) + came.astype(F32)).astype(BF)
        if n:
            outs[-1].ref[...] = value
            continue
        size = value.shape[0] // (len(outs) - 1)
        for part, out in enumerate(outs[:-1]):
            out.ref[...] = value[part * size : (part + 1) * size]


def deal_kernel(ins, outs):
    _, _, z, core = place()
    kept, *came = [given.ref for given in ins]
    for n, far in enumerate((3, 1 + core, 2 - core, 0)):
        at = z ^ far
        if len(came) == 1:
            other = came[0][at]
        else:
            other = jnp.where(at < 2, came[0][at % 2], came[1][at % 2])
        outs[n // 2].ref[n % 2] = (kept[at].astype(F32) + other.astype(F32)).astype(BF)


def total_kernel(ins, outs):
    kept, came, last = [given.ref for given in ins]
    outs[0].ref[...] = (kept[1].astype(F32) + came[1].astype(F32) + last[...].astype(F32)).astype(BF)


def combine(body, name, operands, outs, after=(), scratch=()):
    return kernel(body, name, plain(operands), [(*out, "", 0) for out in outs], after=after, scratch=scratch)


def dp_sources(ins):
    first, second = spots()
    refs = [given.ref for given in ins]
    values = [ref[n] for ref in refs for n in range(2)] if len(refs) == 2 else [ref[...] for ref in refs]
    numbers = (2 * first + second, 2 * (1 - first) + second, 2 * first + 1 - second, 2 * (1 - first) + 1 - second)
    return [(value.astype(F32), number) for value, number in zip(values, numbers)]


def hid_final_kernel(ins, outs, full):
    size = full.shape[0] // 4
    for value, number in dp_sources(ins):
        full[pl.ds(pl.multiple_of(number * size, 16), size), :] = value
    outs[0].ref[...] = full[...].T


def in_final_kernel(ins, outs):
    for value, number in dp_sources(ins):
        outs[0].ref[:, pl.ds(pl.multiple_of(number * WIDTH, 128), WIDTH)] = value


def rest_final_kernel(questions, a, b, c, d, q, k, v, o, bq, bv, bo, bi, bh, g1, s1, g2, s2, loss, entropy):
    lines = jnp.zeros((MORE, LANES), F32)
    few = LINES // 4
    for value, number in dp_sources([Given(None, ref) for ref in (a, b, c, d)]):
        lines = lines + jnp.where(number == 0, value[LINES:, :LANES], 0.0)
        rows = pl.ds(pl.multiple_of(number * few, 8), few)
        for n, out in enumerate((q, k, v, o)):
            out[rows, :] = value[n * few : (n + 1) * few]
    for n, out in enumerate((bq, bv, bo, bh, g1, s1, g2, s2)):
        out[...] = lines[n, :LINES]
    bi[...] = jnp.concatenate([lines[8 + n : 9 + n, :LINES] for n in range(4)], axis=1).reshape(4 * LINES)
    nll, ent = jnp.sum(lines[12:13, :96]), jnp.sum(lines[12:13, 96:192])
    loss[0, 0] = (nll + ENTROPY_WEIGHT * ent) / questions
    entropy[0, 0] = ent / questions


def rest_final(pieces, questions, width):
    part, deep = width // 8, width // 2
    vectors = [shape((size,), F32) for size in (part, part, part, deep, part, part, part, part, part)]
    return pl.pallas_call(
        functools.partial(rest_final_kernel, questions),
        out_shape=[shape((part, width), F32)] * 4 + vectors + [shape((1, 1), F32)] * 2,
        in_specs=[whole()] * 4,
        out_specs=[whole()] * 13 + [whole(pltpu.SMEM)] * 2,
        compiler_params=params(12),
        cost_estimate=cost(0, MIB),
        name="rest_final",
    )(*pieces)


def halve(name, kept, *came, cuts=1, after=()):
    dims = kept.shape[1:]
    outs = [((dims[0] // cuts, *dims[1:]), BF)] * cuts + [(dims, BF)]
    return combine(halve_kernel, name, (kept, *came), outs, after=after)


def deal(name, halves, after=()):
    *send, kept = halves
    came = [exchange(part, over_plane(1)) for part in send]
    return combine(deal_kernel, name, (kept, *came), [((2, *kept.shape[1:]), BF)] * 2, after=after)


def on_this_slice(
    tokens, upstream, w_query, w_key, w_value, w_out, w_in, w_hid, b_query, b_value, b_out, b_in, b_hid,
    gain_one, shift_one, gain_two, shift_two, passages, slots, counts, gen_loglik,
):
    rows, width = tokens.shape
    deep = w_in.shape[1]
    questions = slots.shape[0] * lax.axis_size("dp")
    q_near, k_near, v_near, cls, q, k, v, vec = project(
        (
            tokens, w_key, w_value, w_query, b_value, b_query, w_out, b_out, gain_one, shift_one, w_in, b_in, w_hid, b_hid,
            gain_two, shift_two,
        )
    )
    own = [cls] + [exchange(cls, over_z(n)) for n in (1, 2, 3)]
    p, ctx, n1, i1, low, n1_near, low_near = attend(q_near, k_near, v_near, tokens, w_out, vec)
    near_passages, found = mark(passages, slots.T)
    mine = kernel(collect_kernel, "collect", plain(own), [((4 * cls.shape[0], width), BF, "", 0)], after=(i1,))[0]
    record = search(mine, exchange(mine, over_core), near_passages, found)
    cuts = meet(record, exchange(record, over_core))
    records = [cuts[0]] + [exchange(cuts[n], over_z(n)) for n in (1, 2, 3)]
    act, slope, encoded, sum_two, back, first, sums = forward(low_near, n1_near, vec, w_in, w_hid, upstream, after=(cuts[0],))
    back_near, fix, lead_vec, hid_cut, back = lead(records, cls, counts, gen_loglik.T, first, sums, vec, back, act)
    hid_came = exchange(hid_cut, over_core)
    pre_near, slope_vec, pre = slope_part(back_near, w_hid, slope)
    scratch = [pltpu.VMEM((4 * LINES, deep), F32), pltpu.VMEM((width, rows), BF)]
    in_cut = cut_for_partner(in_send_kernel, "in_send", plain((low, pre_near)), LINES, scratch, 2)
    in_came = [exchange(part, over_core) for part in in_cut]
    block = (width, deep // 8)
    hid_sent, hid_kept = kernel(
        hid_keep_kernel, "hid_keep", plain((back, act, hid_came)), [((2, *block), BF, "", 0)] * 2,
        scratch=[pltpu.VMEM((width, deep // 2), F32)], after=(in_cut[0],),
    )
    hid_came = exchange(hid_sent, over_z_by_core(0))
    attend_low, descend_vec, one, grad = descend(
        pre_near, w_in, fix, sum_two, n1, i1, vec, w_out, after=(hid_kept,)
    )
    into = cut_for_chips(
        in_keep_kernel, "in_keep", plain((low, pre)), in_came, LINES, scratch, 1, after=(attend_low,)
    )
    in_first = exchange(into[0], over_plane(0))
    dq, dk, dv, unattend_vec, input_grad = unattend(grad, p, q, k, v, one, w_query, w_key, w_value, after=(into[1],))
    operands = plain((tokens, ctx, dq, dk, dv, attend_low, lead_vec, slope_vec, descend_vec, unattend_vec))
    more = LINES + MORE
    rest_cut = cut_for_partner(rest_send_kernel, "rest_send", operands, more, scratch, 3)
    rest_came = [exchange(part, over_core) for part in rest_cut]
    hid_sum = combine(pair_kernel, "hid_pair", (hid_kept, hid_came), [(block, BF)], after=(rest_cut[0],))[0]
    hid_last = exchange(hid_sum, over_z_by_core(1))
    in_halves = halve("in_halve", into[1], in_first, after=(hid_sum,))
    rest = cut_for_chips(rest_keep_kernel, "rest_keep", operands, rest_came, more, scratch, 2, after=(in_halves[0],))
    rest_first = exchange(rest[0], over_plane(0)), exchange(rest[1], over_plane(0))
    in_parts = deal("in_deal", in_halves, after=(rest[2],))
    in_came = exchange(in_parts[0], over_z_by_core(0))
    rest_halves = halve("rest_halve", rest[2], *rest_first, cuts=2, after=(in_parts[0],))
    in_pair = combine(pair_kernel, "in_pair", (in_parts[1], in_came), [(in_came.shape[1:], BF)], after=(rest_halves[0],))[0]
    in_last = exchange(in_pair, over_z_by_core(1))
    size = ((width // 2, deep // 8), BF)
    hid_parts = combine(hid_deal_kernel, "hid_deal", (hid_kept, hid_came, hid_last), [size] * 2, after=(in_pair,))
    hid_first = exchange(hid_parts[0], over_plane(0))
    operands = (in_parts[1], in_came, in_last)
    in_sum = combine(total_kernel, "in_total", operands, [(in_pair.shape, BF)], after=(hid_parts[0],))[0]
    in_all = in_sum, exchange(in_sum, over_plane(0)), exchange(in_sum, over_plane(1)), exchange(in_sum, over_both)
    rest_parts = deal("rest_deal", rest_halves, after=(in_sum,))
    rest_came = exchange(rest_parts[0], over_z_by_core(0))
    size = ((width // 4, deep // 8), BF)
    hid_halves = combine(hid_halve_kernel, "hid_halve", (hid_parts[1], hid_first), [size] * 2, after=(rest_parts[0],))
    hid_second = exchange(hid_halves[0], over_plane(1))
    rest_pair = combine(pair_kernel, "rest_pair", (rest_parts[1], rest_came), [(rest_came.shape[1:], BF)], after=(hid_halves[0],))[0]
    grad_in = combine(in_final_kernel, "in_final", in_all, [((LINES, deep), F32)], after=(rest_pair,))[0]
    rest_last = exchange(rest_pair, over_z_by_core(1))
    mine = combine(sum_kernel, "hid_total", (hid_halves[1], hid_second), [size], after=(grad_in,))[0]
    hid_all = mine, exchange(mine, over_plane(0)), exchange(mine, over_plane(1)), exchange(mine, over_both)
    operands = (rest_parts[1], rest_came, rest_last)
    mine = combine(total_kernel, "rest_total", operands, [(rest_pair.shape, BF)], after=(mine,))[0]
    last = mine, exchange(mine, over_plane(0)), exchange(mine, over_plane(1)), exchange(mine, over_both)
    grad_hid = combine(
        hid_final_kernel, "hid_final", hid_all, [((deep // 8, width), F32)], scratch=[pltpu.VMEM((width, deep // 8), F32)],
        after=(mine,),
    )[0]
    *rest, loss, entropy = rest_final(last, questions, width)
    return (
        encoded, input_grad, loss.reshape(()), entropy.reshape(()), *rest[:4], grad_in, grad_hid, *rest[4:],
    )


PRECISE = lax.Precision.HIGHEST


def shortened(array):

    def short(part):
        return part.astype(jnp.bfloat16) if part.dtype == jnp.float32 else part

    return jax.tree.map(short, array)


def product(left_side, right_side):
    return jnp.dot(left_side, right_side, preferred_element_type=jnp.float32)


def times_transpose(left_side, right_side):
    return lax.dot_general(
        left_side, right_side, (((1,), (1,)), ((), ())), preferred_element_type=jnp.float32
    )


def transpose_times(left_side, right_side):
    return lax.dot_general(
        left_side, right_side, (((0,), (0,)), ((), ())), preferred_element_type=jnp.float32
    )


def plain_norm_forward(values, gain_vector, offset):
    center = values - jnp.mean(values, axis=-1, keepdims=True)
    inverse = lax.rsqrt(jnp.mean(center * center, axis=-1, keepdims=True) + NORM_EPSILON)
    normed = center * inverse
    return (normed * gain_vector + offset, normed, inverse)


def plain_norm_backward(incoming, normed, inverse, gain_vector):
    scaled = incoming * gain_vector
    inner = (
        scaled
        - jnp.mean(scaled, axis=-1, keepdims=True)
        - normed * jnp.mean(scaled * normed, axis=-1, keepdims=True)
    )
    return (inverse * inner, jnp.sum(incoming * normed, axis=0), jnp.sum(incoming, axis=0))


def gelu_slope(values):
    cumulative = 0.5 * (1.0 + jax.scipy.special.erf(values * 0.7071067811865476))
    return (
        values * cumulative,
        cumulative + values * jnp.exp(-0.5 * values * values) * 0.3989422804014327,
    )


def on_any_slice(
    tokens,
    upstream,
    w_query,
    w_key,
    w_value,
    w_out,
    w_in,
    w_hid,
    b_query,
    b_value,
    b_out,
    b_in,
    b_hid,
    gain_one,
    shift_one,
    gain_two,
    shift_two,
    passages,
    slots,
    counts,
    gen_loglik,
):
    tok_rows, model_width = tokens.shape
    seq_count = tok_rows // SEQ
    heads_shape = (seq_count, SEQ, HEADS, HDIM)
    inputs = tokens.astype(jnp.float32)
    queries = (product(tokens, w_query) + b_query).astype(jnp.bfloat16).reshape(heads_shape)
    keys_all = product(tokens, w_key).astype(jnp.bfloat16).reshape(heads_shape)
    values_all = (product(tokens, w_value) + b_value).astype(jnp.bfloat16).reshape(heads_shape)
    scores = (
        jnp.einsum("bqhd,bkhd->bhqk", queries, keys_all, preferred_element_type=jnp.float32) * 0.125
    )
    peak = jnp.max(scores, axis=-1, keepdims=True)
    log_total = peak + jnp.log(jnp.sum(jnp.exp(scores - peak), axis=-1, keepdims=True))
    weights_low = jnp.exp(scores - log_total).astype(jnp.bfloat16)
    context = jnp.einsum(
        "bhqk,bkhd->bqhd", weights_low, values_all, preferred_element_type=jnp.float32
    )
    context = context.reshape(tok_rows, model_width).astype(jnp.bfloat16)
    attended = product(context, w_out) + b_out
    hidden_one, normed_one, inverse_one = plain_norm_forward(inputs + attended, gain_one, shift_one)
    hidden_low = hidden_one.astype(jnp.bfloat16)
    pre_act = product(hidden_low, w_in) + b_in
    activated, slope = gelu_slope(pre_act)
    act_low = activated.astype(jnp.bfloat16)
    branch = product(act_low, w_hid) + b_hid
    outputs, normed_two, inverse_two = plain_norm_forward(hidden_one + branch, gain_two, shift_two)
    cls_low = outputs[::SEQ].astype(jnp.bfloat16)
    index_scores = times_transpose(lax.all_gather(cls_low, "index", axis=0, tiled=True), passages)
    group_rows, local_rows = index_scores.shape
    first_row = lax.axis_index("index") * local_rows
    local_slots = slots - first_row
    onehot = (
        lax.broadcasted_iota(jnp.int32, (1, 1, local_rows), 2) == local_slots[:, :, None]
    ).astype(jnp.float32)
    picked_part = jnp.einsum("qr,qsr->qs", index_scores, onehot, precision=PRECISE)
    row_peak = jnp.max(index_scores, axis=1)
    peak_all = lax.pmax(row_peak, "index")
    total_part = jnp.sum(jnp.exp(index_scores - peak_all[:, None]), axis=1)
    total_all, picked = lax.psum((total_part, picked_part), "index")
    index_lse = peak_all + jnp.log(total_all)
    valid = lax.broadcasted_iota(jnp.int32, picked.shape, 1) < counts[:, None]
    joint = picked - index_lse[:, None] + gen_loglik
    masked = jnp.where(valid, joint, -1e30)
    best = jnp.max(masked, axis=1, keepdims=True)
    marginal = best[:, 0] + jnp.log(jnp.sum(jnp.exp(masked - best), axis=1))
    centered = jnp.where(valid, joint - marginal[:, None], 0.0)
    posterior = jnp.where(valid, jnp.exp(masked - marginal[:, None]), 0.0)
    entropy_rows = -jnp.sum(posterior * centered, axis=1)
    nll_total, entropy_total = lax.psum((jnp.sum(-marginal), jnp.sum(entropy_rows)), "dp")
    questions = group_rows * lax.axis_size("dp")
    loss = (nll_total + ENTROPY_WEIGHT * entropy_total) / questions
    entropy = entropy_total / questions
    picked_grad = jnp.where(
        valid, -posterior * (1.0 + ENTROPY_WEIGHT * (centered + entropy_rows[:, None])), 0.0
    )
    score_grad = jnp.exp(index_scores - index_lse[:, None]) + jnp.einsum(
        "qs,qsr->qr", picked_grad, onehot, precision=PRECISE
    )
    score_low = score_grad.astype(jnp.bfloat16)
    cls_grad = lax.psum_scatter(
        product(score_low, passages), "index", scatter_dimension=0, tiled=True
    )
    out_grad = (
        upstream.astype(jnp.float32).reshape(seq_count, SEQ, model_width).at[:, 0].add(cls_grad)
    )
    out_grad = out_grad.reshape(tok_rows, model_width)
    sum_two, grad_gain_two, grad_shift_two = plain_norm_backward(
        out_grad, normed_two, inverse_two, gain_two
    )
    branch_low = sum_two.astype(jnp.bfloat16)
    grad_b_hid = jnp.sum(branch_low.astype(jnp.float32), axis=0)
    grad_w_hid = transpose_times(act_low, branch_low)
    pre_low = (times_transpose(branch_low, w_hid) * slope).astype(jnp.bfloat16)
    grad_b_in = jnp.sum(pre_low.astype(jnp.float32), axis=0)
    grad_w_in = transpose_times(hidden_low, pre_low)
    sum_one, grad_gain_one, grad_shift_one = plain_norm_backward(
        sum_two + times_transpose(pre_low, w_in), normed_one, inverse_one, gain_one
    )
    attend_low = sum_one.astype(jnp.bfloat16)
    grad_b_out = jnp.sum(attend_low.astype(jnp.float32), axis=0)
    grad_w_out = transpose_times(context, attend_low)
    context_grad = times_transpose(attend_low, w_out).astype(jnp.bfloat16).reshape(heads_shape)
    scores_again = (
        jnp.einsum("bqhd,bkhd->bhqk", queries, keys_all, preferred_element_type=jnp.float32) * 0.125
    )
    weights_again = jnp.exp(scores_again - log_total)
    again_low = weights_again.astype(jnp.bfloat16)
    weight_grad = jnp.einsum(
        "bqhd,bkhd->bhqk", context_grad, values_all, preferred_element_type=jnp.float32
    )
    value_grad = jnp.einsum(
        "bhqk,bqhd->bkhd", again_low, context_grad, preferred_element_type=jnp.float32
    )
    value_grad = value_grad.reshape(tok_rows, model_width).astype(jnp.bfloat16)
    logit_grad = weights_again * (
        weight_grad - jnp.sum(weight_grad * weights_again, axis=-1, keepdims=True)
    )
    logit_low = logit_grad.astype(jnp.bfloat16)
    query_grad = (
        jnp.einsum("bhqk,bkhd->bqhd", logit_low, keys_all, preferred_element_type=jnp.float32)
        * 0.125
    )
    query_grad = query_grad.reshape(tok_rows, model_width).astype(jnp.bfloat16)
    key_grad = (
        jnp.einsum("bhqk,bqhd->bkhd", logit_low, queries, preferred_element_type=jnp.float32)
        * 0.125
    )
    key_grad = key_grad.reshape(tok_rows, model_width).astype(jnp.bfloat16)
    input_grad = (
        sum_one
        + times_transpose(query_grad, w_query)
        + times_transpose(key_grad, w_key)
        + times_transpose(value_grad, w_value)
    ).astype(jnp.bfloat16)
    grad_w_query = transpose_times(tokens, query_grad)
    grad_w_key = transpose_times(tokens, key_grad)
    grad_w_value = transpose_times(tokens, value_grad)
    grad_b_query = jnp.sum(query_grad.astype(jnp.float32), axis=0)
    grad_b_value = jnp.sum(value_grad.astype(jnp.float32), axis=0)
    shares = (
        lax.psum_scatter(grad_w_query, "index", scatter_dimension=0, tiled=True),
        lax.psum_scatter(grad_w_key, "index", scatter_dimension=0, tiled=True),
        lax.psum_scatter(grad_w_value, "index", scatter_dimension=0, tiled=True),
        lax.psum_scatter(grad_w_out, "index", scatter_dimension=0, tiled=True),
        lax.psum_scatter(grad_w_in, "index", scatter_dimension=0, tiled=True),
        lax.psum_scatter(grad_w_hid, "index", scatter_dimension=0, tiled=True),
        lax.psum_scatter(grad_b_query, "index", scatter_dimension=0, tiled=True),
        lax.psum_scatter(grad_b_value, "index", scatter_dimension=0, tiled=True),
        lax.psum_scatter(grad_b_out, "index", scatter_dimension=0, tiled=True),
        lax.psum_scatter(grad_b_in, "index", scatter_dimension=0, tiled=True),
        lax.psum_scatter(grad_b_hid, "index", scatter_dimension=0, tiled=True),
        lax.psum_scatter(grad_gain_one, "index", scatter_dimension=0, tiled=True),
        lax.psum_scatter(grad_shift_one, "index", scatter_dimension=0, tiled=True),
        lax.psum_scatter(grad_gain_two, "index", scatter_dimension=0, tiled=True),
        lax.psum_scatter(grad_shift_two, "index", scatter_dimension=0, tiled=True),
    )
    summed = jax.tree.map(
        lambda part: part.astype(jnp.float32), lax.psum(shortened(tuple(shares)), "dp")
    )
    return (outputs.astype(jnp.bfloat16), input_grad, loss, entropy) + tuple(summed)


def solution(mesh):
    here = (mesh.shape["dp"], mesh.shape["index"]) == (4, 8)
    return jax.shard_map(
        on_this_slice if here else on_any_slice,
        mesh=mesh,
        in_specs=(
            P(("dp", "index"), None),
            P(("dp", "index"), None),
            P(),
            P(),
            P(),
            P(),
            P(),
            P(),
            P(),
            P(),
            P(),
            P(),
            P(),
            P(),
            P(),
            P(),
            P(),
            P("index", None),
            P("dp", None),
            P("dp"),
            P("dp", None),
        ),
        out_specs=(
            P(("dp", "index"), None),
            P(("dp", "index"), None),
            P(),
            P(),
            P("index", None),
            P("index", None),
            P("index", None),
            P("index", None),
            P("index", None),
            P("index", None),
            P("index"),
            P("index"),
            P("index"),
            P("index"),
            P("index"),
            P("index"),
            P("index"),
            P("index"),
            P("index"),
        ),
        check_vma=False,
    )
```

```python
import functools
import math

import jax
import jax.numpy as jnp
from jax import lax
from jax.experimental import pallas as pl
from jax.experimental.pallas import tpu as pltpu
from jax.sharding import PartitionSpec as P

HEADS = 12
FEED_PART = 256
SLOT_RECORDS = 13
RECORD_ROWS = 64
HDIM = 64
SEQ = 128
NORM_EPSILON = 1e-06
ENTROPY_WEIGHT = 0.5
BF = jnp.bfloat16
F32 = jnp.float32
MIB = 1 << 20
NEGATIVE = -1e30
WORK = {"in_deal": 5e9, "rest_deal": 1, "hid_deal": 1, "hid_pair": 1}


def dot(left, right):
    return jnp.dot(left, right, preferred_element_type=F32)


def dot_nt(left, right):
    return lax.dot_general(left, right, (((1,), (1,)), ((), ())), preferred_element_type=F32)


def dot_tn(left, right):
    return lax.dot_general(left, right, (((0,), (0,)), ((), ())), preferred_element_type=F32)


B_QUERY, B_VALUE, B_OUT, GAIN_ONE, SHIFT_ONE, B_HID, GAIN_TWO, SHIFT_TWO, B_IN = range(9)


def line(ref, n):
    return ref[n : n + 1, :]


def norm_forward(values):
    center = values - jnp.mean(values, axis=-1, keepdims=True)
    inverse = lax.rsqrt(jnp.mean(center * center, axis=-1, keepdims=True) + NORM_EPSILON)
    return center * inverse, inverse


def norm_backward(scaled, normed, inverse):
    return inverse * (
        scaled
        - jnp.mean(scaled, axis=-1, keepdims=True)
        - normed * jnp.mean(scaled * normed, axis=-1, keepdims=True)
    )


def gelu_and_slope(values):
    cumulative = 0.5 * (1.0 + lax.erf(values * 0.7071067811865476))
    bell = jnp.exp(-0.5 * values * values)
    return values * cumulative, cumulative + values * bell * 0.3989422804014327


def whole(memory=pltpu.VMEM):
    return pl.BlockSpec(memory_space=memory)


def params(limit):
    return pltpu.CompilerParams(vmem_limit_bytes=limit * MIB)


def cost(flops, moved):
    return pl.CostEstimate(flops=int(flops), bytes_accessed=int(moved), transcendentals=0)


def shape(dims, dtype):
    return jax.ShapeDtypeStruct(dims, dtype)


class Given:
    def __init__(self, held, ref, sems=None, parts=0, axis=0):
        self.ref, self.sems, self.parts = ref, sems, parts
        self.waiting = []
        if parts:
            size = ref.shape[axis] // parts
            for n in range(parts):
                cut = (slice(None),) * axis + (pl.ds(n * size, size),)
                source, target = (held, ref) if parts == 1 else (held.at[cut], ref.at[cut])
                self.waiting.append(pltpu.make_async_copy(source, target, sems.at[n]))

    def start(self):
        for copy in self.waiting:
            copy.start()

    def get(self, part=None):
        for n in range(self.parts) if part is None else (part,):
            if self.parts and self.waiting[n] is not None:
                self.waiting[n].wait()
                self.waiting[n] = None
        return self.ref


class Made:
    def __init__(self, ref, far=None, sems=None, parts=0):
        self.ref, self.far, self.sems, self.parts = ref, far, sems, parts
        self.running = []

    def put(self, part=None):
        if not self.parts:
            return
        for n in range(self.parts) if part is None else (part,):
            size = self.ref.shape[0] // self.parts
            cut = pl.ds(n * size, size)
            source, target = (self.ref, self.far) if self.parts == 1 else (self.ref.at[cut], self.far.at[cut])
            copy = pltpu.make_async_copy(source, target, self.sems.at[n])
            copy.start()
            self.running.append(copy)


def kernel(body, name, ins, outs, scratch=(), flops=0, moved=MIB, after=()):
    ins, axes = [part[:2] for part in ins], [(*part, 0)[2] for part in ins]
    operands = [pltpu.with_memory_space_constraint(a, pltpu.HBM) if parts else a for a, parts in ins]
    in_specs = [whole(pl.ANY if parts else pltpu.VMEM) for _, parts in ins]
    operands += after
    in_specs += [whole(pl.ANY)] * len(after)
    near = [(shape if not kind else pltpu.VMEM)(dims, dtype) for dims, dtype, kind, _ in outs if kind != "far"]
    far = [pltpu.HBM(dims, dtype) for dims, dtype, kind, _ in outs if kind in ("far", "both")]
    extra = [pltpu.VMEM(a.shape, a.dtype) for a, parts in ins if parts]
    extra += [pltpu.SemaphoreType.DMA((parts,)) for _, parts in ins if parts]
    extra += [pltpu.VMEM(dims, dtype) for dims, dtype, kind, _ in outs if kind == "far"]
    extra += [pltpu.SemaphoreType.DMA((parts,)) for _, _, _, parts in outs if parts]
    buffers = [part for part in extra + list(scratch) if hasattr(part, "shape") and part.memory_space == pltpu.VMEM]
    limit = sum(math.prod(part.shape) * jnp.dtype(part.dtype).itemsize for part in buffers) // MIB + 8

    def run(*refs):
        refs = list(refs)

        def take(count):
            taken, refs[:] = refs[:count], refs[count:]
            return taken

        given, _, near_refs, far_refs = take(len(ins)), take(len(after)), take(len(near)), take(len(far))
        copied = [n for n, (_, parts) in enumerate(ins) if parts]
        buffers, in_sems = take(len(copied)), take(len(copied))
        results, out_sems = take(sum(kind == "far" for _, _, kind, _ in outs)), take(len(far))
        arguments = []
        for n, (_, parts) in enumerate(ins):
            if parts:
                at = copied.index(n)
                arguments.append(Given(given[n], buffers[at], in_sems[at], parts, axes[n]))
            else:
                arguments.append(Given(None, given[n]))
        for argument in arguments:
            argument.start()
        made = []
        for _, _, kind, parts in outs:
            ref = results.pop(0) if kind == "far" else near_refs.pop(0)
            made.append(Made(ref, far_refs.pop(0), out_sems.pop(0), parts) if parts else Made(ref))
        body(arguments, made, *refs)
        for argument in arguments:
            argument.get()
        for result in made:
            for copy in result.running:
                copy.wait()

    return pl.pallas_call(
        run,
        out_shape=near + far,
        in_specs=in_specs,
        out_specs=[whole()] * len(near) + [whole(pl.ANY)] * len(far),
        scratch_shapes=extra + list(scratch),
        compiler_params=params(limit),
        cost_estimate=cost(WORK.get(name, 1), 1),
        name=name,
    )(*operands)


def place():
    dp, index = lax.axis_index("dp"), lax.axis_index("index")
    return dp % 2, dp // 2, index // 2, index % 2


def exchange(array, move):
    pairs = []
    for dp in range(4):
        for index in range(8):
            y, x, z, core = move(dp // 2, dp % 2, index // 2, index % 2)
            pairs.append((dp * 8 + index, (y * 2 + x) * 8 + z * 2 + core))
    return lax.ppermute(array, ("dp", "index"), pairs)


def over_core(y, x, z, core):
    return y, x, z, 1 - core


def over_plane(turn):
    return lambda y, x, z, core: (y ^ ((core + turn + 1) % 2 == 0), x ^ ((core + turn) % 2 == 0), z, core)


def over_both(y, x, z, core):
    return 1 - y, 1 - x, z, core


def over_z_by_core(turn):
    return lambda y, x, z, core: (y, x, z ^ (1 + (core + turn) % 2), core)


def over_z(step):
    return lambda y, x, z, core: (y, x, z ^ step, core)


def project_kernel(ins, outs):
    tok, wk, wv, wq, bv, bq, wo, bo, g1, s1, wi, bi, wh, bh, g2, s2 = ins
    q_out, k_out, v_out, cls_out, vec_out = outs
    row = lambda given: given.get()[...].reshape(1, -1)
    tokens = tok.get()
    k_out.ref[...] = dot(tokens[...], wk.get()[...]).astype(BF)
    k_out.put()
    v_out.ref[...] = (dot(tokens[...], wv.get()[...]) + row(bv)).astype(BF)
    v_out.put()
    q_out.ref[...] = (dot(tokens[...], wq.get()[...]) + row(bq)).astype(BF)
    q_out.put()
    rows, width = tokens.shape
    count = rows // SEQ
    head_rows = 16
    owned = lax.broadcasted_iota(jnp.int32, (head_rows, width), 1) // HDIM == lax.broadcasted_iota(
        jnp.int32, (head_rows, width), 0
    )
    contexts, firsts = [], []
    for b in range(count):
        query = q_out.ref[b * SEQ : b * SEQ + 16, :][:1].astype(F32)
        spread = jnp.where(owned, query, 0.0).astype(BF)
        scores = dot_nt(spread, k_out.ref[b * SEQ : (b + 1) * SEQ, :]) * 0.125
        raised = jnp.exp(scores - jnp.max(scores, axis=1, keepdims=True))
        weights = (raised / jnp.sum(raised, axis=1, keepdims=True)).astype(BF)
        mixed = dot(weights, v_out.ref[b * SEQ : (b + 1) * SEQ, :])
        contexts.append(jnp.sum(jnp.where(owned, mixed, 0.0), axis=0, keepdims=True))
        firsts.append(tokens[b * SEQ : b * SEQ + 16, :][:1].astype(F32))
    context = jnp.concatenate(contexts + contexts, axis=0).astype(BF)
    first = jnp.concatenate(firsts + firsts, axis=0)
    attended = dot(context, wo.get()[...]) + row(bo)
    normed, _ = norm_forward(first + attended)
    hidden = normed * row(g1) + row(s1)
    flat = row(bi)
    act, _ = gelu_and_slope(dot(hidden.astype(BF), wi.get()[...]) + flat)
    branch = dot(act.astype(BF), wh.get()[...]) + row(bh)
    normed, _ = norm_forward(hidden + branch)
    lines = lax.broadcasted_iota(jnp.int32, (2 * count, width), 0)
    mine = lines // count == lax.axis_index("index") % 2
    cls_out.ref[...] = jnp.where(mine, normed * row(g2) + row(s2), 0.0).astype(BF)
    cls_out.put()
    for n, vector in enumerate((bq, bv, bo, g1, s1, bh, g2, s2)):
        vec_out.ref[n : n + 1, :] = row(vector)
    for n in range(flat.shape[1] // width):
        vec_out.ref[B_IN + n : B_IN + n + 1, :] = flat[:, n * width : (n + 1) * width]
    vec_out.ref[B_IN + flat.shape[1] // width :, :] = jnp.zeros((16 - B_IN - flat.shape[1] // width, width), F32)
    vec_out.put()


def project(sources):
    rows, width = sources[0].shape
    outs = [((rows, width), BF, "both", 1)] * 3 + [((2 * (rows // SEQ), width), BF, "", 0), ((16, width), F32, "both", 1)]
    return kernel(
        project_kernel, "project", [(part, 1) for part in sources], outs, flops=8 * rows * width * width, moved=20 * MIB
    )


def stacked(pair):
    lane = lax.broadcasted_iota(jnp.int32, pair.shape, 1)
    zero = jnp.zeros_like(pair)
    return jnp.concatenate(
        [jnp.where(lane < HDIM, pair, zero), jnp.where(lane < HDIM, zero, pair)], axis=0
    )


def unstacked(tall):
    half = tall.shape[0] // 2
    lane = lax.broadcasted_iota(jnp.int32, (half, tall.shape[1]), 1)
    return jnp.where(lane < HDIM, tall[:half], tall[half:])


def attend_kernel(ins, outs):
    q, k, v, tok, wo, vec = ins
    p_out, ctx_out, n1_out, i1_out, low_out = outs
    rows, width = q.ref.shape
    pair = 2 * HDIM
    many = rows // SEQ
    for b in range(many):
        here = pl.ds(b * SEQ, SEQ)
        for given in (q, k, v):
            given.get(b)
        for h in range(width // pair):
            lanes = pl.ds(h * pair, pair)
            scores = dot_nt(q.ref[here, lanes], stacked(k.ref[here, lanes])) * 0.125
            parts = []
            for part in (scores[:, :SEQ], scores[:, SEQ:]):
                raised = jnp.exp(part - jnp.max(part, axis=1, keepdims=True))
                parts.append(raised * (1.0 / jnp.sum(raised, axis=1, keepdims=True)))
            weights = jnp.concatenate(parts, axis=1).astype(BF)
            p_out.ref[here, pl.ds(h * 2 * SEQ, 2 * SEQ)] = weights
            ctx_out.ref[here, lanes] = dot(weights, stacked(v.ref[here, lanes])).astype(BF)
        p_out.put(b)
    ctx_out.put()
    vectors, tokens, weights = vec.get(), tok.get(), wo.get()
    attended = dot(ctx_out.ref[...], weights[...]) + line(vectors, B_OUT)
    normed, inverse = norm_forward(tokens[...].astype(F32) + attended)
    n1_out.ref[...] = normed
    low_out.ref[...] = (normed * line(vectors, GAIN_ONE) + line(vectors, SHIFT_ONE)).astype(BF)
    i1_out.ref[...] = jnp.broadcast_to(inverse, i1_out.ref.shape)
    for out in (low_out, n1_out, i1_out):
        out.put()


def attend(q, k, v, tokens, wo, vec, after=()):
    rows, width = q.shape
    many = rows // SEQ
    outs = [
        ((rows, HEADS * SEQ), BF, "far", many),
        ((rows, width), BF, "far", 1),
        ((rows, width), F32, "both", 1),
        ((rows, 128), F32, "far", 1),
        ((rows, width), BF, "both", 1),
    ]
    ins = plain((q, k, v, tokens, wo, vec))
    n1_near, low_near, p, ctx, n1, i1, low = kernel(attend_kernel, "attend", ins, outs, after=after)
    return p, ctx, n1, i1, low, n1_near, low_near


def forward_kernel(ins, outs):
    low, n1, vec, wi, wh, up = ins
    act_out, slope_out, enc_out, back_out, sum_out, first_out, vec_out = outs
    rows, width = low.ref.shape
    vectors, weights = vec.get(), wi.get()
    for n in range(slope_out.ref.shape[0]):
        column = n * FEED_PART
        bias = vectors[B_IN + column // width : B_IN + column // width + 1, :][:, column % width : column % width + FEED_PART]
        value, steep = gelu_and_slope(dot(low.ref[...], weights[:, pl.ds(column, FEED_PART)]) + bias)
        act_out.ref[:, pl.ds(column, FEED_PART)] = value.astype(BF)
        slope_out.ref[n] = steep.astype(BF)
        slope_out.put(n)
    act_out.put()
    weights = wh.get()
    firsts, sums = [], []
    for n in range(enc_out.parts):
        size = rows // enc_out.parts
        here = pl.ds(n * size, size)
        branch = dot(act_out.ref[here, :], weights[...]) + line(vectors, B_HID)
        hidden = n1.ref[here, :] * line(vectors, GAIN_ONE) + line(vectors, SHIFT_ONE)
        normed, inverse = norm_forward(hidden + branch)
        enc_out.ref[here, :] = (normed * line(vectors, GAIN_TWO) + line(vectors, SHIFT_TWO)).astype(BF)
        enc_out.put(n)
        incoming = up.ref[here, :].astype(F32)
        back = norm_backward(incoming * line(vectors, GAIN_TWO), normed, inverse)
        sum_out.ref[here, :] = back
        sum_out.put(n)
        short = back.astype(BF)
        back_out.ref[here, :] = short
        wide = jnp.broadcast_to(inverse, normed.shape)
        firsts.append([[value[b : b + 1] for b in range(0, size, SEQ)] for value in (normed, incoming, wide)])
        sums.append(
            [
                jnp.sum(short.astype(F32), axis=0, keepdims=True),
                jnp.sum(incoming * normed, axis=0, keepdims=True),
                jnp.sum(incoming, axis=0, keepdims=True),
            ]
        )
    lines = [part for n in range(3) for block in firsts for part in block[n]]
    first_out.ref[...] = jnp.concatenate(lines + [jnp.zeros((16 - len(lines), width), F32)], axis=0)
    vec_out.ref[...] = jnp.concatenate(
        [functools.reduce(jnp.add, [block[n] for block in sums]) for n in range(3)] + [jnp.zeros((5, width), F32)], axis=0
    )


def forward(low, n1, vec, wi, wh, up, after=()):
    rows, width = low.shape
    deep = wi.shape[1]
    outs = [
        ((rows, deep), BF, "far", 1),
        ((deep // FEED_PART, rows, FEED_PART), BF, "far", deep // FEED_PART),
        ((rows, width), BF, "far", 2),
        ((rows, width), BF, "near", 0),
        ((rows, width), F32, "far", 2),
        ((16, width), F32, "", 0),
        ((8, width), F32, "", 0),
    ]
    ins = plain((low, n1, vec, wi, wh, up))
    back, first, sums, act, slope, encoded, sum_two = kernel(forward_kernel, "forward", ins, outs, after=after)
    return act, slope, encoded, sum_two, back, first, sums


def split(value, pieces):
    found = []
    for _ in range(pieces):
        piece = value.astype(BF).astype(F32)
        found.append(piece)
        value = value - piece
    return found


def packed_numbers(peak, total, width):
    lane = lax.broadcasted_iota(jnp.int32, (peak.shape[0], width), 1)
    packed = jnp.zeros((peak.shape[0], width), F32)
    for n, piece in enumerate(split(peak, 3) + split(total, 3)):
        packed = jnp.where(lane == n, piece, packed)
    return packed


def unpacked_numbers(packed):
    return (
        packed[:, 0:1] + packed[:, 1:2] + packed[:, 2:3],
        packed[:, 3:4] + packed[:, 4:5] + packed[:, 5:6],
    )


def mark_kernel(ins, outs):
    passages, slots = [given.ref for given in ins]
    _, _, z, core = place()
    many, count = slots.shape
    each = count // 4
    spot = lax.broadcasted_iota(jnp.int32, (count, count), 0)
    question = ((spot // each) ^ z) * each + spot % each
    chosen = lax.broadcasted_iota(jnp.int32, (count, count), 1) == question
    local = passages.shape[0]
    lane = lax.broadcasted_iota(jnp.int32, (count, local), 1)
    marks = []
    for j in range(many):
        ids = jnp.sum(jnp.where(chosen, slots[j : j + 1, :].astype(F32), 0.0), axis=1, keepdims=True)
        ids = ids.astype(jnp.int32) - (2 * z + core) * local
        marks.append(jnp.where(lane == ids, 1.0, 0.0).astype(BF))
    rows = dot(jnp.concatenate(marks, axis=0), passages[...]).astype(BF)
    for j in range(many):
        outs[0].ref[j] = rows[j * count : (j + 1) * count, :]


def mark(passages, slots):
    outs = [((*slots.shape, passages.shape[1]), BF, "near", 0)]
    return kernel(mark_kernel, "mark", plain((passages, slots)), outs)[0]


def collect_kernel(ins, outs):
    outs[0].ref[...] = jnp.concatenate([given.ref[...].astype(F32) for given in ins], axis=0).astype(BF)


def search_kernel(ins, outs):
    mine, theirs, passages, found = [given.ref for given in ins]
    (out,) = outs
    many = found.shape[0]
    cls = (mine[...].astype(F32) + theirs[...].astype(F32)).astype(BF)
    out.ref[:many] = found[...]
    scores = dot_nt(cls, passages[...])
    width = passages.shape[1]
    peak = jnp.max(scores, axis=1, keepdims=True)
    raised = jnp.exp(scores - peak)
    total = jnp.sum(raised, axis=1, keepdims=True)
    mixed = dot(raised.astype(BF), passages[...])
    for n, piece in enumerate(split(mixed, 2)):
        out.ref[many + n] = piece.astype(BF)
    out.ref[many + 2] = packed_numbers(peak, total, width).astype(BF)


def search(mine, theirs, passages, found):
    local, width = passages.shape
    many, count, _ = found.shape
    outs = [((many + 3, count, width), BF, "", 0)]
    ins = [(part, 0) for part in (mine, theirs, passages, found)]
    return kernel(search_kernel, "search", ins, outs, flops=4 * count * local * width)[0]


def joined(records):
    peak = functools.reduce(jnp.maximum, [r[2] for r in records])
    scales = [jnp.exp(r[2] - peak) for r in records]
    rows = functools.reduce(jnp.add, [r[0] for r in records])
    mixed = functools.reduce(jnp.add, [r[1] * s for r, s in zip(records, scales)])
    total = functools.reduce(jnp.add, [r[3] * s for r, s in zip(records, scales)])
    return rows, mixed, peak, total


def meet_kernel(ins, outs):
    records = []
    for given in ins:
        array = given.get()[...].astype(F32)
        many = array.shape[0] - 3
        records.append((array[:many], array[many] + array[many + 1], *unpacked_numbers(array[many + 2])))
    rows, mixed, peak, total = joined(records)
    width = mixed.shape[1]
    lines = [rows[j] for j in range(rows.shape[0])] + split(mixed, 2) + [packed_numbers(peak, total, width)]
    each = mixed.shape[0] // 4
    half = each // 2
    first = lax.axis_index("index") % 2 == 0
    fill = [jnp.zeros((outs[0].ref.shape[0] - len(lines) * half, width), F32)]
    for n, out in enumerate(outs):
        cut = [part[n * each : (n + 1) * each] for part in lines]
        cut = [jnp.where(first, part[:half], part[half:]) for part in cut]
        out.ref[...] = jnp.concatenate(cut + fill, axis=0).astype(BF)
        out.put()


def meet(mine, theirs):
    outs = [((RECORD_ROWS, mine.shape[2]), BF, "", 0)] * 4
    return kernel(meet_kernel, "meet", [(mine, 0), (theirs, 0)], outs)


def question_grad(records, cls, counts, loglik):
    many = loglik.shape[0]
    asked = cls.shape[0] // 2
    parted = []
    for record in records:
        array = record[...].astype(F32)
        lines = [array[n * asked : (n + 1) * asked] for n in range(many + 3)]
        parted.append((jnp.stack(lines[:many]), lines[many] + lines[many + 1], *unpacked_numbers(lines[many + 2])))
    found, mixed, peak, total = joined(parted)
    lse = peak + jnp.log(total)
    index = lax.axis_index("index")
    both = cls[...].astype(F32)
    question = both[:asked] + both[asked:]
    lane = lax.broadcasted_iota(jnp.int32, (asked, many), 1)
    picked = jnp.zeros((asked, many), F32)
    for j in range(many):
        picked = jnp.where(lane == j, jnp.sum(question * found[j], axis=1, keepdims=True), picked)
    questions = loglik.shape[1]
    spot = lax.broadcasted_iota(jnp.int32, (asked, questions), 0) + index * asked
    chosen = lax.broadcasted_iota(jnp.int32, (asked, questions), 1) == spot
    near = jnp.zeros((asked, many), F32)
    for j in range(many):
        value = jnp.sum(jnp.where(chosen, loglik[j : j + 1, :], 0.0), axis=1, keepdims=True)
        near = jnp.where(lane == j, value, near)
    limits = counts[...].reshape(1, questions).astype(F32)
    limits = jnp.sum(jnp.where(chosen, limits, 0.0), axis=1, keepdims=True).astype(jnp.int32)
    valid = lane < limits
    joint = picked - lse + near
    masked = jnp.where(valid, joint, NEGATIVE)
    best = jnp.max(masked, axis=1, keepdims=True)
    marginal = best + jnp.log(jnp.sum(jnp.exp(masked - best), axis=1, keepdims=True))
    centered = jnp.where(valid, joint - marginal, 0.0)
    posterior = jnp.where(valid, jnp.exp(masked - marginal), 0.0)
    entropy = -jnp.sum(posterior * centered, axis=1, keepdims=True)
    picked_grad = jnp.where(valid, -posterior * (1.0 + ENTROPY_WEIGHT * (centered + entropy)), 0.0)
    grad = mixed * (1.0 / total)
    for j in range(many):
        grad = grad + picked_grad[:, j : j + 1] * found[j]
    return grad, jnp.sum(-marginal), jnp.sum(entropy)


def lead_kernel(ins, outs, full):
    r0, r1, r2, r3, cls, counts, loglik, first, sums, vec, back, act = ins
    back_out, fix_out, vec_out, send_out = outs
    records = [given.get() for given in (r0, r1, r2, r3)]
    grad, nll, entropy = question_grad(records, cls.get(), counts.get(), loglik.get())
    many, width = grad.shape
    normed, incoming, inverse = [first.ref[...][n * many : (n + 1) * many] for n in range(3)]
    gain = line(vec.get(), GAIN_TWO)
    old = norm_backward(incoming * gain, normed, inverse[:, :1])
    new = norm_backward((incoming + grad) * gain, normed, inverse[:, :1])
    low = new.astype(BF).astype(F32)
    fix_out.ref[...] = jnp.concatenate([new, jnp.zeros((8 - many, width), F32)], axis=0)
    back_out.ref[...] = back.get()[...]
    top = lax.broadcasted_iota(jnp.int32, (16, width), 0) == 0
    for b in range(many):
        here = pl.ds(b * SEQ, 16)
        rows = back_out.ref[here, :].astype(F32)
        back_out.ref[here, :] = jnp.where(top, low[b : b + 1], rows).astype(BF)
    back_out.put()
    spread = lax.broadcasted_iota(jnp.int32, (1, width), 1)
    numbers = jnp.where(spread == 0, nll, jnp.where(spread == 1, entropy, 0.0))
    old_sums = sums.ref[...]
    change = low - old.astype(BF).astype(F32)
    vec_out.ref[...] = jnp.concatenate(
        [
            old_sums[0:1] + jnp.sum(change, axis=0, keepdims=True),
            old_sums[1:2] + jnp.sum(grad * normed, axis=0, keepdims=True),
            old_sums[2:3] + jnp.sum(grad, axis=0, keepdims=True),
            numbers,
            jnp.zeros((4, width), F32),
        ],
        axis=0,
    )
    _, _, _, core = place()
    hid_product(1 - core, back_out.ref, act.get(), full)
    hid_send(send_out, full)


def lead(records, cls, counts, loglik, first, sums, vec, back, act):
    rows, width = back.shape
    deep = act.shape[1]
    outs = [
        ((rows, width), BF, "both", 1),
        ((8, width), F32, "", 0),
        ((8, width), F32, "", 0),
        ((4, width, deep // 8), BF, "", 0),
    ]
    ins = [(part, 0) for part in (*records, cls)] + [(counts, 1), (loglik, 1), (first, 0), (sums, 0), (vec, 1), (back, 0), (act, 1)]
    return kernel(
        lead_kernel, "lead", ins, outs, scratch=[pltpu.VMEM((width, deep // 2), F32)], flops=rows * width * deep
    )


def slope_kernel(ins, outs):
    low, wh, slope = ins
    pre_out, vec_out = outs
    parts = slope.ref.shape[0]
    width = low.ref.shape[1]
    biases = []
    for n in range(parts):
        here = pl.ds(n * FEED_PART, FEED_PART)
        pre = (dot_nt(low.ref[...], wh.ref[here, :]) * slope.ref[n].astype(F32)).astype(BF)
        pre_out.ref[:, here] = pre
        biases.append(jnp.sum(pre.astype(F32), axis=0, keepdims=True))
    pre_out.put()
    flat = jnp.concatenate(biases, axis=1)
    vec_out.ref[...] = jnp.concatenate(
        [flat[:, n * width : (n + 1) * width] for n in range(flat.shape[1] // width)] + [jnp.zeros((4, width), F32)], axis=0
    )


def descend_kernel(ins, outs):
    pre, wi, fix, sum_two, n1, i1, vec, wo = ins
    attend_out, one_out, grad_out, vec_out = outs
    rows, width = n1.ref.shape
    size = rows // one_out.parts
    gain = None
    sums = []
    spot = lax.broadcasted_iota(jnp.int32, (size, 1), 0)
    for n in range(one_out.parts):
        here = pl.ds(n * size, size)
        back = dot_nt(pre.ref[here, :], wi.ref[...])
        before = sum_two.get(n)[here, :]
        for b in range(size // SEQ):
            question = n * size // SEQ + b
            before = jnp.where(spot == b * SEQ, fix.ref[question : question + 1, :], before)
        incoming = before + back
        normed = n1.get(n)[here, :]
        gain = line(vec.get(), GAIN_ONE) if gain is None else gain
        one = norm_backward(incoming * gain, normed, i1.get()[here, :1])
        one_out.ref[here, :] = one
        one_out.put(n)
        attend_low = one.astype(BF)
        attend_out.ref[here, :] = attend_low
        grad_out.ref[here, :] = dot_nt(attend_low, wo.ref[...]).astype(BF)
        grad_out.put(n)
        sums.append(
            [
                jnp.sum(attend_low.astype(F32), axis=0, keepdims=True),
                jnp.sum(incoming * normed, axis=0, keepdims=True),
                jnp.sum(incoming, axis=0, keepdims=True),
            ]
        )
    vec_out.ref[...] = jnp.concatenate(
        [functools.reduce(jnp.add, [block[n] for block in sums]) for n in range(3)] + [jnp.zeros((5, width), F32)], axis=0
    )


def slope_part(low, wh, slope):
    rows, width = low.shape
    outs = [((rows, wh.shape[0]), BF, "near", 0), ((8, width), F32, "", 0)]
    return kernel(slope_kernel, "slope", plain((low, wh, slope)), outs)


def descend(pre, wi, fix, sum_two, n1, i1, vec, wo, after=()):
    rows, width = n1.shape
    outs = [
        ((rows, width), BF, "near", 0),
        ((rows, width), F32, "far", 2),
        ((rows, width), BF, "near", 0),
        ((8, width), F32, "", 0),
    ]
    ins = [(pre, 0), (wi, 0), (fix, 0), (sum_two, 2), (n1, 2), (i1, 1), (vec, 1), (wo, 0)]
    return kernel(descend_kernel, "descend", ins, outs, after=after)


def unattend_kernel(ins, outs):
    grad, p, q, k, v, one, wq, wk, wv = ins
    dq_out, dk_out, dv_out, input_out, vec_out = outs
    rows, width = q.ref.shape
    pair = 2 * HDIM
    pairs = range(width // pair)
    for b in range(rows // SEQ):
        here = pl.ds(b * SEQ, SEQ)
        lanes = [pl.ds(h * pair, pair) for h in pairs]
        weights = [p.ref[here, pl.ds(h * 2 * SEQ, 2 * SEQ)] for h in pairs]
        incoming = [grad.ref[here, at] for at in lanes]
        sloped = [dot_nt(incoming[h], stacked(v.ref[here, lanes[h]])) for h in pairs]
        values = [unstacked(dot_tn(weights[h], incoming[h])).astype(BF) for h in pairs]
        lows = []
        for h in pairs:
            parts = []
            for n in range(2):
                exact = weights[h][:, n * SEQ : (n + 1) * SEQ].astype(F32)
                steep = sloped[h][:, n * SEQ : (n + 1) * SEQ]
                parts.append(exact * (steep - jnp.sum(steep * exact, axis=1, keepdims=True)))
            lows.append(jnp.concatenate(parts, axis=1).astype(BF))
        queries = [(dot(lows[h], stacked(k.ref[here, lanes[h]])) * 0.125).astype(BF) for h in pairs]
        keys = [(unstacked(dot_tn(lows[h], q.ref[here, lanes[h]])) * 0.125).astype(BF) for h in pairs]
        for h in pairs:
            dv_out.ref[here, lanes[h]] = values[h]
            dq_out.ref[here, lanes[h]] = queries[h]
            dk_out.ref[here, lanes[h]] = keys[h]
    for out in (dq_out, dk_out, dv_out):
        out.put()
    input_out.ref[...] = (
        one.get()[...]
        + dot_nt(dq_out.ref[...], wq.get()[...])
        + dot_nt(dk_out.ref[...], wk.get()[...])
        + dot_nt(dv_out.ref[...], wv.get()[...])
    ).astype(BF)
    input_out.put()
    vec_out.ref[...] = jnp.concatenate(
        [
            jnp.sum(dq_out.ref[...].astype(F32), axis=0, keepdims=True),
            jnp.sum(dv_out.ref[...].astype(F32), axis=0, keepdims=True),
            jnp.zeros((6, width), F32),
        ],
        axis=0,
    )
    vec_out.put()


def unattend(grad, p, q, k, v, one, wq, wk, wv, after=()):
    rows, width = q.shape
    many = rows // SEQ
    outs = [((rows, width), BF, "near", 0)] * 3 + [((rows, width), BF, "far", 1), ((8, width), F32, "", 0)]
    ins = [(part, 0) for part in (grad, p, q, k, v, one, wq, wk, wv)]
    return kernel(unattend_kernel, "unattend", ins, outs, flops=8 * rows * width * width, after=after)


LINES = 96
LANES = 384
WIDTH = 768
MORE = 16


def hid_product(core, low, act, full):
    each = act.shape[1] // 8
    parts = [act[:, pl.ds(pl.multiple_of((2 * z + core) * each, 128), each)] for z in range(4)]
    full[...] = dot_tn(low[...], jnp.concatenate(parts, axis=1))


def hid_send(out, full):
    each = full.shape[1] // 4
    for z in range(4):
        out.ref[z] = full[:, z * each : (z + 1) * each].astype(BF)


def hid_keep_kernel(ins, outs, full):
    low, act, came = [given.get() for given in ins]
    _, _, z, core = place()
    hid_product(core, low, act, full)
    each = full.shape[1] // 4
    for n, far in enumerate((3, 1 + core, 2 - core, 0)):
        lanes = pl.ds(pl.multiple_of((z ^ far) * each, 128), each)
        outs[n // 2].ref[n % 2] = (full[:, lanes] + came[z ^ far].astype(F32)).astype(BF)


def sum_kernel(ins, outs):
    outs[0].ref[...] = functools.reduce(jnp.add, [given.get()[...].astype(F32) for given in ins]).astype(BF)


def pair_kernel(ins, outs):
    kept, came = [given.ref for given in ins]
    outs[0].ref[...] = (kept[0].astype(F32) + came[0].astype(F32)).astype(BF)


def hid_deal_kernel(ins, outs):
    first, _ = spots()
    kept, came, last = [given.ref for given in ins]
    size = outs[0].ref.shape[0]
    for out, number in zip(outs, (1 - first, first)):
        cut = pl.ds(pl.multiple_of(number * size, 16), size)
        out.ref[...] = (kept[1, cut, :].astype(F32) + came[1, cut, :].astype(F32) + last[cut, :].astype(F32)).astype(BF)


def hid_halve_kernel(ins, outs):
    _, second = spots()
    kept, came = [given.ref for given in ins]
    size = outs[0].ref.shape[0]
    for out, number in zip(outs, (1 - second, second)):
        cut = pl.ds(pl.multiple_of(number * size, 16), size)
        out.ref[...] = (kept[cut, :].astype(F32) + came[cut, :].astype(F32)).astype(BF)


def spots(other=0):
    x, y, _, core = place()
    core = core ^ other
    return jnp.where(core == 0, x, y), jnp.where(core == 0, y, x)


def turned_rows(turned, core):
    size = turned.shape[0] // 8
    return jnp.concatenate(
        [turned[pl.ds(pl.multiple_of((2 * z + core) * size, 16), size), :] for z in range(4)], axis=0
    )


def vector_lines(vectors, core):
    lead_vec, slope_vec, descend_vec, unattend_vec = [given.get() for given in vectors]
    eight = jnp.concatenate(
        [unattend_vec[0:2, :], descend_vec[0:1, :], lead_vec[0:1, :], descend_vec[1:3, :], lead_vec[1:3, :]], axis=0
    )
    deep = slope_vec[0:4, :]
    device = lax.axis_index("dp") * 8 + lax.axis_index("index")
    lane = lax.broadcasted_iota(jnp.int32, (1, LANES), 1)
    terms = jnp.zeros((1, LANES), F32)
    for n, piece in enumerate(split(lead_vec[3:4, 0:1], 3) + split(lead_vec[3:4, 1:2], 3)):
        terms = jnp.where(lane == 32 * n + device, piece, terms)
    found = []
    for z in range(4):
        both = []
        for index in (2 * z, 2 * z + 1):
            at = (index % 2) * LANES
            cuts = [eight[:, index * LINES : (index + 1) * LINES]]
            cuts += [deep[index // 2 : index // 2 + 1, at + n * LINES : at + (n + 1) * LINES] for n in range(4)]
            both.append(jnp.concatenate(cuts, axis=0))
        part = jnp.where(core == 0, both[0], both[1])
        part = jnp.concatenate([part, jnp.zeros((part.shape[0], LANES - LINES), F32)], axis=1)
        part = jnp.concatenate([part, terms, jnp.zeros((MORE - part.shape[0] - 1, LANES), F32)], axis=0)
        found.append(jnp.concatenate([part, jnp.zeros((MORE, WIDTH - LANES), F32)], axis=1))
    return found


def cut(full, wide, narrow, vectors, came, target, other=0):
    few = LINES // 4
    mine, _ = spots(other)
    for role in range(2):
        first = mine if role else 1 - mine
        for second in range(2):
            for z in range(4):
                parts = []
                if wide:
                    lanes = pl.ds(pl.multiple_of((first * 2 + second) * WIDTH, 128), WIDTH)
                    parts.append(full[z * LINES : (z + 1) * LINES, lanes])
                rows = pl.ds(pl.multiple_of(first * 2 * few, 8) + z * LINES + second * few, few)
                for n in range(narrow):
                    parts.append(full[rows, n * WIDTH : (n + 1) * WIDTH])
                if vectors is not None:
                    parts.append(jnp.where(first == 0, vectors[z], 0.0) if second == 0 else jnp.zeros((MORE, WIDTH), F32))
                part = jnp.concatenate(parts, axis=0)
                if came is not None:
                    part = part + came(role, second, z).astype(F32)
                target(role, second, z)[...] = part.astype(BF)


def in_product(ins, core, full, turned):
    low, pre = ins
    turned[...] = low.ref[...].T
    full[...] = dot(turned_rows(turned, core), pre.ref[...])
    return full.shape[1]


def in_send_kernel(ins, outs, full, turned):
    _, _, _, core = place()
    wide = in_product(ins, 1 - core, full, turned)
    cut(full, wide, 0, None, None, lambda role, second, z: outs[role].ref.at[second, z], 1)


def in_keep_kernel(ins, outs, full, turned):
    _, _, _, core = place()
    wide = in_product(ins[:2], core, full, turned)
    came = lambda role, second, z: ins[2 + role].ref[second, z]
    cut(full, wide, 0, None, came, lambda role, second, z: outs[role].ref.at[second, z])


def rest_product(ins, core, full, turned):
    tok, ctx, *grads = ins
    turned[...] = tok.ref[...].T
    left = turned_rows(turned, core)
    for n, grad in enumerate(grads):
        width = grad.ref.shape[1]
        if n == len(grads) - 1:
            turned[...] = ctx.ref[...].T
            left = turned_rows(turned, core)
        full[:, n * width : (n + 1) * width] = dot(left, grad.ref[...])


def rest_send_kernel(ins, outs, full, turned):
    _, _, _, core = place()
    rest_product(ins[:6], 1 - core, full, turned)
    vectors = vector_lines(ins[6:10], 1 - core)
    def target(role, second, z):
        array, at = unit(role, second, z)
        return outs[array].ref.at[at]

    cut(full, 0, 4, vectors, None, target, 1)


def rest_keep_kernel(ins, outs, full, turned):
    _, _, _, core = place()
    rest_product(ins[:6], core, full, turned)
    def came(role, second, z):
        array, at = unit(role, second, z)
        return ins[10 + array].ref[at]

    vectors = vector_lines(ins[6:10], core)
    cut(full, 0, 4, vectors, came, lambda role, second, z: (outs[2].ref.at[second] if role else outs[second].ref).at[z])


def plain(operands):
    return [(part, 0) for part in operands]


def unit(role, second, z):
    n = role * 8 + second * 4 + z
    return (0, n) if n < 6 else ((n - 1) // 5, (n - 1) % 5)


def cut_for_partner(body, name, ins, lines, scratch, cuts, after=()):
    dims = [(2, 4)] * 2 if cuts == 2 else [(6,), (5,), (5,)]
    return kernel(body, name, ins, [((*part, lines, WIDTH), BF, "", 0) for part in dims], scratch=scratch, after=after)


def cut_for_chips(body, name, ins, came, lines, scratch, cuts, after=()):
    outs = [((2, 4, lines, WIDTH), BF, "", 0)]
    outs = (outs if cuts == 1 else [((4, lines, WIDTH), BF, "", 0)] * 2) + outs
    return kernel(body, name, [*ins, *plain(came)], outs, scratch=scratch, after=after)


def halve_kernel(ins, outs):
    _, mine = spots()
    kept = ins[0].ref
    for n, second in enumerate((1 - mine, mine)):
        if len(ins) == 2:
            came = ins[1].ref[second]
        else:
            came = jnp.where(second == 0, ins[1].ref[...], ins[2].ref[...])
        value = (kept[second].astype(F32) + came.astype(F32)).astype(BF)
        if n:
            outs[-1].ref[...] = value
            continue
        size = value.shape[0] // (len(outs) - 1)
        for part, out in enumerate(outs[:-1]):
            out.ref[...] = value[part * size : (part + 1) * size]


def deal_kernel(ins, outs):
    _, _, z, core = place()
    kept, *came = [given.ref for given in ins]
    for n, far in enumerate((3, 1 + core, 2 - core, 0)):
        at = z ^ far
        if len(came) == 1:
            other = came[0][at]
        else:
            other = jnp.where(at < 2, came[0][at % 2], came[1][at % 2])
        outs[n // 2].ref[n % 2] = (kept[at].astype(F32) + other.astype(F32)).astype(BF)


def total_kernel(ins, outs):
    kept, came, last = [given.ref for given in ins]
    outs[0].ref[...] = (kept[1].astype(F32) + came[1].astype(F32) + last[...].astype(F32)).astype(BF)


def combine(body, name, operands, outs, after=(), scratch=()):
    return kernel(body, name, plain(operands), [(*out, "", 0) for out in outs], after=after, scratch=scratch)


def dp_sources(ins):
    first, second = spots()
    refs = [given.ref for given in ins]
    values = [ref[n] for ref in refs for n in range(2)] if len(refs) == 2 else [ref[...] for ref in refs]
    numbers = (2 * first + second, 2 * (1 - first) + second, 2 * first + 1 - second, 2 * (1 - first) + 1 - second)
    return [(value.astype(F32), number) for value, number in zip(values, numbers)]


def hid_final_kernel(ins, outs, full):
    size = full.shape[0] // 4
    for value, number in dp_sources(ins):
        full[pl.ds(pl.multiple_of(number * size, 16), size), :] = value
    outs[0].ref[...] = full[...].T


def in_final_kernel(ins, outs):
    for value, number in dp_sources(ins):
        outs[0].ref[:, pl.ds(pl.multiple_of(number * WIDTH, 128), WIDTH)] = value


def rest_final_kernel(questions, a, b, c, d, q, k, v, o, bq, bv, bo, bi, bh, g1, s1, g2, s2, loss, entropy):
    lines = jnp.zeros((MORE, LANES), F32)
    few = LINES // 4
    for value, number in dp_sources([Given(None, ref) for ref in (a, b, c, d)]):
        lines = lines + jnp.where(number == 0, value[LINES:, :LANES], 0.0)
        rows = pl.ds(pl.multiple_of(number * few, 8), few)
        for n, out in enumerate((q, k, v, o)):
            out[rows, :] = value[n * few : (n + 1) * few]
    for n, out in enumerate((bq, bv, bo, bh, g1, s1, g2, s2)):
        out[...] = lines[n, :LINES]
    bi[...] = jnp.concatenate([lines[8 + n : 9 + n, :LINES] for n in range(4)], axis=1).reshape(4 * LINES)
    nll, ent = jnp.sum(lines[12:13, :96]), jnp.sum(lines[12:13, 96:192])
    loss[0, 0] = (nll + ENTROPY_WEIGHT * ent) / questions
    entropy[0, 0] = ent / questions


def rest_final(pieces, questions, width):
    part, deep = width // 8, width // 2
    vectors = [shape((size,), F32) for size in (part, part, part, deep, part, part, part, part, part)]
    return pl.pallas_call(
        functools.partial(rest_final_kernel, questions),
        out_shape=[shape((part, width), F32)] * 4 + vectors + [shape((1, 1), F32)] * 2,
        in_specs=[whole()] * 4,
        out_specs=[whole()] * 13 + [whole(pltpu.SMEM)] * 2,
        compiler_params=params(12),
        cost_estimate=cost(0, MIB),
        name="rest_final",
    )(*pieces)


def halve(name, kept, *came, cuts=1, after=()):
    dims = kept.shape[1:]
    outs = [((dims[0] // cuts, *dims[1:]), BF)] * cuts + [(dims, BF)]
    return combine(halve_kernel, name, (kept, *came), outs, after=after)


def deal(name, halves, after=()):
    *send, kept = halves
    came = [exchange(part, over_plane(1)) for part in send]
    return combine(deal_kernel, name, (kept, *came), [((2, *kept.shape[1:]), BF)] * 2, after=after)


def on_this_slice(
    tokens, upstream, w_query, w_key, w_value, w_out, w_in, w_hid, b_query, b_value, b_out, b_in, b_hid,
    gain_one, shift_one, gain_two, shift_two, passages, slots, counts, gen_loglik,
):
    rows, width = tokens.shape
    deep = w_in.shape[1]
    questions = slots.shape[0] * lax.axis_size("dp")
    q_near, k_near, v_near, cls, vec_near, q, k, v, vec = project(
        (
            tokens, w_key, w_value, w_query, b_value, b_query, w_out, b_out, gain_one, shift_one, w_in, b_in, w_hid, b_hid,
            gain_two, shift_two,
        )
    )
    own = [cls] + [exchange(cls, over_z(n)) for n in (1, 2, 3)]
    p, ctx, n1, i1, low, n1_near, low_near = attend(q_near, k_near, v_near, tokens, w_out, vec_near)
    found = mark(passages, slots.T)
    mine = kernel(collect_kernel, "collect", plain(own), [((4 * cls.shape[0], width), BF, "", 0)], after=(low_near,))[0]
    record = search(mine, exchange(mine, over_core), passages, found)
    cuts = meet(record, exchange(record, over_core))
    records = [cuts[0]] + [exchange(cuts[n], over_z(n)) for n in (1, 2, 3)]
    act, slope, encoded, sum_two, back, first, sums = forward(low_near, n1_near, vec, w_in, w_hid, upstream, after=(cuts[0],))
    back_near, fix, lead_vec, hid_cut, back = lead(records, cls, counts, gen_loglik.T, first, sums, vec, back, act)
    hid_came = exchange(hid_cut, over_core)
    pre, slope_vec = slope_part(back_near, w_hid, slope)
    scratch = [pltpu.VMEM((4 * LINES, deep), F32), pltpu.VMEM((width, rows), BF)]
    in_cut = cut_for_partner(in_send_kernel, "in_send", plain((low, pre)), LINES, scratch, 2)
    in_came = [exchange(part, over_core) for part in in_cut]
    block = (width, deep // 8)
    hid_sent, hid_kept = kernel(
        hid_keep_kernel, "hid_keep", plain((back, act, hid_came)), [((2, *block), BF, "", 0)] * 2,
        scratch=[pltpu.VMEM((width, deep // 2), F32)], after=(in_cut[0],),
    )
    hid_came = exchange(hid_sent, over_z_by_core(0))
    attend_low, grad, descend_vec, one = descend(
        pre, w_in, fix, sum_two, n1, i1, vec, w_out, after=(hid_kept,)
    )
    into = cut_for_chips(
        in_keep_kernel, "in_keep", plain((low, pre)), in_came, LINES, scratch, 1, after=(attend_low,)
    )
    in_first = exchange(into[0], over_plane(0))
    dq, dk, dv, unattend_vec, input_grad = unattend(grad, p, q, k, v, one, w_query, w_key, w_value, after=(into[1],))
    operands = plain((tokens, ctx, dq, dk, dv, attend_low, lead_vec, slope_vec, descend_vec, unattend_vec))
    more = LINES + MORE
    rest_cut = cut_for_partner(rest_send_kernel, "rest_send", operands, more, scratch, 3)
    rest_came = [exchange(part, over_core) for part in rest_cut]
    hid_sum = combine(pair_kernel, "hid_pair", (hid_kept, hid_came), [(block, BF)], after=(rest_cut[0],))[0]
    hid_last = exchange(hid_sum, over_z_by_core(1))
    in_halves = halve("in_halve", into[1], in_first, after=(hid_sum,))
    rest = cut_for_chips(rest_keep_kernel, "rest_keep", operands, rest_came, more, scratch, 2, after=(in_halves[0],))
    rest_first = exchange(rest[0], over_plane(0)), exchange(rest[1], over_plane(0))
    in_parts = deal("in_deal", in_halves, after=(rest[2],))
    in_came = exchange(in_parts[0], over_z_by_core(0))
    rest_halves = halve("rest_halve", rest[2], *rest_first, cuts=2, after=(in_parts[0],))
    in_pair = combine(pair_kernel, "in_pair", (in_parts[1], in_came), [(in_came.shape[1:], BF)], after=(rest_halves[0],))[0]
    in_last = exchange(in_pair, over_z_by_core(1))
    size = ((width // 2, deep // 8), BF)
    hid_parts = combine(hid_deal_kernel, "hid_deal", (hid_kept, hid_came, hid_last), [size] * 2, after=(in_pair,))
    hid_first = exchange(hid_parts[0], over_plane(0))
    operands = (in_parts[1], in_came, in_last)
    in_sum = combine(total_kernel, "in_total", operands, [(in_pair.shape, BF)], after=(hid_parts[0],))[0]
    in_all = in_sum, exchange(in_sum, over_plane(0)), exchange(in_sum, over_plane(1)), exchange(in_sum, over_both)
    rest_parts = deal("rest_deal", rest_halves, after=(in_sum,))
    rest_came = exchange(rest_parts[0], over_z_by_core(0))
    size = ((width // 4, deep // 8), BF)
    hid_halves = combine(hid_halve_kernel, "hid_halve", (hid_parts[1], hid_first), [size] * 2, after=(rest_parts[0],))
    hid_second = exchange(hid_halves[0], over_plane(1))
    rest_pair = combine(pair_kernel, "rest_pair", (rest_parts[1], rest_came), [(rest_came.shape[1:], BF)], after=(hid_halves[0],))[0]
    grad_in = combine(in_final_kernel, "in_final", in_all, [((LINES, deep), F32)], after=(rest_pair,))[0]
    rest_last = exchange(rest_pair, over_z_by_core(1))
    mine = combine(sum_kernel, "hid_total", (hid_halves[1], hid_second), [size], after=(grad_in,))[0]
    hid_all = mine, exchange(mine, over_plane(0)), exchange(mine, over_plane(1)), exchange(mine, over_both)
    operands = (rest_parts[1], rest_came, rest_last)
    mine = combine(total_kernel, "rest_total", operands, [(rest_pair.shape, BF)], after=(mine,))[0]
    last = mine, exchange(mine, over_plane(0)), exchange(mine, over_plane(1)), exchange(mine, over_both)
    grad_hid = combine(
        hid_final_kernel, "hid_final", hid_all, [((deep // 8, width), F32)], scratch=[pltpu.VMEM((width, deep // 8), F32)],
        after=(mine,),
    )[0]
    *rest, loss, entropy = rest_final(last, questions, width)
    return (
        encoded, input_grad, loss.reshape(()), entropy.reshape(()), *rest[:4], grad_in, grad_hid, *rest[4:],
    )


PRECISE = lax.Precision.HIGHEST


def shortened(array):

    def short(part):
        return part.astype(jnp.bfloat16) if part.dtype == jnp.float32 else part

    return jax.tree.map(short, array)


def product(left_side, right_side):
    return jnp.dot(left_side, right_side, preferred_element_type=jnp.float32)


def times_transpose(left_side, right_side):
    return lax.dot_general(
        left_side, right_side, (((1,), (1,)), ((), ())), preferred_element_type=jnp.float32
    )


def transpose_times(left_side, right_side):
    return lax.dot_general(
        left_side, right_side, (((0,), (0,)), ((), ())), preferred_element_type=jnp.float32
    )


def plain_norm_forward(values, gain_vector, offset):
    center = values - jnp.mean(values, axis=-1, keepdims=True)
    inverse = lax.rsqrt(jnp.mean(center * center, axis=-1, keepdims=True) + NORM_EPSILON)
    normed = center * inverse
    return (normed * gain_vector + offset, normed, inverse)


def plain_norm_backward(incoming, normed, inverse, gain_vector):
    scaled = incoming * gain_vector
    inner = (
        scaled
        - jnp.mean(scaled, axis=-1, keepdims=True)
        - normed * jnp.mean(scaled * normed, axis=-1, keepdims=True)
    )
    return (inverse * inner, jnp.sum(incoming * normed, axis=0), jnp.sum(incoming, axis=0))


def gelu_slope(values):
    cumulative = 0.5 * (1.0 + jax.scipy.special.erf(values * 0.7071067811865476))
    return (
        values * cumulative,
        cumulative + values * jnp.exp(-0.5 * values * values) * 0.3989422804014327,
    )


def on_any_slice(
    tokens,
    upstream,
    w_query,
    w_key,
    w_value,
    w_out,
    w_in,
    w_hid,
    b_query,
    b_value,
    b_out,
    b_in,
    b_hid,
    gain_one,
    shift_one,
    gain_two,
    shift_two,
    passages,
    slots,
    counts,
    gen_loglik,
):
    tok_rows, model_width = tokens.shape
    seq_count = tok_rows // SEQ
    heads_shape = (seq_count, SEQ, HEADS, HDIM)
    inputs = tokens.astype(jnp.float32)
    queries = (product(tokens, w_query) + b_query).astype(jnp.bfloat16).reshape(heads_shape)
    keys_all = product(tokens, w_key).astype(jnp.bfloat16).reshape(heads_shape)
    values_all = (product(tokens, w_value) + b_value).astype(jnp.bfloat16).reshape(heads_shape)
    scores = (
        jnp.einsum("bqhd,bkhd->bhqk", queries, keys_all, preferred_element_type=jnp.float32) * 0.125
    )
    peak = jnp.max(scores, axis=-1, keepdims=True)
    log_total = peak + jnp.log(jnp.sum(jnp.exp(scores - peak), axis=-1, keepdims=True))
    weights_low = jnp.exp(scores - log_total).astype(jnp.bfloat16)
    context = jnp.einsum(
        "bhqk,bkhd->bqhd", weights_low, values_all, preferred_element_type=jnp.float32
    )
    context = context.reshape(tok_rows, model_width).astype(jnp.bfloat16)
    attended = product(context, w_out) + b_out
    hidden_one, normed_one, inverse_one = plain_norm_forward(inputs + attended, gain_one, shift_one)
    hidden_low = hidden_one.astype(jnp.bfloat16)
    pre_act = product(hidden_low, w_in) + b_in
    activated, slope = gelu_slope(pre_act)
    act_low = activated.astype(jnp.bfloat16)
    branch = product(act_low, w_hid) + b_hid
    outputs, normed_two, inverse_two = plain_norm_forward(hidden_one + branch, gain_two, shift_two)
    cls_low = outputs[::SEQ].astype(jnp.bfloat16)
    index_scores = times_transpose(lax.all_gather(cls_low, "index", axis=0, tiled=True), passages)
    group_rows, local_rows = index_scores.shape
    first_row = lax.axis_index("index") * local_rows
    local_slots = slots - first_row
    onehot = (
        lax.broadcasted_iota(jnp.int32, (1, 1, local_rows), 2) == local_slots[:, :, None]
    ).astype(jnp.float32)
    picked_part = jnp.einsum("qr,qsr->qs", index_scores, onehot, precision=PRECISE)
    row_peak = jnp.max(index_scores, axis=1)
    peak_all = lax.pmax(row_peak, "index")
    total_part = jnp.sum(jnp.exp(index_scores - peak_all[:, None]), axis=1)
    total_all, picked = lax.psum((total_part, picked_part), "index")
    index_lse = peak_all + jnp.log(total_all)
    valid = lax.broadcasted_iota(jnp.int32, picked.shape, 1) < counts[:, None]
    joint = picked - index_lse[:, None] + gen_loglik
    masked = jnp.where(valid, joint, -1e30)
    best = jnp.max(masked, axis=1, keepdims=True)
    marginal = best[:, 0] + jnp.log(jnp.sum(jnp.exp(masked - best), axis=1))
    centered = jnp.where(valid, joint - marginal[:, None], 0.0)
    posterior = jnp.where(valid, jnp.exp(masked - marginal[:, None]), 0.0)
    entropy_rows = -jnp.sum(posterior * centered, axis=1)
    nll_total, entropy_total = lax.psum((jnp.sum(-marginal), jnp.sum(entropy_rows)), "dp")
    questions = group_rows * lax.axis_size("dp")
    loss = (nll_total + ENTROPY_WEIGHT * entropy_total) / questions
    entropy = entropy_total / questions
    picked_grad = jnp.where(
        valid, -posterior * (1.0 + ENTROPY_WEIGHT * (centered + entropy_rows[:, None])), 0.0
    )
    score_grad = jnp.exp(index_scores - index_lse[:, None]) + jnp.einsum(
        "qs,qsr->qr", picked_grad, onehot, precision=PRECISE
    )
    score_low = score_grad.astype(jnp.bfloat16)
    cls_grad = lax.psum_scatter(
        product(score_low, passages), "index", scatter_dimension=0, tiled=True
    )
    out_grad = (
        upstream.astype(jnp.float32).reshape(seq_count, SEQ, model_width).at[:, 0].add(cls_grad)
    )
    out_grad = out_grad.reshape(tok_rows, model_width)
    sum_two, grad_gain_two, grad_shift_two = plain_norm_backward(
        out_grad, normed_two, inverse_two, gain_two
    )
    branch_low = sum_two.astype(jnp.bfloat16)
    grad_b_hid = jnp.sum(branch_low.astype(jnp.float32), axis=0)
    grad_w_hid = transpose_times(act_low, branch_low)
    pre_low = (times_transpose(branch_low, w_hid) * slope).astype(jnp.bfloat16)
    grad_b_in = jnp.sum(pre_low.astype(jnp.float32), axis=0)
    grad_w_in = transpose_times(hidden_low, pre_low)
    sum_one, grad_gain_one, grad_shift_one = plain_norm_backward(
        sum_two + times_transpose(pre_low, w_in), normed_one, inverse_one, gain_one
    )
    attend_low = sum_one.astype(jnp.bfloat16)
    grad_b_out = jnp.sum(attend_low.astype(jnp.float32), axis=0)
    grad_w_out = transpose_times(context, attend_low)
    context_grad = times_transpose(attend_low, w_out).astype(jnp.bfloat16).reshape(heads_shape)
    scores_again = (
        jnp.einsum("bqhd,bkhd->bhqk", queries, keys_all, preferred_element_type=jnp.float32) * 0.125
    )
    weights_again = jnp.exp(scores_again - log_total)
    again_low = weights_again.astype(jnp.bfloat16)
    weight_grad = jnp.einsum(
        "bqhd,bkhd->bhqk", context_grad, values_all, preferred_element_type=jnp.float32
    )
    value_grad = jnp.einsum(
        "bhqk,bqhd->bkhd", again_low, context_grad, preferred_element_type=jnp.float32
    )
    value_grad = value_grad.reshape(tok_rows, model_width).astype(jnp.bfloat16)
    logit_grad = weights_again * (
        weight_grad - jnp.sum(weight_grad * weights_again, axis=-1, keepdims=True)
    )
    logit_low = logit_grad.astype(jnp.bfloat16)
    query_grad = (
        jnp.einsum("bhqk,bkhd->bqhd", logit_low, keys_all, preferred_element_type=jnp.float32)
        * 0.125
    )
    query_grad = query_grad.reshape(tok_rows, model_width).astype(jnp.bfloat16)
    key_grad = (
        jnp.einsum("bhqk,bqhd->bkhd", logit_low, queries, preferred_element_type=jnp.float32)
        * 0.125
    )
    key_grad = key_grad.reshape(tok_rows, model_width).astype(jnp.bfloat16)
    input_grad = (
        sum_one
        + times_transpose(query_grad, w_query)
        + times_transpose(key_grad, w_key)
        + times_transpose(value_grad, w_value)
    ).astype(jnp.bfloat16)
    grad_w_query = transpose_times(tokens, query_grad)
    grad_w_key = transpose_times(tokens, key_grad)
    grad_w_value = transpose_times(tokens, value_grad)
    grad_b_query = jnp.sum(query_grad.astype(jnp.float32), axis=0)
    grad_b_value = jnp.sum(value_grad.astype(jnp.float32), axis=0)
    shares = (
        lax.psum_scatter(grad_w_query, "index", scatter_dimension=0, tiled=True),
        lax.psum_scatter(grad_w_key, "index", scatter_dimension=0, tiled=True),
        lax.psum_scatter(grad_w_value, "index", scatter_dimension=0, tiled=True),
        lax.psum_scatter(grad_w_out, "index", scatter_dimension=0, tiled=True),
        lax.psum_scatter(grad_w_in, "index", scatter_dimension=0, tiled=True),
        lax.psum_scatter(grad_w_hid, "index", scatter_dimension=0, tiled=True),
        lax.psum_scatter(grad_b_query, "index", scatter_dimension=0, tiled=True),
        lax.psum_scatter(grad_b_value, "index", scatter_dimension=0, tiled=True),
        lax.psum_scatter(grad_b_out, "index", scatter_dimension=0, tiled=True),
        lax.psum_scatter(grad_b_in, "index", scatter_dimension=0, tiled=True),
        lax.psum_scatter(grad_b_hid, "index", scatter_dimension=0, tiled=True),
        lax.psum_scatter(grad_gain_one, "index", scatter_dimension=0, tiled=True),
        lax.psum_scatter(grad_shift_one, "index", scatter_dimension=0, tiled=True),
        lax.psum_scatter(grad_gain_two, "index", scatter_dimension=0, tiled=True),
        lax.psum_scatter(grad_shift_two, "index", scatter_dimension=0, tiled=True),
    )
    summed = jax.tree.map(
        lambda part: part.astype(jnp.float32), lax.psum(shortened(tuple(shares)), "dp")
    )
    return (outputs.astype(jnp.bfloat16), input_grad, loss, entropy) + tuple(summed)


def solution(mesh):
    here = (mesh.shape["dp"], mesh.shape["index"]) == (4, 8)
    return jax.shard_map(
        on_this_slice if here else on_any_slice,
        mesh=mesh,
        in_specs=(
            P(("dp", "index"), None),
            P(("dp", "index"), None),
            P(),
            P(),
            P(),
            P(),
            P(),
            P(),
            P(),
            P(),
            P(),
            P(),
            P(),
            P(),
            P(),
            P(),
            P(),
            P("index", None),
            P("dp", None),
            P("dp"),
            P("dp", None),
        ),
        out_specs=(
            P(("dp", "index"), None),
            P(("dp", "index"), None),
            P(),
            P(),
            P("index", None),
            P("index", None),
            P("index", None),
            P("index", None),
            P("index", None),
            P("index", None),
            P("index"),
            P("index"),
            P("index"),
            P("index"),
            P("index"),
            P("index"),
            P("index"),
            P("index"),
            P("index"),
        ),
        check_vma=False,
    )
```

```python
import functools
import math

import jax
import jax.numpy as jnp
from jax import lax
from jax.experimental import pallas as pl
from jax.experimental.pallas import tpu as pltpu
from jax.sharding import PartitionSpec as P

HEADS = 12
FEED_PART = 256
SLOT_RECORDS = 13
RECORD_ROWS = 64
HDIM = 64
SEQ = 128
NORM_EPSILON = 1e-06
ENTROPY_WEIGHT = 0.5
BF = jnp.bfloat16
F32 = jnp.float32
MIB = 1 << 20
NEGATIVE = -1e30
WORK = {"in_deal": 5e9, "rest_deal": 1, "hid_deal": 1, "hid_pair": 1}


def dot(left, right):
    return jnp.dot(left, right, preferred_element_type=F32)


def dot_nt(left, right):
    return lax.dot_general(left, right, (((1,), (1,)), ((), ())), preferred_element_type=F32)


def dot_tn(left, right):
    return lax.dot_general(left, right, (((0,), (0,)), ((), ())), preferred_element_type=F32)


B_QUERY, B_VALUE, B_OUT, GAIN_ONE, SHIFT_ONE, B_HID, GAIN_TWO, SHIFT_TWO, B_IN = range(9)


def line(ref, n):
    return ref[n : n + 1, :]


def norm_forward(values):
    center = values - jnp.mean(values, axis=-1, keepdims=True)
    inverse = lax.rsqrt(jnp.mean(center * center, axis=-1, keepdims=True) + NORM_EPSILON)
    return center * inverse, inverse


def norm_backward(scaled, normed, inverse):
    return inverse * (
        scaled
        - jnp.mean(scaled, axis=-1, keepdims=True)
        - normed * jnp.mean(scaled * normed, axis=-1, keepdims=True)
    )


def gelu_and_slope(values):
    cumulative = 0.5 * (1.0 + lax.erf(values * 0.7071067811865476))
    bell = jnp.exp(-0.5 * values * values)
    return values * cumulative, cumulative + values * bell * 0.3989422804014327


def whole(memory=pltpu.VMEM):
    return pl.BlockSpec(memory_space=memory)


def params(limit):
    return pltpu.CompilerParams(vmem_limit_bytes=limit * MIB)


def cost(flops, moved):
    return pl.CostEstimate(flops=int(flops), bytes_accessed=int(moved), transcendentals=0)


def shape(dims, dtype):
    return jax.ShapeDtypeStruct(dims, dtype)


class Given:
    def __init__(self, held, ref, sems=None, parts=0, axis=0):
        self.ref, self.sems, self.parts = ref, sems, parts
        self.waiting = []
        if parts:
            size = ref.shape[axis] // parts
            for n in range(parts):
                cut = (slice(None),) * axis + (pl.ds(n * size, size),)
                source, target = (held, ref) if parts == 1 else (held.at[cut], ref.at[cut])
                self.waiting.append(pltpu.make_async_copy(source, target, sems.at[n]))

    def start(self):
        for copy in self.waiting:
            copy.start()

    def get(self, part=None):
        for n in range(self.parts) if part is None else (part,):
            if self.parts and self.waiting[n] is not None:
                self.waiting[n].wait()
                self.waiting[n] = None
        return self.ref


class Made:
    def __init__(self, ref, far=None, sems=None, parts=0):
        self.ref, self.far, self.sems, self.parts = ref, far, sems, parts
        self.running = []

    def put(self, part=None):
        if not self.parts:
            return
        for n in range(self.parts) if part is None else (part,):
            size = self.ref.shape[0] // self.parts
            cut = pl.ds(n * size, size)
            source, target = (self.ref, self.far) if self.parts == 1 else (self.ref.at[cut], self.far.at[cut])
            copy = pltpu.make_async_copy(source, target, self.sems.at[n])
            copy.start()
            self.running.append(copy)


def kernel(body, name, ins, outs, scratch=(), flops=0, moved=MIB, after=()):
    ins, axes = [part[:2] for part in ins], [(*part, 0)[2] for part in ins]
    operands = [pltpu.with_memory_space_constraint(a, pltpu.HBM) if parts else a for a, parts in ins]
    in_specs = [whole(pl.ANY if parts else pltpu.VMEM) for _, parts in ins]
    operands += after
    in_specs += [whole(pl.ANY)] * len(after)
    near = [(shape if not kind else pltpu.VMEM)(dims, dtype) for dims, dtype, kind, _ in outs if kind != "far"]
    far = [pltpu.HBM(dims, dtype) for dims, dtype, kind, _ in outs if kind in ("far", "both")]
    extra = [pltpu.VMEM(a.shape, a.dtype) for a, parts in ins if parts]
    extra += [pltpu.SemaphoreType.DMA((parts,)) for _, parts in ins if parts]
    extra += [pltpu.VMEM(dims, dtype) for dims, dtype, kind, _ in outs if kind == "far"]
    extra += [pltpu.SemaphoreType.DMA((parts,)) for _, _, _, parts in outs if parts]
    buffers = [part for part in extra + list(scratch) if hasattr(part, "shape") and part.memory_space == pltpu.VMEM]
    limit = sum(math.prod(part.shape) * jnp.dtype(part.dtype).itemsize for part in buffers) // MIB + 8

    def run(*refs):
        refs = list(refs)

        def take(count):
            taken, refs[:] = refs[:count], refs[count:]
            return taken

        given, _, near_refs, far_refs = take(len(ins)), take(len(after)), take(len(near)), take(len(far))
        copied = [n for n, (_, parts) in enumerate(ins) if parts]
        buffers, in_sems = take(len(copied)), take(len(copied))
        results, out_sems = take(sum(kind == "far" for _, _, kind, _ in outs)), take(len(far))
        arguments = []
        for n, (_, parts) in enumerate(ins):
            if parts:
                at = copied.index(n)
                arguments.append(Given(given[n], buffers[at], in_sems[at], parts, axes[n]))
            else:
                arguments.append(Given(None, given[n]))
        for argument in arguments:
            argument.start()
        made = []
        for _, _, kind, parts in outs:
            ref = results.pop(0) if kind == "far" else near_refs.pop(0)
            made.append(Made(ref, far_refs.pop(0), out_sems.pop(0), parts) if parts else Made(ref))
        body(arguments, made, *refs)
        for argument in arguments:
            argument.get()
        for result in made:
            for copy in result.running:
                copy.wait()

    return pl.pallas_call(
        run,
        out_shape=near + far,
        in_specs=in_specs,
        out_specs=[whole()] * len(near) + [whole(pl.ANY)] * len(far),
        scratch_shapes=extra + list(scratch),
        compiler_params=params(limit),
        cost_estimate=cost(WORK.get(name, 1), 1),
        name=name,
    )(*operands)


def place():
    dp, index = lax.axis_index("dp"), lax.axis_index("index")
    return dp % 2, dp // 2, index // 2, index % 2


def exchange(array, move):
    pairs = []
    for dp in range(4):
        for index in range(8):
            y, x, z, core = move(dp // 2, dp % 2, index // 2, index % 2)
            pairs.append((dp * 8 + index, (y * 2 + x) * 8 + z * 2 + core))
    return lax.ppermute(array, ("dp", "index"), pairs)


def over_core(y, x, z, core):
    return y, x, z, 1 - core


def over_plane(turn):
    return lambda y, x, z, core: (y ^ ((core + turn + 1) % 2 == 0), x ^ ((core + turn) % 2 == 0), z, core)


def over_both(y, x, z, core):
    return 1 - y, 1 - x, z, core


def over_z_by_core(turn):
    return lambda y, x, z, core: (y, x, z ^ (1 + (core + turn) % 2), core)


def over_z(step):
    return lambda y, x, z, core: (y, x, z ^ step, core)


def project_kernel(ins, outs):
    tok, wk, wv, wq, bv, bq, wo, bo, g1, s1, wi, bi, wh, bh, g2, s2 = ins
    q_out, k_out, v_out, cls_out, vec_out = outs
    row = lambda given: given.get()[...].reshape(1, -1)
    tokens = tok.get()
    k_out.ref[...] = dot(tokens[...], wk.get()[...]).astype(BF)
    k_out.put()
    v_out.ref[...] = (dot(tokens[...], wv.get()[...]) + row(bv)).astype(BF)
    v_out.put()
    q_out.ref[...] = (dot(tokens[...], wq.get()[...]) + row(bq)).astype(BF)
    q_out.put()
    rows, width = tokens.shape
    count = rows // SEQ
    head_rows = 16
    owned = lax.broadcasted_iota(jnp.int32, (head_rows, width), 1) // HDIM == lax.broadcasted_iota(
        jnp.int32, (head_rows, width), 0
    )
    contexts, firsts = [], []
    for b in range(count):
        query = q_out.ref[b * SEQ : b * SEQ + 16, :][:1].astype(F32)
        spread = jnp.where(owned, query, 0.0).astype(BF)
        scores = dot_nt(spread, k_out.ref[b * SEQ : (b + 1) * SEQ, :]) * 0.125
        raised = jnp.exp(scores - jnp.max(scores, axis=1, keepdims=True))
        weights = (raised / jnp.sum(raised, axis=1, keepdims=True)).astype(BF)
        mixed = dot(weights, v_out.ref[b * SEQ : (b + 1) * SEQ, :])
        contexts.append(jnp.sum(jnp.where(owned, mixed, 0.0), axis=0, keepdims=True))
        firsts.append(tokens[b * SEQ : b * SEQ + 16, :][:1].astype(F32))
    context = jnp.concatenate(contexts + contexts, axis=0).astype(BF)
    first = jnp.concatenate(firsts + firsts, axis=0)
    attended = dot(context, wo.get()[...]) + row(bo)
    normed, _ = norm_forward(first + attended)
    hidden = normed * row(g1) + row(s1)
    flat = row(bi)
    act, _ = gelu_and_slope(dot(hidden.astype(BF), wi.get()[...]) + flat)
    branch = dot(act.astype(BF), wh.get()[...]) + row(bh)
    normed, _ = norm_forward(hidden + branch)
    lines = lax.broadcasted_iota(jnp.int32, (2 * count, width), 0)
    mine = lines // count == lax.axis_index("index") % 2
    cls_out.ref[...] = jnp.where(mine, normed * row(g2) + row(s2), 0.0).astype(BF)
    cls_out.put()
    for n, vector in enumerate((bq, bv, bo, g1, s1, bh, g2, s2)):
        vec_out.ref[n : n + 1, :] = row(vector)
    for n in range(flat.shape[1] // width):
        vec_out.ref[B_IN + n : B_IN + n + 1, :] = flat[:, n * width : (n + 1) * width]
    vec_out.ref[B_IN + flat.shape[1] // width :, :] = jnp.zeros((16 - B_IN - flat.shape[1] // width, width), F32)
    vec_out.put()


def project(sources):
    rows, width = sources[0].shape
    outs = [((rows, width), BF, "both", 1)] * 3 + [((2 * (rows // SEQ), width), BF, "", 0), ((16, width), F32, "both", 1)]
    return kernel(
        project_kernel, "project", [(part, 1) for part in sources], outs, flops=8 * rows * width * width, moved=20 * MIB
    )


def stacked(pair):
    lane = lax.broadcasted_iota(jnp.int32, pair.shape, 1)
    zero = jnp.zeros_like(pair)
    return jnp.concatenate(
        [jnp.where(lane < HDIM, pair, zero), jnp.where(lane < HDIM, zero, pair)], axis=0
    )


def unstacked(tall):
    half = tall.shape[0] // 2
    lane = lax.broadcasted_iota(jnp.int32, (half, tall.shape[1]), 1)
    return jnp.where(lane < HDIM, tall[:half], tall[half:])


def attend_kernel(ins, outs):
    q, k, v, tok, wo, vec = ins
    p_out, ctx_out, n1_out, i1_out, low_out = outs
    rows, width = q.ref.shape
    pair = 2 * HDIM
    many = rows // SEQ
    for b in range(many):
        here = pl.ds(b * SEQ, SEQ)
        for given in (q, k, v):
            given.get(b)
        for h in range(width // pair):
            lanes = pl.ds(h * pair, pair)
            scores = dot_nt(q.ref[here, lanes], stacked(k.ref[here, lanes])) * 0.125
            parts = []
            for part in (scores[:, :SEQ], scores[:, SEQ:]):
                raised = jnp.exp(part - jnp.max(part, axis=1, keepdims=True))
                parts.append(raised * (1.0 / jnp.sum(raised, axis=1, keepdims=True)))
            weights = jnp.concatenate(parts, axis=1).astype(BF)
            p_out.ref[here, pl.ds(h * 2 * SEQ, 2 * SEQ)] = weights
            ctx_out.ref[here, lanes] = dot(weights, stacked(v.ref[here, lanes])).astype(BF)
        p_out.put(b)
    ctx_out.put()
    vectors, tokens, weights = vec.get(), tok.get(), wo.get()
    attended = dot(ctx_out.ref[...], weights[...]) + line(vectors, B_OUT)
    normed, inverse = norm_forward(tokens[...].astype(F32) + attended)
    n1_out.ref[...] = normed
    low_out.ref[...] = (normed * line(vectors, GAIN_ONE) + line(vectors, SHIFT_ONE)).astype(BF)
    i1_out.ref[...] = jnp.broadcast_to(inverse, i1_out.ref.shape)
    for out in (low_out, n1_out, i1_out):
        out.put()


def attend(q, k, v, tokens, wo, vec, after=()):
    rows, width = q.shape
    many = rows // SEQ
    outs = [
        ((rows, HEADS * SEQ), BF, "far", many),
        ((rows, width), BF, "far", 1),
        ((rows, width), F32, "both", 1),
        ((rows, 128), F32, "far", 1),
        ((rows, width), BF, "both", 1),
    ]
    ins = plain((q, k, v, tokens, wo, vec))
    n1_near, low_near, p, ctx, n1, i1, low = kernel(attend_kernel, "attend", ins, outs, after=after)
    return p, ctx, n1, i1, low, n1_near, low_near


def forward_kernel(ins, outs):
    low, n1, vec, wi, wh, up = ins
    act_out, slope_out, enc_out, back_out, sum_out, first_out, vec_out = outs
    rows, width = low.ref.shape
    vectors, weights = vec.get(), wi.get()
    for n in range(slope_out.ref.shape[0]):
        column = n * FEED_PART
        bias = vectors[B_IN + column // width : B_IN + column // width + 1, :][:, column % width : column % width + FEED_PART]
        value, steep = gelu_and_slope(dot(low.ref[...], weights[:, pl.ds(column, FEED_PART)]) + bias)
        act_out.ref[:, pl.ds(column, FEED_PART)] = value.astype(BF)
        slope_out.ref[n] = steep.astype(BF)
        slope_out.put(n)
    act_out.put()
    weights = wh.get()
    firsts, sums = [], []
    for n in range(enc_out.parts):
        size = rows // enc_out.parts
        here = pl.ds(n * size, size)
        branch = dot(act_out.ref[here, :], weights[...]) + line(vectors, B_HID)
        hidden = n1.ref[here, :] * line(vectors, GAIN_ONE) + line(vectors, SHIFT_ONE)
        normed, inverse = norm_forward(hidden + branch)
        enc_out.ref[here, :] = (normed * line(vectors, GAIN_TWO) + line(vectors, SHIFT_TWO)).astype(BF)
        enc_out.put(n)
        incoming = up.ref[here, :].astype(F32)
        back = norm_backward(incoming * line(vectors, GAIN_TWO), normed, inverse)
        sum_out.ref[here, :] = back
        sum_out.put(n)
        short = back.astype(BF)
        back_out.ref[here, :] = short
        wide = jnp.broadcast_to(inverse, normed.shape)
        firsts.append([[value[b : b + 1] for b in range(0, size, SEQ)] for value in (normed, incoming, wide)])
        sums.append(
            [
                jnp.sum(short.astype(F32), axis=0, keepdims=True),
                jnp.sum(incoming * normed, axis=0, keepdims=True),
                jnp.sum(incoming, axis=0, keepdims=True),
            ]
        )
    lines = [part for n in range(3) for block in firsts for part in block[n]]
    first_out.ref[...] = jnp.concatenate(lines + [jnp.zeros((16 - len(lines), width), F32)], axis=0)
    vec_out.ref[...] = jnp.concatenate(
        [functools.reduce(jnp.add, [block[n] for block in sums]) for n in range(3)] + [jnp.zeros((5, width), F32)], axis=0
    )


def forward(low, n1, vec, wi, wh, up, after=()):
    rows, width = low.shape
    deep = wi.shape[1]
    outs = [
        ((rows, deep), BF, "far", 1),
        ((deep // FEED_PART, rows, FEED_PART), BF, "far", deep // FEED_PART),
        ((rows, width), BF, "far", 2),
        ((rows, width), BF, "near", 0),
        ((rows, width), F32, "far", 2),
        ((16, width), F32, "", 0),
        ((8, width), F32, "", 0),
    ]
    ins = plain((low, n1, vec, wi, wh, up))
    back, first, sums, act, slope, encoded, sum_two = kernel(forward_kernel, "forward", ins, outs, after=after)
    return act, slope, encoded, sum_two, back, first, sums


def split(value, pieces):
    found = []
    for _ in range(pieces):
        piece = value.astype(BF).astype(F32)
        found.append(piece)
        value = value - piece
    return found


def packed_numbers(peak, total, width):
    lane = lax.broadcasted_iota(jnp.int32, (peak.shape[0], width), 1)
    packed = jnp.zeros((peak.shape[0], width), F32)
    for n, piece in enumerate(split(peak, 3) + split(total, 3)):
        packed = jnp.where(lane == n, piece, packed)
    return packed


def unpacked_numbers(packed):
    return (
        packed[:, 0:1] + packed[:, 1:2] + packed[:, 2:3],
        packed[:, 3:4] + packed[:, 4:5] + packed[:, 5:6],
    )


def mark_kernel(ins, outs):
    passages, slots = [given.ref for given in ins]
    _, _, z, core = place()
    many, count = slots.shape
    each = count // 4
    spot = lax.broadcasted_iota(jnp.int32, (count, count), 0)
    question = ((spot // each) ^ z) * each + spot % each
    chosen = lax.broadcasted_iota(jnp.int32, (count, count), 1) == question
    local = passages.shape[0]
    lane = lax.broadcasted_iota(jnp.int32, (count, local), 1)
    marks = []
    for j in range(many):
        ids = jnp.sum(jnp.where(chosen, slots[j : j + 1, :].astype(F32), 0.0), axis=1, keepdims=True)
        ids = ids.astype(jnp.int32) - (2 * z + core) * local
        marks.append(jnp.where(lane == ids, 1.0, 0.0).astype(BF))
    rows = dot(jnp.concatenate(marks, axis=0), passages[...]).astype(BF)
    for j in range(many):
        outs[0].ref[j] = rows[j * count : (j + 1) * count, :]


def mark(passages, slots):
    outs = [((*slots.shape, passages.shape[1]), BF, "near", 0)]
    return kernel(mark_kernel, "mark", plain((passages, slots)), outs)[0]


def collect_kernel(ins, outs):
    outs[0].ref[...] = jnp.concatenate([given.ref[...].astype(F32) for given in ins], axis=0).astype(BF)


def search_kernel(ins, outs):
    mine, theirs, passages, found = [given.ref for given in ins]
    (out,) = outs
    many = found.shape[0]
    cls = (mine[...].astype(F32) + theirs[...].astype(F32)).astype(BF)
    out.ref[:many] = found[...]
    scores = dot_nt(cls, passages[...])
    width = passages.shape[1]
    peak = jnp.max(scores, axis=1, keepdims=True)
    raised = jnp.exp(scores - peak)
    total = jnp.sum(raised, axis=1, keepdims=True)
    mixed = dot(raised.astype(BF), passages[...])
    for n, piece in enumerate(split(mixed, 2)):
        out.ref[many + n] = piece.astype(BF)
    out.ref[many + 2] = packed_numbers(peak, total, width).astype(BF)


def search(mine, theirs, passages, found):
    local, width = passages.shape
    many, count, _ = found.shape
    outs = [((many + 3, count, width), BF, "", 0)]
    ins = [(part, 0) for part in (mine, theirs, passages, found)]
    return kernel(search_kernel, "search", ins, outs, flops=4 * count * local * width)[0]


def joined(records):
    peak = functools.reduce(jnp.maximum, [r[2] for r in records])
    scales = [jnp.exp(r[2] - peak) for r in records]
    rows = functools.reduce(jnp.add, [r[0] for r in records])
    mixed = functools.reduce(jnp.add, [r[1] * s for r, s in zip(records, scales)])
    total = functools.reduce(jnp.add, [r[3] * s for r, s in zip(records, scales)])
    return rows, mixed, peak, total


def meet_kernel(ins, outs):
    records = []
    for given in ins:
        array = given.get()[...].astype(F32)
        many = array.shape[0] - 3
        records.append((array[:many], array[many] + array[many + 1], *unpacked_numbers(array[many + 2])))
    rows, mixed, peak, total = joined(records)
    width = mixed.shape[1]
    lines = [rows[j] for j in range(rows.shape[0])] + split(mixed, 2) + [packed_numbers(peak, total, width)]
    each = mixed.shape[0] // 4
    half = each // 2
    first = lax.axis_index("index") % 2 == 0
    fill = [jnp.zeros((outs[0].ref.shape[0] - len(lines) * half, width), F32)]
    for n, out in enumerate(outs):
        cut = [part[n * each : (n + 1) * each] for part in lines]
        cut = [jnp.where(first, part[:half], part[half:]) for part in cut]
        out.ref[...] = jnp.concatenate(cut + fill, axis=0).astype(BF)
        out.put()


def meet(mine, theirs):
    outs = [((RECORD_ROWS, mine.shape[2]), BF, "", 0)] * 4
    return kernel(meet_kernel, "meet", [(mine, 0), (theirs, 0)], outs)


def question_grad(records, cls, counts, loglik):
    many = loglik.shape[0]
    asked = cls.shape[0] // 2
    parted = []
    for record in records:
        array = record[...].astype(F32)
        lines = [array[n * asked : (n + 1) * asked] for n in range(many + 3)]
        parted.append((jnp.stack(lines[:many]), lines[many] + lines[many + 1], *unpacked_numbers(lines[many + 2])))
    found, mixed, peak, total = joined(parted)
    lse = peak + jnp.log(total)
    index = lax.axis_index("index")
    both = cls[...].astype(F32)
    question = both[:asked] + both[asked:]
    lane = lax.broadcasted_iota(jnp.int32, (asked, many), 1)
    picked = jnp.zeros((asked, many), F32)
    for j in range(many):
        picked = jnp.where(lane == j, jnp.sum(question * found[j], axis=1, keepdims=True), picked)
    questions = loglik.shape[1]
    spot = lax.broadcasted_iota(jnp.int32, (asked, questions), 0) + index * asked
    chosen = lax.broadcasted_iota(jnp.int32, (asked, questions), 1) == spot
    near = jnp.zeros((asked, many), F32)
    for j in range(many):
        value = jnp.sum(jnp.where(chosen, loglik[j : j + 1, :], 0.0), axis=1, keepdims=True)
        near = jnp.where(lane == j, value, near)
    limits = counts[...].reshape(1, questions).astype(F32)
    limits = jnp.sum(jnp.where(chosen, limits, 0.0), axis=1, keepdims=True).astype(jnp.int32)
    valid = lane < limits
    joint = picked - lse + near
    masked = jnp.where(valid, joint, NEGATIVE)
    best = jnp.max(masked, axis=1, keepdims=True)
    marginal = best + jnp.log(jnp.sum(jnp.exp(masked - best), axis=1, keepdims=True))
    centered = jnp.where(valid, joint - marginal, 0.0)
    posterior = jnp.where(valid, jnp.exp(masked - marginal), 0.0)
    entropy = -jnp.sum(posterior * centered, axis=1, keepdims=True)
    picked_grad = jnp.where(valid, -posterior * (1.0 + ENTROPY_WEIGHT * (centered + entropy)), 0.0)
    grad = mixed * (1.0 / total)
    for j in range(many):
        grad = grad + picked_grad[:, j : j + 1] * found[j]
    return grad, jnp.sum(-marginal), jnp.sum(entropy)


def lead_kernel(ins, outs, full):
    r0, r1, r2, r3, cls, counts, loglik, first, sums, vec, back, act = ins
    back_out, fix_out, vec_out, send_out = outs
    records = [given.get() for given in (r0, r1, r2, r3)]
    grad, nll, entropy = question_grad(records, cls.get(), counts.get(), loglik.get())
    many, width = grad.shape
    normed, incoming, inverse = [first.ref[...][n * many : (n + 1) * many] for n in range(3)]
    gain = line(vec.get(), GAIN_TWO)
    old = norm_backward(incoming * gain, normed, inverse[:, :1])
    new = norm_backward((incoming + grad) * gain, normed, inverse[:, :1])
    low = new.astype(BF).astype(F32)
    fix_out.ref[...] = jnp.concatenate([new, jnp.zeros((8 - many, width), F32)], axis=0)
    back_out.ref[...] = back.get()[...]
    top = lax.broadcasted_iota(jnp.int32, (16, width), 0) == 0
    for b in range(many):
        here = pl.ds(b * SEQ, 16)
        rows = back_out.ref[here, :].astype(F32)
        back_out.ref[here, :] = jnp.where(top, low[b : b + 1], rows).astype(BF)
    back_out.put()
    spread = lax.broadcasted_iota(jnp.int32, (1, width), 1)
    numbers = jnp.where(spread == 0, nll, jnp.where(spread == 1, entropy, 0.0))
    old_sums = sums.ref[...]
    change = low - old.astype(BF).astype(F32)
    vec_out.ref[...] = jnp.concatenate(
        [
            old_sums[0:1] + jnp.sum(change, axis=0, keepdims=True),
            old_sums[1:2] + jnp.sum(grad * normed, axis=0, keepdims=True),
            old_sums[2:3] + jnp.sum(grad, axis=0, keepdims=True),
            numbers,
            jnp.zeros((4, width), F32),
        ],
        axis=0,
    )
    _, _, _, core = place()
    hid_product(1 - core, back_out.ref, act.get(), full)
    hid_send(send_out, full)


def lead(records, cls, counts, loglik, first, sums, vec, back, act):
    rows, width = back.shape
    deep = act.shape[1]
    outs = [
        ((rows, width), BF, "both", 1),
        ((8, width), F32, "", 0),
        ((8, width), F32, "", 0),
        ((4, width, deep // 8), BF, "", 0),
    ]
    ins = [(part, 0) for part in (*records, cls)] + [(counts, 1), (loglik, 1), (first, 0), (sums, 0), (vec, 1), (back, 0), (act, 1)]
    return kernel(
        lead_kernel, "lead", ins, outs, scratch=[pltpu.VMEM((width, deep // 2), F32)], flops=rows * width * deep
    )


def slope_kernel(ins, outs):
    low, wh, slope = ins
    pre_out, vec_out = outs
    parts = slope.ref.shape[0]
    width = low.ref.shape[1]
    biases = []
    for n in range(parts):
        here = pl.ds(n * FEED_PART, FEED_PART)
        pre = (dot_nt(low.ref[...], wh.ref[here, :]) * slope.ref[n].astype(F32)).astype(BF)
        pre_out.ref[:, here] = pre
        biases.append(jnp.sum(pre.astype(F32), axis=0, keepdims=True))
    pre_out.put()
    flat = jnp.concatenate(biases, axis=1)
    vec_out.ref[...] = jnp.concatenate(
        [flat[:, n * width : (n + 1) * width] for n in range(flat.shape[1] // width)] + [jnp.zeros((4, width), F32)], axis=0
    )


def descend_kernel(ins, outs):
    pre, wi, fix, sum_two, n1, i1, vec, wo = ins
    attend_out, one_out, grad_out, vec_out = outs
    rows, width = n1.ref.shape
    size = rows // one_out.parts
    gain = None
    sums = []
    spot = lax.broadcasted_iota(jnp.int32, (size, 1), 0)
    for n in range(one_out.parts):
        here = pl.ds(n * size, size)
        back = dot_nt(pre.ref[here, :], wi.ref[...])
        before = sum_two.get(n)[here, :]
        for b in range(size // SEQ):
            question = n * size // SEQ + b
            before = jnp.where(spot == b * SEQ, fix.ref[question : question + 1, :], before)
        incoming = before + back
        normed = n1.get(n)[here, :]
        gain = line(vec.get(), GAIN_ONE) if gain is None else gain
        one = norm_backward(incoming * gain, normed, i1.get()[here, :1])
        one_out.ref[here, :] = one
        one_out.put(n)
        attend_low = one.astype(BF)
        attend_out.ref[here, :] = attend_low
        grad_out.ref[here, :] = dot_nt(attend_low, wo.ref[...]).astype(BF)
        grad_out.put(n)
        sums.append(
            [
                jnp.sum(attend_low.astype(F32), axis=0, keepdims=True),
                jnp.sum(incoming * normed, axis=0, keepdims=True),
                jnp.sum(incoming, axis=0, keepdims=True),
            ]
        )
    vec_out.ref[...] = jnp.concatenate(
        [functools.reduce(jnp.add, [block[n] for block in sums]) for n in range(3)] + [jnp.zeros((5, width), F32)], axis=0
    )


def slope_part(low, wh, slope):
    rows, width = low.shape
    outs = [((rows, wh.shape[0]), BF, "near", 0), ((8, width), F32, "", 0)]
    return kernel(slope_kernel, "slope", plain((low, wh, slope)), outs)


def descend(pre, wi, fix, sum_two, n1, i1, vec, wo, after=()):
    rows, width = n1.shape
    outs = [
        ((rows, width), BF, "near", 0),
        ((rows, width), F32, "far", 2),
        ((rows, width), BF, "near", 0),
        ((8, width), F32, "", 0),
    ]
    ins = [(pre, 0), (wi, 0), (fix, 0), (sum_two, 2), (n1, 2), (i1, 1), (vec, 1), (wo, 0)]
    return kernel(descend_kernel, "descend", ins, outs, after=after)


def unattend_kernel(ins, outs):
    grad, p, q, k, v, one, wq, wk, wv = ins
    dq_out, dk_out, dv_out, input_out, vec_out = outs
    rows, width = q.ref.shape
    pair = 2 * HDIM
    pairs = range(width // pair)
    for b in range(rows // SEQ):
        here = pl.ds(b * SEQ, SEQ)
        lanes = [pl.ds(h * pair, pair) for h in pairs]
        weights = [p.ref[here, pl.ds(h * 2 * SEQ, 2 * SEQ)] for h in pairs]
        incoming = [grad.ref[here, at] for at in lanes]
        sloped = [dot_nt(incoming[h], stacked(v.ref[here, lanes[h]])) for h in pairs]
        values = [unstacked(dot_tn(weights[h], incoming[h])).astype(BF) for h in pairs]
        lows = []
        for h in pairs:
            parts = []
            for n in range(2):
                exact = weights[h][:, n * SEQ : (n + 1) * SEQ].astype(F32)
                steep = sloped[h][:, n * SEQ : (n + 1) * SEQ]
                parts.append(exact * (steep - jnp.sum(steep * exact, axis=1, keepdims=True)))
            lows.append(jnp.concatenate(parts, axis=1).astype(BF))
        queries = [(dot(lows[h], stacked(k.ref[here, lanes[h]])) * 0.125).astype(BF) for h in pairs]
        keys = [(unstacked(dot_tn(lows[h], q.ref[here, lanes[h]])) * 0.125).astype(BF) for h in pairs]
        for h in pairs:
            dv_out.ref[here, lanes[h]] = values[h]
            dq_out.ref[here, lanes[h]] = queries[h]
            dk_out.ref[here, lanes[h]] = keys[h]
    for out in (dq_out, dk_out, dv_out):
        out.put()
    input_out.ref[...] = (
        one.get()[...]
        + dot_nt(dq_out.ref[...], wq.get()[...])
        + dot_nt(dk_out.ref[...], wk.get()[...])
        + dot_nt(dv_out.ref[...], wv.get()[...])
    ).astype(BF)
    input_out.put()
    vec_out.ref[...] = jnp.concatenate(
        [
            jnp.sum(dq_out.ref[...].astype(F32), axis=0, keepdims=True),
            jnp.sum(dv_out.ref[...].astype(F32), axis=0, keepdims=True),
            jnp.zeros((6, width), F32),
        ],
        axis=0,
    )
    vec_out.put()


def unattend(grad, p, q, k, v, one, wq, wk, wv, after=()):
    rows, width = q.shape
    many = rows // SEQ
    outs = [((rows, width), BF, "near", 0)] * 3 + [((rows, width), BF, "far", 1), ((8, width), F32, "", 0)]
    ins = [(part, 0) for part in (grad, p, q, k, v, one, wq, wk, wv)]
    return kernel(unattend_kernel, "unattend", ins, outs, flops=8 * rows * width * width, after=after)


LINES = 96
LANES = 384
WIDTH = 768
MORE = 16


def hid_product(core, low, act, full):
    each = act.shape[1] // 8
    parts = [act[:, pl.ds(pl.multiple_of((2 * z + core) * each, 128), each)] for z in range(4)]
    full[...] = dot_tn(low[...], jnp.concatenate(parts, axis=1))


def hid_send(out, full):
    each = full.shape[1] // 4
    for z in range(4):
        out.ref[z] = full[:, z * each : (z + 1) * each].astype(BF)


def hid_keep_kernel(ins, outs, full):
    low, act, came = [given.get() for given in ins]
    _, _, z, core = place()
    hid_product(core, low, act, full)
    each = full.shape[1] // 4
    for n, far in enumerate((3, 1 + core, 2 - core, 0)):
        lanes = pl.ds(pl.multiple_of((z ^ far) * each, 128), each)
        outs[n // 2].ref[n % 2] = (full[:, lanes] + came[z ^ far].astype(F32)).astype(BF)


def sum_kernel(ins, outs):
    outs[0].ref[...] = functools.reduce(jnp.add, [given.get()[...].astype(F32) for given in ins]).astype(BF)


def pair_kernel(ins, outs):
    kept, came = [given.ref for given in ins]
    outs[0].ref[...] = (kept[0].astype(F32) + came[0].astype(F32)).astype(BF)


def hid_deal_kernel(ins, outs):
    first, _ = spots()
    kept, came, last = [given.ref for given in ins]
    size = outs[0].ref.shape[0]
    for out, number in zip(outs, (1 - first, first)):
        cut = pl.ds(pl.multiple_of(number * size, 16), size)
        out.ref[...] = (kept[1, cut, :].astype(F32) + came[1, cut, :].astype(F32) + last[cut, :].astype(F32)).astype(BF)


def hid_halve_kernel(ins, outs):
    _, second = spots()
    kept, came = [given.ref for given in ins]
    size = outs[0].ref.shape[0]
    for out, number in zip(outs, (1 - second, second)):
        cut = pl.ds(pl.multiple_of(number * size, 16), size)
        out.ref[...] = (kept[cut, :].astype(F32) + came[cut, :].astype(F32)).astype(BF)


def spots(other=0):
    x, y, _, core = place()
    core = core ^ other
    return jnp.where(core == 0, x, y), jnp.where(core == 0, y, x)


def turned_rows(turned, core):
    size = turned.shape[0] // 8
    return jnp.concatenate(
        [turned[pl.ds(pl.multiple_of((2 * z + core) * size, 16), size), :] for z in range(4)], axis=0
    )


def vector_lines(vectors, core):
    lead_vec, slope_vec, descend_vec, unattend_vec = [given.get() for given in vectors]
    eight = jnp.concatenate(
        [unattend_vec[0:2, :], descend_vec[0:1, :], lead_vec[0:1, :], descend_vec[1:3, :], lead_vec[1:3, :]], axis=0
    )
    deep = slope_vec[0:4, :]
    device = lax.axis_index("dp") * 8 + lax.axis_index("index")
    lane = lax.broadcasted_iota(jnp.int32, (1, LANES), 1)
    terms = jnp.zeros((1, LANES), F32)
    for n, piece in enumerate(split(lead_vec[3:4, 0:1], 3) + split(lead_vec[3:4, 1:2], 3)):
        terms = jnp.where(lane == 32 * n + device, piece, terms)
    found = []
    for z in range(4):
        both = []
        for index in (2 * z, 2 * z + 1):
            at = (index % 2) * LANES
            cuts = [eight[:, index * LINES : (index + 1) * LINES]]
            cuts += [deep[index // 2 : index // 2 + 1, at + n * LINES : at + (n + 1) * LINES] for n in range(4)]
            both.append(jnp.concatenate(cuts, axis=0))
        part = jnp.where(core == 0, both[0], both[1])
        part = jnp.concatenate([part, jnp.zeros((part.shape[0], LANES - LINES), F32)], axis=1)
        part = jnp.concatenate([part, terms, jnp.zeros((MORE - part.shape[0] - 1, LANES), F32)], axis=0)
        found.append(jnp.concatenate([part, jnp.zeros((MORE, WIDTH - LANES), F32)], axis=1))
    return found


def cut(full, wide, narrow, vectors, came, target, other=0):
    few = LINES // 4
    mine, _ = spots(other)
    for role in range(2):
        first = mine if role else 1 - mine
        for second in range(2):
            for z in range(4):
                parts = []
                if wide:
                    lanes = pl.ds(pl.multiple_of((first * 2 + second) * WIDTH, 128), WIDTH)
                    parts.append(full[z * LINES : (z + 1) * LINES, lanes])
                rows = pl.ds(pl.multiple_of(first * 2 * few, 8) + z * LINES + second * few, few)
                for n in range(narrow):
                    parts.append(full[rows, n * WIDTH : (n + 1) * WIDTH])
                if vectors is not None:
                    parts.append(jnp.where(first == 0, vectors[z], 0.0) if second == 0 else jnp.zeros((MORE, WIDTH), F32))
                part = jnp.concatenate(parts, axis=0)
                if came is not None:
                    part = part + came(role, second, z).astype(F32)
                target(role, second, z)[...] = part.astype(BF)


def in_product(ins, core, full, turned):
    low, pre = ins
    turned[...] = low.ref[...].T
    full[...] = dot(turned_rows(turned, core), pre.ref[...])
    return full.shape[1]


def in_send_kernel(ins, outs, full, turned):
    _, _, _, core = place()
    wide = in_product(ins, 1 - core, full, turned)
    cut(full, wide, 0, None, None, lambda role, second, z: outs[role].ref.at[second, z], 1)


def in_keep_kernel(ins, outs, full, turned):
    _, _, _, core = place()
    wide = in_product(ins[:2], core, full, turned)
    came = lambda role, second, z: ins[2 + role].ref[second, z]
    cut(full, wide, 0, None, came, lambda role, second, z: outs[role].ref.at[second, z])


def rest_product(ins, core, full, turned):
    tok, ctx, *grads = ins
    turned[...] = tok.ref[...].T
    left = turned_rows(turned, core)
    for n, grad in enumerate(grads):
        width = grad.ref.shape[1]
        if n == len(grads) - 1:
            turned[...] = ctx.ref[...].T
            left = turned_rows(turned, core)
        full[:, n * width : (n + 1) * width] = dot(left, grad.ref[...])


def rest_send_kernel(ins, outs, full, turned):
    _, _, _, core = place()
    rest_product(ins[:6], 1 - core, full, turned)
    vectors = vector_lines(ins[6:10], 1 - core)
    def target(role, second, z):
        array, at = unit(role, second, z)
        return outs[array].ref.at[at]

    cut(full, 0, 4, vectors, None, target, 1)


def rest_keep_kernel(ins, outs, full, turned):
    _, _, _, core = place()
    rest_product(ins[:6], core, full, turned)
    def came(role, second, z):
        array, at = unit(role, second, z)
        return ins[10 + array].ref[at]

    vectors = vector_lines(ins[6:10], core)
    cut(full, 0, 4, vectors, came, lambda role, second, z: (outs[2].ref.at[second] if role else outs[second].ref).at[z])


def plain(operands):
    return [(part, 0) for part in operands]


def unit(role, second, z):
    n = role * 8 + second * 4 + z
    return (0, n) if n < 6 else ((n - 1) // 5, (n - 1) % 5)


def cut_for_partner(body, name, ins, lines, scratch, cuts, after=()):
    dims = [(2, 4)] * 2 if cuts == 2 else [(6,), (5,), (5,)]
    return kernel(body, name, ins, [((*part, lines, WIDTH), BF, "", 0) for part in dims], scratch=scratch, after=after)


def cut_for_chips(body, name, ins, came, lines, scratch, cuts, after=()):
    outs = [((2, 4, lines, WIDTH), BF, "", 0)]
    outs = (outs if cuts == 1 else [((4, lines, WIDTH), BF, "", 0)] * 2) + outs
    return kernel(body, name, [*ins, *plain(came)], outs, scratch=scratch, after=after)


def halve_kernel(ins, outs):
    _, mine = spots()
    kept = ins[0].ref
    for n, second in enumerate((1 - mine, mine)):
        if len(ins) == 2:
            came = ins[1].ref[second]
        else:
            came = jnp.where(second == 0, ins[1].ref[...], ins[2].ref[...])
        value = (kept[second].astype(F32) + came.astype(F32)).astype(BF)
        if n:
            outs[-1].ref[...] = value
            continue
        size = value.shape[0] // (len(outs) - 1)
        for part, out in enumerate(outs[:-1]):
            out.ref[...] = value[part * size : (part + 1) * size]


def deal_kernel(ins, outs):
    _, _, z, core = place()
    kept, *came = [given.ref for given in ins]
    for n, far in enumerate((3, 1 + core, 2 - core, 0)):
        at = z ^ far
        if len(came) == 1:
            other = came[0][at]
        else:
            other = jnp.where(at < 2, came[0][at % 2], came[1][at % 2])
        outs[n // 2].ref[n % 2] = (kept[at].astype(F32) + other.astype(F32)).astype(BF)


def total_kernel(ins, outs):
    kept, came, last = [given.ref for given in ins]
    outs[0].ref[...] = (kept[1].astype(F32) + came[1].astype(F32) + last[...].astype(F32)).astype(BF)


def combine(body, name, operands, outs, after=(), scratch=()):
    return kernel(body, name, plain(operands), [(*out, "", 0) for out in outs], after=after, scratch=scratch)


def dp_sources(ins):
    first, second = spots()
    refs = [given.ref for given in ins]
    values = [ref[n] for ref in refs for n in range(2)] if len(refs) == 2 else [ref[...] for ref in refs]
    numbers = (2 * first + second, 2 * (1 - first) + second, 2 * first + 1 - second, 2 * (1 - first) + 1 - second)
    return [(value.astype(F32), number) for value, number in zip(values, numbers)]


def hid_final_kernel(ins, outs, full):
    size = full.shape[0] // 4
    for value, number in dp_sources(ins):
        full[pl.ds(pl.multiple_of(number * size, 16), size), :] = value
    outs[0].ref[...] = full[...].T


def in_final_kernel(ins, outs):
    for value, number in dp_sources(ins):
        outs[0].ref[:, pl.ds(pl.multiple_of(number * WIDTH, 128), WIDTH)] = value


def rest_final_kernel(questions, a, b, c, d, q, k, v, o, bq, bv, bo, bi, bh, g1, s1, g2, s2, loss, entropy):
    lines = jnp.zeros((MORE, LANES), F32)
    few = LINES // 4
    for value, number in dp_sources([Given(None, ref) for ref in (a, b, c, d)]):
        lines = lines + jnp.where(number == 0, value[LINES:, :LANES], 0.0)
        rows = pl.ds(pl.multiple_of(number * few, 8), few)
        for n, out in enumerate((q, k, v, o)):
            out[rows, :] = value[n * few : (n + 1) * few]
    for n, out in enumerate((bq, bv, bo, bh, g1, s1, g2, s2)):
        out[...] = lines[n, :LINES]
    bi[...] = jnp.concatenate([lines[8 + n : 9 + n, :LINES] for n in range(4)], axis=1).reshape(4 * LINES)
    nll, ent = jnp.sum(lines[12:13, :96]), jnp.sum(lines[12:13, 96:192])
    loss[0, 0] = (nll + ENTROPY_WEIGHT * ent) / questions
    entropy[0, 0] = ent / questions


def rest_final(pieces, questions, width):
    part, deep = width // 8, width // 2
    vectors = [shape((size,), F32) for size in (part, part, part, deep, part, part, part, part, part)]
    return pl.pallas_call(
        functools.partial(rest_final_kernel, questions),
        out_shape=[shape((part, width), F32)] * 4 + vectors + [shape((1, 1), F32)] * 2,
        in_specs=[whole()] * 4,
        out_specs=[whole()] * 13 + [whole(pltpu.SMEM)] * 2,
        compiler_params=params(12),
        cost_estimate=cost(0, MIB),
        name="rest_final",
    )(*pieces)


def halve(name, kept, *came, cuts=1, after=()):
    dims = kept.shape[1:]
    outs = [((dims[0] // cuts, *dims[1:]), BF)] * cuts + [(dims, BF)]
    return combine(halve_kernel, name, (kept, *came), outs, after=after)


def deal(name, halves, after=()):
    *send, kept = halves
    came = [exchange(part, over_plane(1)) for part in send]
    return combine(deal_kernel, name, (kept, *came), [((2, *kept.shape[1:]), BF)] * 2, after=after)


def on_this_slice(
    tokens, upstream, w_query, w_key, w_value, w_out, w_in, w_hid, b_query, b_value, b_out, b_in, b_hid,
    gain_one, shift_one, gain_two, shift_two, passages, slots, counts, gen_loglik,
):
    rows, width = tokens.shape
    deep = w_in.shape[1]
    questions = slots.shape[0] * lax.axis_size("dp")
    q_near, k_near, v_near, cls, vec_near, q, k, v, vec = project(
        (
            tokens, w_key, w_value, w_query, b_value, b_query, w_out, b_out, gain_one, shift_one, w_in, b_in, w_hid, b_hid,
            gain_two, shift_two,
        )
    )
    own = [cls] + [exchange(cls, over_z(n)) for n in (1, 2, 3)]
    p, ctx, n1, i1, low, n1_near, low_near = attend(q_near, k_near, v_near, tokens, w_out, vec_near)
    found = mark(passages, slots.T)
    mine = kernel(collect_kernel, "collect", plain(own), [((4 * cls.shape[0], width), BF, "", 0)], after=(low_near,))[0]
    record = search(mine, exchange(mine, over_core), passages, found)
    cuts = meet(record, exchange(record, over_core))
    records = [cuts[0]] + [exchange(cuts[n], over_z(n)) for n in (1, 2, 3)]
    act, slope, encoded, sum_two, back, first, sums = forward(low_near, n1_near, vec, w_in, w_hid, upstream, after=(cuts[0],))
    back_near, fix, lead_vec, hid_cut, back = lead(records, cls, counts, gen_loglik.T, first, sums, vec, back, act)
    hid_came = exchange(hid_cut, over_core)
    pre, slope_vec = slope_part(back_near, w_hid, slope)
    scratch = [pltpu.VMEM((4 * LINES, deep), F32), pltpu.VMEM((width, rows), BF)]
    in_cut = cut_for_partner(in_send_kernel, "in_send", plain((low, pre)), LINES, scratch, 2)
    in_came = [exchange(part, over_core) for part in in_cut]
    block = (width, deep // 8)
    hid_sent, hid_kept = kernel(
        hid_keep_kernel, "hid_keep", plain((back, act, hid_came)), [((2, *block), BF, "", 0)] * 2,
        scratch=[pltpu.VMEM((width, deep // 2), F32)], after=(in_cut[0],),
    )
    hid_came = exchange(hid_sent, over_z_by_core(0))
    attend_low, grad, descend_vec, one = descend(
        pre, w_in, fix, sum_two, n1, i1, vec, w_out, after=(hid_kept,)
    )
    into = cut_for_chips(
        in_keep_kernel, "in_keep", plain((low, pre)), in_came, LINES, scratch, 1, after=(attend_low,)
    )
    in_first = exchange(into[0], over_plane(0))
    dq, dk, dv, unattend_vec, input_grad = unattend(grad, p, q, k, v, one, w_query, w_key, w_value, after=(into[1],))
    operands = plain((tokens, ctx, dq, dk, dv, attend_low, lead_vec, slope_vec, descend_vec, unattend_vec))
    more = LINES + MORE
    rest_cut = cut_for_partner(rest_send_kernel, "rest_send", operands, more, scratch, 3)
    rest_came = [exchange(part, over_core) for part in rest_cut]
    hid_sum = combine(pair_kernel, "hid_pair", (hid_kept, hid_came), [(block, BF)], after=(rest_cut[0],))[0]
    hid_last = exchange(hid_sum, over_z_by_core(1))
    in_halves = halve("in_halve", into[1], in_first, after=(hid_sum,))
    rest = cut_for_chips(rest_keep_kernel, "rest_keep", operands, rest_came, more, scratch, 2, after=(in_halves[0],))
    rest_first = exchange(rest[0], over_plane(0)), exchange(rest[1], over_plane(0))
    in_parts = deal("in_deal", in_halves, after=(rest[2],))
    in_came = exchange(in_parts[0], over_z_by_core(0))
    rest_halves = halve("rest_halve", rest[2], *rest_first, cuts=2, after=(in_parts[0],))
    in_pair = combine(pair_kernel, "in_pair", (in_parts[1], in_came), [(in_came.shape[1:], BF)], after=(rest_halves[0],))[0]
    in_last = exchange(in_pair, over_z_by_core(1))
    size = ((width // 2, deep // 8), BF)
    hid_parts = combine(hid_deal_kernel, "hid_deal", (hid_kept, hid_came, hid_last), [size] * 2, after=(in_pair,))
    hid_first = exchange(hid_parts[0], over_plane(0))
    operands = (in_parts[1], in_came, in_last)
    in_sum = combine(total_kernel, "in_total", operands, [(in_pair.shape, BF)], after=(hid_parts[0],))[0]
    in_all = in_sum, exchange(in_sum, over_plane(0)), exchange(in_sum, over_plane(1)), exchange(in_sum, over_both)
    rest_parts = deal("rest_deal", rest_halves, after=(in_sum,))
    rest_came = exchange(rest_parts[0], over_z_by_core(0))
    size = ((width // 4, deep // 8), BF)
    hid_halves = combine(hid_halve_kernel, "hid_halve", (hid_parts[1], hid_first), [size] * 2, after=(rest_parts[0],))
    hid_second = exchange(hid_halves[0], over_plane(1))
    rest_pair = combine(pair_kernel, "rest_pair", (rest_parts[1], rest_came), [(rest_came.shape[1:], BF)], after=(hid_halves[0],))[0]
    grad_in = combine(in_final_kernel, "in_final", in_all, [((LINES, deep), F32)], after=(rest_pair,))[0]
    rest_last = exchange(rest_pair, over_z_by_core(1))
    done = pltpu.with_memory_space_constraint(grad_in, pltpu.HBM)
    mine = combine(sum_kernel, "hid_total", (hid_halves[1], hid_second), [size], after=(done,))[0]
    hid_all = mine, exchange(mine, over_plane(0)), exchange(mine, over_plane(1)), exchange(mine, over_both)
    operands = (rest_parts[1], rest_came, rest_last)
    mine = combine(total_kernel, "rest_total", operands, [(rest_pair.shape, BF)], after=(mine,))[0]
    last = mine, exchange(mine, over_plane(0)), exchange(mine, over_plane(1)), exchange(mine, over_both)
    grad_hid = combine(
        hid_final_kernel, "hid_final", hid_all, [((deep // 8, width), F32)], scratch=[pltpu.VMEM((width, deep // 8), F32)],
        after=(mine,),
    )[0]
    *rest, loss, entropy = rest_final(last, questions, width)
    return (
        encoded, input_grad, loss.reshape(()), entropy.reshape(()), *rest[:4], grad_in, grad_hid, *rest[4:],
    )


PRECISE = lax.Precision.HIGHEST


def shortened(array):

    def short(part):
        return part.astype(jnp.bfloat16) if part.dtype == jnp.float32 else part

    return jax.tree.map(short, array)


def product(left_side, right_side):
    return jnp.dot(left_side, right_side, preferred_element_type=jnp.float32)


def times_transpose(left_side, right_side):
    return lax.dot_general(
        left_side, right_side, (((1,), (1,)), ((), ())), preferred_element_type=jnp.float32
    )


def transpose_times(left_side, right_side):
    return lax.dot_general(
        left_side, right_side, (((0,), (0,)), ((), ())), preferred_element_type=jnp.float32
    )


def plain_norm_forward(values, gain_vector, offset):
    center = values - jnp.mean(values, axis=-1, keepdims=True)
    inverse = lax.rsqrt(jnp.mean(center * center, axis=-1, keepdims=True) + NORM_EPSILON)
    normed = center * inverse
    return (normed * gain_vector + offset, normed, inverse)


def plain_norm_backward(incoming, normed, inverse, gain_vector):
    scaled = incoming * gain_vector
    inner = (
        scaled
        - jnp.mean(scaled, axis=-1, keepdims=True)
        - normed * jnp.mean(scaled * normed, axis=-1, keepdims=True)
    )
    return (inverse * inner, jnp.sum(incoming * normed, axis=0), jnp.sum(incoming, axis=0))


def gelu_slope(values):
    cumulative = 0.5 * (1.0 + jax.scipy.special.erf(values * 0.7071067811865476))
    return (
        values * cumulative,
        cumulative + values * jnp.exp(-0.5 * values * values) * 0.3989422804014327,
    )


def on_any_slice(
    tokens,
    upstream,
    w_query,
    w_key,
    w_value,
    w_out,
    w_in,
    w_hid,
    b_query,
    b_value,
    b_out,
    b_in,
    b_hid,
    gain_one,
    shift_one,
    gain_two,
    shift_two,
    passages,
    slots,
    counts,
    gen_loglik,
):
    tok_rows, model_width = tokens.shape
    seq_count = tok_rows // SEQ
    heads_shape = (seq_count, SEQ, HEADS, HDIM)
    inputs = tokens.astype(jnp.float32)
    queries = (product(tokens, w_query) + b_query).astype(jnp.bfloat16).reshape(heads_shape)
    keys_all = product(tokens, w_key).astype(jnp.bfloat16).reshape(heads_shape)
    values_all = (product(tokens, w_value) + b_value).astype(jnp.bfloat16).reshape(heads_shape)
    scores = (
        jnp.einsum("bqhd,bkhd->bhqk", queries, keys_all, preferred_element_type=jnp.float32) * 0.125
    )
    peak = jnp.max(scores, axis=-1, keepdims=True)
    log_total = peak + jnp.log(jnp.sum(jnp.exp(scores - peak), axis=-1, keepdims=True))
    weights_low = jnp.exp(scores - log_total).astype(jnp.bfloat16)
    context = jnp.einsum(
        "bhqk,bkhd->bqhd", weights_low, values_all, preferred_element_type=jnp.float32
    )
    context = context.reshape(tok_rows, model_width).astype(jnp.bfloat16)
    attended = product(context, w_out) + b_out
    hidden_one, normed_one, inverse_one = plain_norm_forward(inputs + attended, gain_one, shift_one)
    hidden_low = hidden_one.astype(jnp.bfloat16)
    pre_act = product(hidden_low, w_in) + b_in
    activated, slope = gelu_slope(pre_act)
    act_low = activated.astype(jnp.bfloat16)
    branch = product(act_low, w_hid) + b_hid
    outputs, normed_two, inverse_two = plain_norm_forward(hidden_one + branch, gain_two, shift_two)
    cls_low = outputs[::SEQ].astype(jnp.bfloat16)
    index_scores = times_transpose(lax.all_gather(cls_low, "index", axis=0, tiled=True), passages)
    group_rows, local_rows = index_scores.shape
    first_row = lax.axis_index("index") * local_rows
    local_slots = slots - first_row
    onehot = (
        lax.broadcasted_iota(jnp.int32, (1, 1, local_rows), 2) == local_slots[:, :, None]
    ).astype(jnp.float32)
    picked_part = jnp.einsum("qr,qsr->qs", index_scores, onehot, precision=PRECISE)
    row_peak = jnp.max(index_scores, axis=1)
    peak_all = lax.pmax(row_peak, "index")
    total_part = jnp.sum(jnp.exp(index_scores - peak_all[:, None]), axis=1)
    total_all, picked = lax.psum((total_part, picked_part), "index")
    index_lse = peak_all + jnp.log(total_all)
    valid = lax.broadcasted_iota(jnp.int32, picked.shape, 1) < counts[:, None]
    joint = picked - index_lse[:, None] + gen_loglik
    masked = jnp.where(valid, joint, -1e30)
    best = jnp.max(masked, axis=1, keepdims=True)
    marginal = best[:, 0] + jnp.log(jnp.sum(jnp.exp(masked - best), axis=1))
    centered = jnp.where(valid, joint - marginal[:, None], 0.0)
    posterior = jnp.where(valid, jnp.exp(masked - marginal[:, None]), 0.0)
    entropy_rows = -jnp.sum(posterior * centered, axis=1)
    nll_total, entropy_total = lax.psum((jnp.sum(-marginal), jnp.sum(entropy_rows)), "dp")
    questions = group_rows * lax.axis_size("dp")
    loss = (nll_total + ENTROPY_WEIGHT * entropy_total) / questions
    entropy = entropy_total / questions
    picked_grad = jnp.where(
        valid, -posterior * (1.0 + ENTROPY_WEIGHT * (centered + entropy_rows[:, None])), 0.0
    )
    score_grad = jnp.exp(index_scores - index_lse[:, None]) + jnp.einsum(
        "qs,qsr->qr", picked_grad, onehot, precision=PRECISE
    )
    score_low = score_grad.astype(jnp.bfloat16)
    cls_grad = lax.psum_scatter(
        product(score_low, passages), "index", scatter_dimension=0, tiled=True
    )
    out_grad = (
        upstream.astype(jnp.float32).reshape(seq_count, SEQ, model_width).at[:, 0].add(cls_grad)
    )
    out_grad = out_grad.reshape(tok_rows, model_width)
    sum_two, grad_gain_two, grad_shift_two = plain_norm_backward(
        out_grad, normed_two, inverse_two, gain_two
    )
    branch_low = sum_two.astype(jnp.bfloat16)
    grad_b_hid = jnp.sum(branch_low.astype(jnp.float32), axis=0)
    grad_w_hid = transpose_times(act_low, branch_low)
    pre_low = (times_transpose(branch_low, w_hid) * slope).astype(jnp.bfloat16)
    grad_b_in = jnp.sum(pre_low.astype(jnp.float32), axis=0)
    grad_w_in = transpose_times(hidden_low, pre_low)
    sum_one, grad_gain_one, grad_shift_one = plain_norm_backward(
        sum_two + times_transpose(pre_low, w_in), normed_one, inverse_one, gain_one
    )
    attend_low = sum_one.astype(jnp.bfloat16)
    grad_b_out = jnp.sum(attend_low.astype(jnp.float32), axis=0)
    grad_w_out = transpose_times(context, attend_low)
    context_grad = times_transpose(attend_low, w_out).astype(jnp.bfloat16).reshape(heads_shape)
    scores_again = (
        jnp.einsum("bqhd,bkhd->bhqk", queries, keys_all, preferred_element_type=jnp.float32) * 0.125
    )
    weights_again = jnp.exp(scores_again - log_total)
    again_low = weights_again.astype(jnp.bfloat16)
    weight_grad = jnp.einsum(
        "bqhd,bkhd->bhqk", context_grad, values_all, preferred_element_type=jnp.float32
    )
    value_grad = jnp.einsum(
        "bhqk,bqhd->bkhd", again_low, context_grad, preferred_element_type=jnp.float32
    )
    value_grad = value_grad.reshape(tok_rows, model_width).astype(jnp.bfloat16)
    logit_grad = weights_again * (
        weight_grad - jnp.sum(weight_grad * weights_again, axis=-1, keepdims=True)
    )
    logit_low = logit_grad.astype(jnp.bfloat16)
    query_grad = (
        jnp.einsum("bhqk,bkhd->bqhd", logit_low, keys_all, preferred_element_type=jnp.float32)
        * 0.125
    )
    query_grad = query_grad.reshape(tok_rows, model_width).astype(jnp.bfloat16)
    key_grad = (
        jnp.einsum("bhqk,bqhd->bkhd", logit_low, queries, preferred_element_type=jnp.float32)
        * 0.125
    )
    key_grad = key_grad.reshape(tok_rows, model_width).astype(jnp.bfloat16)
    input_grad = (
        sum_one
        + times_transpose(query_grad, w_query)
        + times_transpose(key_grad, w_key)
        + times_transpose(value_grad, w_value)
    ).astype(jnp.bfloat16)
    grad_w_query = transpose_times(tokens, query_grad)
    grad_w_key = transpose_times(tokens, key_grad)
    grad_w_value = transpose_times(tokens, value_grad)
    grad_b_query = jnp.sum(query_grad.astype(jnp.float32), axis=0)
    grad_b_value = jnp.sum(value_grad.astype(jnp.float32), axis=0)
    shares = (
        lax.psum_scatter(grad_w_query, "index", scatter_dimension=0, tiled=True),
        lax.psum_scatter(grad_w_key, "index", scatter_dimension=0, tiled=True),
        lax.psum_scatter(grad_w_value, "index", scatter_dimension=0, tiled=True),
        lax.psum_scatter(grad_w_out, "index", scatter_dimension=0, tiled=True),
        lax.psum_scatter(grad_w_in, "index", scatter_dimension=0, tiled=True),
        lax.psum_scatter(grad_w_hid, "index", scatter_dimension=0, tiled=True),
        lax.psum_scatter(grad_b_query, "index", scatter_dimension=0, tiled=True),
        lax.psum_scatter(grad_b_value, "index", scatter_dimension=0, tiled=True),
        lax.psum_scatter(grad_b_out, "index", scatter_dimension=0, tiled=True),
        lax.psum_scatter(grad_b_in, "index", scatter_dimension=0, tiled=True),
        lax.psum_scatter(grad_b_hid, "index", scatter_dimension=0, tiled=True),
        lax.psum_scatter(grad_gain_one, "index", scatter_dimension=0, tiled=True),
        lax.psum_scatter(grad_shift_one, "index", scatter_dimension=0, tiled=True),
        lax.psum_scatter(grad_gain_two, "index", scatter_dimension=0, tiled=True),
        lax.psum_scatter(grad_shift_two, "index", scatter_dimension=0, tiled=True),
    )
    summed = jax.tree.map(
        lambda part: part.astype(jnp.float32), lax.psum(shortened(tuple(shares)), "dp")
    )
    return (outputs.astype(jnp.bfloat16), input_grad, loss, entropy) + tuple(summed)


def solution(mesh):
    here = (mesh.shape["dp"], mesh.shape["index"]) == (4, 8)
    return jax.shard_map(
        on_this_slice if here else on_any_slice,
        mesh=mesh,
        in_specs=(
            P(("dp", "index"), None),
            P(("dp", "index"), None),
            P(),
            P(),
            P(),
            P(),
            P(),
            P(),
            P(),
            P(),
            P(),
            P(),
            P(),
            P(),
            P(),
            P(),
            P(),
            P("index", None),
            P("dp", None),
            P("dp"),
            P("dp", None),
        ),
        out_specs=(
            P(("dp", "index"), None),
            P(("dp", "index"), None),
            P(),
            P(),
            P("index", None),
            P("index", None),
            P("index", None),
            P("index", None),
            P("index", None),
            P("index", None),
            P("index"),
            P("index"),
            P("index"),
            P("index"),
            P("index"),
            P("index"),
            P("index"),
            P("index"),
            P("index"),
        ),
        check_vma=False,
    )
```

```python
import functools
import math

import jax
import jax.numpy as jnp
from jax import lax
from jax.experimental import pallas as pl
from jax.experimental.pallas import tpu as pltpu
from jax.sharding import PartitionSpec as P

HEADS = 12
FEED_PART = 256
SLOT_RECORDS = 13
RECORD_ROWS = 64
HDIM = 64
SEQ = 128
NORM_EPSILON = 1e-06
ENTROPY_WEIGHT = 0.5
BF = jnp.bfloat16
F32 = jnp.float32
MIB = 1 << 20
NEGATIVE = -1e30
WORK = {"in_deal": 5e9, "rest_deal": 1, "hid_deal": 1, "hid_pair": 1}


def dot(left, right):
    return jnp.dot(left, right, preferred_element_type=F32)


def dot_nt(left, right):
    return lax.dot_general(left, right, (((1,), (1,)), ((), ())), preferred_element_type=F32)


def dot_tn(left, right):
    return lax.dot_general(left, right, (((0,), (0,)), ((), ())), preferred_element_type=F32)


B_QUERY, B_VALUE, B_OUT, GAIN_ONE, SHIFT_ONE, B_HID, GAIN_TWO, SHIFT_TWO, B_IN = range(9)


def line(ref, n):
    return ref[n : n + 1, :]


def norm_forward(values):
    center = values - jnp.mean(values, axis=-1, keepdims=True)
    inverse = lax.rsqrt(jnp.mean(center * center, axis=-1, keepdims=True) + NORM_EPSILON)
    return center * inverse, inverse


def norm_backward(scaled, normed, inverse):
    return inverse * (
        scaled
        - jnp.mean(scaled, axis=-1, keepdims=True)
        - normed * jnp.mean(scaled * normed, axis=-1, keepdims=True)
    )


def gelu_and_slope(values):
    cumulative = 0.5 * (1.0 + lax.erf(values * 0.7071067811865476))
    bell = jnp.exp(-0.5 * values * values)
    return values * cumulative, cumulative + values * bell * 0.3989422804014327


def whole(memory=pltpu.VMEM):
    return pl.BlockSpec(memory_space=memory)


def params(limit):
    return pltpu.CompilerParams(vmem_limit_bytes=limit * MIB)


def cost(flops, moved):
    return pl.CostEstimate(flops=int(flops), bytes_accessed=int(moved), transcendentals=0)


def shape(dims, dtype):
    return jax.ShapeDtypeStruct(dims, dtype)


class Given:
    def __init__(self, held, ref, sems=None, parts=0, axis=0):
        self.ref, self.sems, self.parts = ref, sems, parts
        self.waiting = []
        if parts:
            size = ref.shape[axis] // parts
            for n in range(parts):
                cut = (slice(None),) * axis + (pl.ds(n * size, size),)
                source, target = (held, ref) if parts == 1 else (held.at[cut], ref.at[cut])
                self.waiting.append(pltpu.make_async_copy(source, target, sems.at[n]))

    def start(self):
        for copy in self.waiting:
            copy.start()

    def get(self, part=None):
        for n in range(self.parts) if part is None else (part,):
            if self.parts and self.waiting[n] is not None:
                self.waiting[n].wait()
                self.waiting[n] = None
        return self.ref


class Made:
    def __init__(self, ref, far=None, sems=None, parts=0):
        self.ref, self.far, self.sems, self.parts = ref, far, sems, parts
        self.running = []

    def put(self, part=None):
        if not self.parts:
            return
        for n in range(self.parts) if part is None else (part,):
            size = self.ref.shape[0] // self.parts
            cut = pl.ds(n * size, size)
            source, target = (self.ref, self.far) if self.parts == 1 else (self.ref.at[cut], self.far.at[cut])
            copy = pltpu.make_async_copy(source, target, self.sems.at[n])
            copy.start()
            self.running.append(copy)


def kernel(body, name, ins, outs, scratch=(), flops=0, moved=MIB, after=()):
    ins, axes = [part[:2] for part in ins], [(*part, 0)[2] for part in ins]
    operands = [pltpu.with_memory_space_constraint(a, pltpu.HBM) if parts else a for a, parts in ins]
    in_specs = [whole(pl.ANY if parts else pltpu.VMEM) for _, parts in ins]
    operands += after
    in_specs += [whole(pl.ANY)] * len(after)
    near = [(shape if not kind else pltpu.VMEM)(dims, dtype) for dims, dtype, kind, _ in outs if kind != "far"]
    far = [pltpu.HBM(dims, dtype) for dims, dtype, kind, _ in outs if kind in ("far", "both")]
    extra = [pltpu.VMEM(a.shape, a.dtype) for a, parts in ins if parts]
    extra += [pltpu.SemaphoreType.DMA((parts,)) for _, parts in ins if parts]
    extra += [pltpu.VMEM(dims, dtype) for dims, dtype, kind, _ in outs if kind == "far"]
    extra += [pltpu.SemaphoreType.DMA((parts,)) for _, _, _, parts in outs if parts]
    buffers = [part for part in extra + list(scratch) if hasattr(part, "shape") and part.memory_space == pltpu.VMEM]
    limit = sum(math.prod(part.shape) * jnp.dtype(part.dtype).itemsize for part in buffers) // MIB + 8

    def run(*refs):
        refs = list(refs)

        def take(count):
            taken, refs[:] = refs[:count], refs[count:]
            return taken

        given, _, near_refs, far_refs = take(len(ins)), take(len(after)), take(len(near)), take(len(far))
        copied = [n for n, (_, parts) in enumerate(ins) if parts]
        buffers, in_sems = take(len(copied)), take(len(copied))
        results, out_sems = take(sum(kind == "far" for _, _, kind, _ in outs)), take(len(far))
        arguments = []
        for n, (_, parts) in enumerate(ins):
            if parts:
                at = copied.index(n)
                arguments.append(Given(given[n], buffers[at], in_sems[at], parts, axes[n]))
            else:
                arguments.append(Given(None, given[n]))
        for argument in arguments:
            argument.start()
        made = []
        for _, _, kind, parts in outs:
            ref = results.pop(0) if kind == "far" else near_refs.pop(0)
            made.append(Made(ref, far_refs.pop(0), out_sems.pop(0), parts) if parts else Made(ref))
        body(arguments, made, *refs)
        for argument in arguments:
            argument.get()
        for result in made:
            for copy in result.running:
                copy.wait()

    return pl.pallas_call(
        run,
        out_shape=near + far,
        in_specs=in_specs,
        out_specs=[whole()] * len(near) + [whole(pl.ANY)] * len(far),
        scratch_shapes=extra + list(scratch),
        compiler_params=params(limit),
        cost_estimate=cost(WORK.get(name, 1), 1),
        name=name,
    )(*operands)


def place():
    dp, index = lax.axis_index("dp"), lax.axis_index("index")
    return dp % 2, dp // 2, index // 2, index % 2


def exchange(array, move):
    pairs = []
    for dp in range(4):
        for index in range(8):
            y, x, z, core = move(dp // 2, dp % 2, index // 2, index % 2)
            pairs.append((dp * 8 + index, (y * 2 + x) * 8 + z * 2 + core))
    return lax.ppermute(array, ("dp", "index"), pairs)


def over_core(y, x, z, core):
    return y, x, z, 1 - core


def over_plane(turn):
    return lambda y, x, z, core: (y ^ ((core + turn + 1) % 2 == 0), x ^ ((core + turn) % 2 == 0), z, core)


def over_both(y, x, z, core):
    return 1 - y, 1 - x, z, core


def over_z_by_core(turn):
    return lambda y, x, z, core: (y, x, z ^ (1 + (core + turn) % 2), core)


def over_z(step):
    return lambda y, x, z, core: (y, x, z ^ step, core)


def project_kernel(ins, outs):
    tok, wk, wv, wq, bv, bq, wo, bo, g1, s1, wi, bi, wh, bh, g2, s2 = ins
    q_out, k_out, v_out, cls_out, vec_out = outs
    row = lambda given: given.get()[...].reshape(1, -1)
    tokens = tok.get()
    k_out.ref[...] = dot(tokens[...], wk.get()[...]).astype(BF)
    k_out.put()
    v_out.ref[...] = (dot(tokens[...], wv.get()[...]) + row(bv)).astype(BF)
    v_out.put()
    q_out.ref[...] = (dot(tokens[...], wq.get()[...]) + row(bq)).astype(BF)
    q_out.put()
    rows, width = tokens.shape
    count = rows // SEQ
    head_rows = 16
    owned = lax.broadcasted_iota(jnp.int32, (head_rows, width), 1) // HDIM == lax.broadcasted_iota(
        jnp.int32, (head_rows, width), 0
    )
    contexts, firsts = [], []
    for b in range(count):
        query = q_out.ref[b * SEQ : b * SEQ + 16, :][:1].astype(F32)
        spread = jnp.where(owned, query, 0.0).astype(BF)
        scores = dot_nt(spread, k_out.ref[b * SEQ : (b + 1) * SEQ, :]) * 0.125
        raised = jnp.exp(scores - jnp.max(scores, axis=1, keepdims=True))
        weights = (raised / jnp.sum(raised, axis=1, keepdims=True)).astype(BF)
        mixed = dot(weights, v_out.ref[b * SEQ : (b + 1) * SEQ, :])
        contexts.append(jnp.sum(jnp.where(owned, mixed, 0.0), axis=0, keepdims=True))
        firsts.append(tokens[b * SEQ : b * SEQ + 16, :][:1].astype(F32))
    context = jnp.concatenate(contexts + contexts, axis=0).astype(BF)
    first = jnp.concatenate(firsts + firsts, axis=0)
    attended = dot(context, wo.get()[...]) + row(bo)
    normed, _ = norm_forward(first + attended)
    hidden = normed * row(g1) + row(s1)
    flat = row(bi)
    act, _ = gelu_and_slope(dot(hidden.astype(BF), wi.get()[...]) + flat)
    branch = dot(act.astype(BF), wh.get()[...]) + row(bh)
    normed, _ = norm_forward(hidden + branch)
    lines = lax.broadcasted_iota(jnp.int32, (2 * count, width), 0)
    mine = lines // count == lax.axis_index("index") % 2
    cls_out.ref[...] = jnp.where(mine, normed * row(g2) + row(s2), 0.0).astype(BF)
    cls_out.put()
    for n, vector in enumerate((bq, bv, bo, g1, s1, bh, g2, s2)):
        vec_out.ref[n : n + 1, :] = row(vector)
    for n in range(flat.shape[1] // width):
        vec_out.ref[B_IN + n : B_IN + n + 1, :] = flat[:, n * width : (n + 1) * width]
    vec_out.ref[B_IN + flat.shape[1] // width :, :] = jnp.zeros((16 - B_IN - flat.shape[1] // width, width), F32)
    vec_out.put()


def project(sources):
    rows, width = sources[0].shape
    outs = [((rows, width), BF, "both", 1)] * 3 + [((2 * (rows // SEQ), width), BF, "", 0), ((16, width), F32, "both", 1)]
    return kernel(
        project_kernel, "project", [(part, 1) for part in sources], outs, flops=8 * rows * width * width, moved=20 * MIB
    )


def stacked(pair):
    lane = lax.broadcasted_iota(jnp.int32, pair.shape, 1)
    zero = jnp.zeros_like(pair)
    return jnp.concatenate(
        [jnp.where(lane < HDIM, pair, zero), jnp.where(lane < HDIM, zero, pair)], axis=0
    )


def unstacked(tall):
    half = tall.shape[0] // 2
    lane = lax.broadcasted_iota(jnp.int32, (half, tall.shape[1]), 1)
    return jnp.where(lane < HDIM, tall[:half], tall[half:])


def attend_kernel(ins, outs):
    q, k, v, tok, wo, vec = ins
    p_out, ctx_out, n1_out, i1_out, low_out = outs
    rows, width = q.ref.shape
    pair = 2 * HDIM
    many = rows // SEQ
    for b in range(many):
        here = pl.ds(b * SEQ, SEQ)
        for given in (q, k, v):
            given.get(b)
        for h in range(width // pair):
            lanes = pl.ds(h * pair, pair)
            scores = dot_nt(q.ref[here, lanes], stacked(k.ref[here, lanes])) * 0.125
            parts = []
            for part in (scores[:, :SEQ], scores[:, SEQ:]):
                raised = jnp.exp(part - jnp.max(part, axis=1, keepdims=True))
                parts.append(raised * (1.0 / jnp.sum(raised, axis=1, keepdims=True)))
            weights = jnp.concatenate(parts, axis=1).astype(BF)
            p_out.ref[here, pl.ds(h * 2 * SEQ, 2 * SEQ)] = weights
            ctx_out.ref[here, lanes] = dot(weights, stacked(v.ref[here, lanes])).astype(BF)
        p_out.put(b)
    ctx_out.put()
    vectors, tokens, weights = vec.get(), tok.get(), wo.get()
    attended = dot(ctx_out.ref[...], weights[...]) + line(vectors, B_OUT)
    normed, inverse = norm_forward(tokens[...].astype(F32) + attended)
    n1_out.ref[...] = normed
    low_out.ref[...] = (normed * line(vectors, GAIN_ONE) + line(vectors, SHIFT_ONE)).astype(BF)
    i1_out.ref[...] = jnp.broadcast_to(inverse, i1_out.ref.shape)
    for out in (low_out, n1_out, i1_out):
        out.put()


def attend(q, k, v, tokens, wo, vec, after=()):
    rows, width = q.shape
    many = rows // SEQ
    outs = [
        ((rows, HEADS * SEQ), BF, "far", many),
        ((rows, width), BF, "far", 1),
        ((rows, width), F32, "both", 1),
        ((rows, 128), F32, "far", 1),
        ((rows, width), BF, "both", 1),
    ]
    ins = plain((q, k, v, tokens, wo, vec))
    n1_near, low_near, p, ctx, n1, i1, low = kernel(attend_kernel, "attend", ins, outs, after=after)
    return p, ctx, n1, i1, low, n1_near, low_near


def forward_kernel(ins, outs):
    low, n1, vec, wi, wh, up = ins
    act_out, slope_out, enc_out, back_out, sum_out, first_out, vec_out = outs
    rows, width = low.ref.shape
    vectors, weights = vec.get(), wi.get()
    for n in range(slope_out.ref.shape[0]):
        column = n * FEED_PART
        bias = vectors[B_IN + column // width : B_IN + column // width + 1, :][:, column % width : column % width + FEED_PART]
        value, steep = gelu_and_slope(dot(low.ref[...], weights[:, pl.ds(column, FEED_PART)]) + bias)
        act_out.ref[:, pl.ds(column, FEED_PART)] = value.astype(BF)
        slope_out.ref[n] = steep.astype(BF)
        slope_out.put(n)
    act_out.put()
    weights = wh.get()
    firsts, sums = [], []
    for n in range(enc_out.parts):
        size = rows // enc_out.parts
        here = pl.ds(n * size, size)
        branch = dot(act_out.ref[here, :], weights[...]) + line(vectors, B_HID)
        hidden = n1.ref[here, :] * line(vectors, GAIN_ONE) + line(vectors, SHIFT_ONE)
        normed, inverse = norm_forward(hidden + branch)
        enc_out.ref[here, :] = (normed * line(vectors, GAIN_TWO) + line(vectors, SHIFT_TWO)).astype(BF)
        enc_out.put(n)
        incoming = up.ref[here, :].astype(F32)
        back = norm_backward(incoming * line(vectors, GAIN_TWO), normed, inverse)
        sum_out.ref[here, :] = back
        sum_out.put(n)
        short = back.astype(BF)
        back_out.ref[here, :] = short
        wide = jnp.broadcast_to(inverse, normed.shape)
        firsts.append([[value[b : b + 1] for b in range(0, size, SEQ)] for value in (normed, incoming, wide)])
        sums.append(
            [
                jnp.sum(short.astype(F32), axis=0, keepdims=True),
                jnp.sum(incoming * normed, axis=0, keepdims=True),
                jnp.sum(incoming, axis=0, keepdims=True),
            ]
        )
    lines = [part for n in range(3) for block in firsts for part in block[n]]
    first_out.ref[...] = jnp.concatenate(lines + [jnp.zeros((16 - len(lines), width), F32)], axis=0)
    vec_out.ref[...] = jnp.concatenate(
        [functools.reduce(jnp.add, [block[n] for block in sums]) for n in range(3)] + [jnp.zeros((5, width), F32)], axis=0
    )


def forward(low, n1, vec, wi, wh, up, after=()):
    rows, width = low.shape
    deep = wi.shape[1]
    outs = [
        ((rows, deep), BF, "far", 1),
        ((deep // FEED_PART, rows, FEED_PART), BF, "far", deep // FEED_PART),
        ((rows, width), BF, "far", 2),
        ((rows, width), BF, "near", 0),
        ((rows, width), F32, "far", 2),
        ((16, width), F32, "", 0),
        ((8, width), F32, "", 0),
    ]
    ins = plain((low, n1, vec, wi, wh, up))
    back, first, sums, act, slope, encoded, sum_two = kernel(forward_kernel, "forward", ins, outs, after=after)
    return act, slope, encoded, sum_two, back, first, sums


def split(value, pieces):
    found = []
    for _ in range(pieces):
        piece = value.astype(BF).astype(F32)
        found.append(piece)
        value = value - piece
    return found


def packed_numbers(peak, total, width):
    lane = lax.broadcasted_iota(jnp.int32, (peak.shape[0], width), 1)
    packed = jnp.zeros((peak.shape[0], width), F32)
    for n, piece in enumerate(split(peak, 3) + split(total, 3)):
        packed = jnp.where(lane == n, piece, packed)
    return packed


def unpacked_numbers(packed):
    return (
        packed[:, 0:1] + packed[:, 1:2] + packed[:, 2:3],
        packed[:, 3:4] + packed[:, 4:5] + packed[:, 5:6],
    )


def mark_kernel(ins, outs):
    passages, slots = [given.ref for given in ins]
    _, _, z, core = place()
    many, count = slots.shape
    each = count // 4
    spot = lax.broadcasted_iota(jnp.int32, (count, count), 0)
    question = ((spot // each) ^ z) * each + spot % each
    chosen = lax.broadcasted_iota(jnp.int32, (count, count), 1) == question
    local = passages.shape[0]
    lane = lax.broadcasted_iota(jnp.int32, (count, local), 1)
    marks = []
    for j in range(many):
        ids = jnp.sum(jnp.where(chosen, slots[j : j + 1, :].astype(F32), 0.0), axis=1, keepdims=True)
        ids = ids.astype(jnp.int32) - (2 * z + core) * local
        marks.append(jnp.where(lane == ids, 1.0, 0.0).astype(BF))
    rows = dot(jnp.concatenate(marks, axis=0), passages[...]).astype(BF)
    for j in range(many):
        outs[0].ref[j] = rows[j * count : (j + 1) * count, :]


def mark(passages, slots):
    outs = [((*slots.shape, passages.shape[1]), BF, "near", 0)]
    return kernel(mark_kernel, "mark", plain((passages, slots)), outs)[0]


def collect_kernel(ins, outs):
    outs[0].ref[...] = jnp.concatenate([given.ref[...].astype(F32) for given in ins], axis=0).astype(BF)


def search_kernel(ins, outs):
    mine, theirs, passages, found = [given.ref for given in ins]
    (out,) = outs
    many = found.shape[0]
    cls = (mine[...].astype(F32) + theirs[...].astype(F32)).astype(BF)
    out.ref[:many] = found[...]
    scores = dot_nt(cls, passages[...])
    width = passages.shape[1]
    peak = jnp.max(scores, axis=1, keepdims=True)
    raised = jnp.exp(scores - peak)
    total = jnp.sum(raised, axis=1, keepdims=True)
    mixed = dot(raised.astype(BF), passages[...])
    for n, piece in enumerate(split(mixed, 2)):
        out.ref[many + n] = piece.astype(BF)
    out.ref[many + 2] = packed_numbers(peak, total, width).astype(BF)


def search(mine, theirs, passages, found):
    local, width = passages.shape
    many, count, _ = found.shape
    outs = [((many + 3, count, width), BF, "", 0)]
    ins = [(part, 0) for part in (mine, theirs, passages, found)]
    return kernel(search_kernel, "search", ins, outs, flops=4 * count * local * width)[0]


def joined(records):
    peak = functools.reduce(jnp.maximum, [r[2] for r in records])
    scales = [jnp.exp(r[2] - peak) for r in records]
    rows = functools.reduce(jnp.add, [r[0] for r in records])
    mixed = functools.reduce(jnp.add, [r[1] * s for r, s in zip(records, scales)])
    total = functools.reduce(jnp.add, [r[3] * s for r, s in zip(records, scales)])
    return rows, mixed, peak, total


def meet_kernel(ins, outs):
    records = []
    for given in ins:
        array = given.get()[...].astype(F32)
        many = array.shape[0] - 3
        records.append((array[:many], array[many] + array[many + 1], *unpacked_numbers(array[many + 2])))
    rows, mixed, peak, total = joined(records)
    width = mixed.shape[1]
    lines = [rows[j] for j in range(rows.shape[0])] + split(mixed, 2) + [packed_numbers(peak, total, width)]
    each = mixed.shape[0] // 4
    half = each // 2
    first = lax.axis_index("index") % 2 == 0
    fill = [jnp.zeros((outs[0].ref.shape[0] - len(lines) * half, width), F32)]
    for n, out in enumerate(outs):
        cut = [part[n * each : (n + 1) * each] for part in lines]
        cut = [jnp.where(first, part[:half], part[half:]) for part in cut]
        out.ref[...] = jnp.concatenate(cut + fill, axis=0).astype(BF)
        out.put()


def meet(mine, theirs):
    outs = [((RECORD_ROWS, mine.shape[2]), BF, "", 0)] * 4
    return kernel(meet_kernel, "meet", [(mine, 0), (theirs, 0)], outs)


def question_grad(records, cls, counts, loglik):
    many = loglik.shape[0]
    asked = cls.shape[0] // 2
    parted = []
    for record in records:
        array = record[...].astype(F32)
        lines = [array[n * asked : (n + 1) * asked] for n in range(many + 3)]
        parted.append((jnp.stack(lines[:many]), lines[many] + lines[many + 1], *unpacked_numbers(lines[many + 2])))
    found, mixed, peak, total = joined(parted)
    lse = peak + jnp.log(total)
    index = lax.axis_index("index")
    both = cls[...].astype(F32)
    question = both[:asked] + both[asked:]
    lane = lax.broadcasted_iota(jnp.int32, (asked, many), 1)
    picked = jnp.zeros((asked, many), F32)
    for j in range(many):
        picked = jnp.where(lane == j, jnp.sum(question * found[j], axis=1, keepdims=True), picked)
    questions = loglik.shape[1]
    spot = lax.broadcasted_iota(jnp.int32, (asked, questions), 0) + index * asked
    chosen = lax.broadcasted_iota(jnp.int32, (asked, questions), 1) == spot
    near = jnp.zeros((asked, many), F32)
    for j in range(many):
        value = jnp.sum(jnp.where(chosen, loglik[j : j + 1, :], 0.0), axis=1, keepdims=True)
        near = jnp.where(lane == j, value, near)
    limits = counts[...].reshape(1, questions).astype(F32)
    limits = jnp.sum(jnp.where(chosen, limits, 0.0), axis=1, keepdims=True).astype(jnp.int32)
    valid = lane < limits
    joint = picked - lse + near
    masked = jnp.where(valid, joint, NEGATIVE)
    best = jnp.max(masked, axis=1, keepdims=True)
    marginal = best + jnp.log(jnp.sum(jnp.exp(masked - best), axis=1, keepdims=True))
    centered = jnp.where(valid, joint - marginal, 0.0)
    posterior = jnp.where(valid, jnp.exp(masked - marginal), 0.0)
    entropy = -jnp.sum(posterior * centered, axis=1, keepdims=True)
    picked_grad = jnp.where(valid, -posterior * (1.0 + ENTROPY_WEIGHT * (centered + entropy)), 0.0)
    grad = mixed * (1.0 / total)
    for j in range(many):
        grad = grad + picked_grad[:, j : j + 1] * found[j]
    return grad, jnp.sum(-marginal), jnp.sum(entropy)


def lead_kernel(ins, outs, full):
    r0, r1, r2, r3, cls, counts, loglik, first, sums, vec, back, act = ins
    back_out, fix_out, vec_out, send_out = outs
    records = [given.get() for given in (r0, r1, r2, r3)]
    grad, nll, entropy = question_grad(records, cls.get(), counts.get(), loglik.get())
    many, width = grad.shape
    normed, incoming, inverse = [first.ref[...][n * many : (n + 1) * many] for n in range(3)]
    gain = line(vec.get(), GAIN_TWO)
    old = norm_backward(incoming * gain, normed, inverse[:, :1])
    new = norm_backward((incoming + grad) * gain, normed, inverse[:, :1])
    low = new.astype(BF).astype(F32)
    fix_out.ref[...] = jnp.concatenate([new, jnp.zeros((8 - many, width), F32)], axis=0)
    back_out.ref[...] = back.get()[...]
    top = lax.broadcasted_iota(jnp.int32, (16, width), 0) == 0
    for b in range(many):
        here = pl.ds(b * SEQ, 16)
        rows = back_out.ref[here, :].astype(F32)
        back_out.ref[here, :] = jnp.where(top, low[b : b + 1], rows).astype(BF)
    back_out.put()
    spread = lax.broadcasted_iota(jnp.int32, (1, width), 1)
    numbers = jnp.where(spread == 0, nll, jnp.where(spread == 1, entropy, 0.0))
    old_sums = sums.ref[...]
    change = low - old.astype(BF).astype(F32)
    vec_out.ref[...] = jnp.concatenate(
        [
            old_sums[0:1] + jnp.sum(change, axis=0, keepdims=True),
            old_sums[1:2] + jnp.sum(grad * normed, axis=0, keepdims=True),
            old_sums[2:3] + jnp.sum(grad, axis=0, keepdims=True),
            numbers,
            jnp.zeros((4, width), F32),
        ],
        axis=0,
    )
    _, _, _, core = place()
    hid_product(1 - core, back_out.ref, act.get(), full)
    hid_send(send_out, full)


def lead(records, cls, counts, loglik, first, sums, vec, back, act):
    rows, width = back.shape
    deep = act.shape[1]
    outs = [
        ((rows, width), BF, "near", 0),
        ((8, width), F32, "", 0),
        ((8, width), F32, "", 0),
        ((4, width, deep // 8), BF, "", 0),
    ]
    ins = [(part, 0) for part in (*records, cls)] + [(counts, 1), (loglik, 1), (first, 0), (sums, 0), (vec, 1), (back, 0), (act, 1)]
    return kernel(
        lead_kernel, "lead", ins, outs, scratch=[pltpu.VMEM((width, deep // 2), F32)], flops=rows * width * deep
    )


def slope_kernel(ins, outs):
    low, wh, slope = ins
    pre_out, vec_out = outs
    parts = slope.ref.shape[0]
    width = low.ref.shape[1]
    biases = []
    for n in range(parts):
        here = pl.ds(n * FEED_PART, FEED_PART)
        pre = (dot_nt(low.ref[...], wh.ref[here, :]) * slope.ref[n].astype(F32)).astype(BF)
        pre_out.ref[:, here] = pre
        biases.append(jnp.sum(pre.astype(F32), axis=0, keepdims=True))
    pre_out.put()
    flat = jnp.concatenate(biases, axis=1)
    vec_out.ref[...] = jnp.concatenate(
        [flat[:, n * width : (n + 1) * width] for n in range(flat.shape[1] // width)] + [jnp.zeros((4, width), F32)], axis=0
    )


def descend_kernel(ins, outs):
    pre, wi, fix, sum_two, n1, i1, vec, wo = ins
    attend_out, one_out, grad_out, vec_out = outs
    rows, width = n1.ref.shape
    size = rows // one_out.parts
    gain = None
    sums = []
    spot = lax.broadcasted_iota(jnp.int32, (size, 1), 0)
    for n in range(one_out.parts):
        here = pl.ds(n * size, size)
        back = dot_nt(pre.ref[here, :], wi.ref[...])
        before = sum_two.get(n)[here, :]
        for b in range(size // SEQ):
            question = n * size // SEQ + b
            before = jnp.where(spot == b * SEQ, fix.ref[question : question + 1, :], before)
        incoming = before + back
        normed = n1.get(n)[here, :]
        gain = line(vec.get(), GAIN_ONE) if gain is None else gain
        one = norm_backward(incoming * gain, normed, i1.get()[here, :1])
        one_out.ref[here, :] = one
        one_out.put(n)
        attend_low = one.astype(BF)
        attend_out.ref[here, :] = attend_low
        grad_out.ref[here, :] = dot_nt(attend_low, wo.ref[...]).astype(BF)
        grad_out.put(n)
        sums.append(
            [
                jnp.sum(attend_low.astype(F32), axis=0, keepdims=True),
                jnp.sum(incoming * normed, axis=0, keepdims=True),
                jnp.sum(incoming, axis=0, keepdims=True),
            ]
        )
    vec_out.ref[...] = jnp.concatenate(
        [functools.reduce(jnp.add, [block[n] for block in sums]) for n in range(3)] + [jnp.zeros((5, width), F32)], axis=0
    )


def slope_part(low, wh, slope):
    rows, width = low.shape
    outs = [((rows, wh.shape[0]), BF, "near", 0), ((8, width), F32, "", 0)]
    return kernel(slope_kernel, "slope", plain((low, wh, slope)), outs)


def descend(pre, wi, fix, sum_two, n1, i1, vec, wo, after=()):
    rows, width = n1.shape
    outs = [
        ((rows, width), BF, "near", 0),
        ((rows, width), F32, "far", 2),
        ((rows, width), BF, "near", 0),
        ((8, width), F32, "", 0),
    ]
    ins = [(pre, 0), (wi, 0), (fix, 0), (sum_two, 2), (n1, 2), (i1, 1), (vec, 1), (wo, 0)]
    return kernel(descend_kernel, "descend", ins, outs, after=after)


def unattend_kernel(ins, outs):
    grad, p, q, k, v, one, wq, wk, wv = ins
    dq_out, dk_out, dv_out, input_out, vec_out = outs
    rows, width = q.ref.shape
    pair = 2 * HDIM
    pairs = range(width // pair)
    for b in range(rows // SEQ):
        here = pl.ds(b * SEQ, SEQ)
        lanes = [pl.ds(h * pair, pair) for h in pairs]
        weights = [p.ref[here, pl.ds(h * 2 * SEQ, 2 * SEQ)] for h in pairs]
        incoming = [grad.ref[here, at] for at in lanes]
        sloped = [dot_nt(incoming[h], stacked(v.ref[here, lanes[h]])) for h in pairs]
        values = [unstacked(dot_tn(weights[h], incoming[h])).astype(BF) for h in pairs]
        lows = []
        for h in pairs:
            parts = []
            for n in range(2):
                exact = weights[h][:, n * SEQ : (n + 1) * SEQ].astype(F32)
                steep = sloped[h][:, n * SEQ : (n + 1) * SEQ]
                parts.append(exact * (steep - jnp.sum(steep * exact, axis=1, keepdims=True)))
            lows.append(jnp.concatenate(parts, axis=1).astype(BF))
        queries = [(dot(lows[h], stacked(k.ref[here, lanes[h]])) * 0.125).astype(BF) for h in pairs]
        keys = [(unstacked(dot_tn(lows[h], q.ref[here, lanes[h]])) * 0.125).astype(BF) for h in pairs]
        for h in pairs:
            dv_out.ref[here, lanes[h]] = values[h]
            dq_out.ref[here, lanes[h]] = queries[h]
            dk_out.ref[here, lanes[h]] = keys[h]
    for out in (dq_out, dk_out, dv_out):
        out.put()
    input_out.ref[...] = (
        one.get()[...]
        + dot_nt(dq_out.ref[...], wq.get()[...])
        + dot_nt(dk_out.ref[...], wk.get()[...])
        + dot_nt(dv_out.ref[...], wv.get()[...])
    ).astype(BF)
    input_out.put()
    vec_out.ref[...] = jnp.concatenate(
        [
            jnp.sum(dq_out.ref[...].astype(F32), axis=0, keepdims=True),
            jnp.sum(dv_out.ref[...].astype(F32), axis=0, keepdims=True),
            jnp.zeros((6, width), F32),
        ],
        axis=0,
    )
    vec_out.put()


def unattend(grad, p, q, k, v, one, wq, wk, wv, after=()):
    rows, width = q.shape
    many = rows // SEQ
    outs = [((rows, width), BF, "near", 0)] * 3 + [((rows, width), BF, "far", 1), ((8, width), F32, "", 0)]
    ins = [(part, 0) for part in (grad, p, q, k, v, one, wq, wk, wv)]
    return kernel(unattend_kernel, "unattend", ins, outs, flops=8 * rows * width * width, after=after)


LINES = 96
LANES = 384
WIDTH = 768
MORE = 16


def hid_product(core, low, act, full):
    each = act.shape[1] // 8
    parts = [act[:, pl.ds(pl.multiple_of((2 * z + core) * each, 128), each)] for z in range(4)]
    full[...] = dot_tn(low[...], jnp.concatenate(parts, axis=1))


def hid_send(out, full):
    each = full.shape[1] // 4
    for z in range(4):
        out.ref[z] = full[:, z * each : (z + 1) * each].astype(BF)


def hid_keep_kernel(ins, outs, full):
    low, act, came = [given.get() for given in ins]
    _, _, z, core = place()
    hid_product(core, low, act, full)
    each = full.shape[1] // 4
    for n, far in enumerate((3, 1 + core, 2 - core, 0)):
        lanes = pl.ds(pl.multiple_of((z ^ far) * each, 128), each)
        outs[n // 2].ref[n % 2] = (full[:, lanes] + came[z ^ far].astype(F32)).astype(BF)


def sum_kernel(ins, outs):
    outs[0].ref[...] = functools.reduce(jnp.add, [given.get()[...].astype(F32) for given in ins]).astype(BF)


def pair_kernel(ins, outs):
    kept, came = [given.ref for given in ins]
    outs[0].ref[...] = (kept[0].astype(F32) + came[0].astype(F32)).astype(BF)


def hid_deal_kernel(ins, outs):
    first, _ = spots()
    kept, came, last = [given.ref for given in ins]
    size = outs[0].ref.shape[0]
    for out, number in zip(outs, (1 - first, first)):
        cut = pl.ds(pl.multiple_of(number * size, 16), size)
        out.ref[...] = (kept[1, cut, :].astype(F32) + came[1, cut, :].astype(F32) + last[cut, :].astype(F32)).astype(BF)


def hid_halve_kernel(ins, outs):
    _, second = spots()
    kept, came = [given.ref for given in ins]
    size = outs[0].ref.shape[0]
    for out, number in zip(outs, (1 - second, second)):
        cut = pl.ds(pl.multiple_of(number * size, 16), size)
        out.ref[...] = (kept[cut, :].astype(F32) + came[cut, :].astype(F32)).astype(BF)


def spots(other=0):
    x, y, _, core = place()
    core = core ^ other
    return jnp.where(core == 0, x, y), jnp.where(core == 0, y, x)


def turned_rows(turned, core):
    size = turned.shape[0] // 8
    return jnp.concatenate(
        [turned[pl.ds(pl.multiple_of((2 * z + core) * size, 16), size), :] for z in range(4)], axis=0
    )


def vector_lines(vectors, core):
    lead_vec, slope_vec, descend_vec, unattend_vec = [given.get() for given in vectors]
    eight = jnp.concatenate(
        [unattend_vec[0:2, :], descend_vec[0:1, :], lead_vec[0:1, :], descend_vec[1:3, :], lead_vec[1:3, :]], axis=0
    )
    deep = slope_vec[0:4, :]
    device = lax.axis_index("dp") * 8 + lax.axis_index("index")
    lane = lax.broadcasted_iota(jnp.int32, (1, LANES), 1)
    terms = jnp.zeros((1, LANES), F32)
    for n, piece in enumerate(split(lead_vec[3:4, 0:1], 3) + split(lead_vec[3:4, 1:2], 3)):
        terms = jnp.where(lane == 32 * n + device, piece, terms)
    found = []
    for z in range(4):
        both = []
        for index in (2 * z, 2 * z + 1):
            at = (index % 2) * LANES
            cuts = [eight[:, index * LINES : (index + 1) * LINES]]
            cuts += [deep[index // 2 : index // 2 + 1, at + n * LINES : at + (n + 1) * LINES] for n in range(4)]
            both.append(jnp.concatenate(cuts, axis=0))
        part = jnp.where(core == 0, both[0], both[1])
        part = jnp.concatenate([part, jnp.zeros((part.shape[0], LANES - LINES), F32)], axis=1)
        part = jnp.concatenate([part, terms, jnp.zeros((MORE - part.shape[0] - 1, LANES), F32)], axis=0)
        found.append(jnp.concatenate([part, jnp.zeros((MORE, WIDTH - LANES), F32)], axis=1))
    return found


def cut(full, wide, narrow, vectors, came, target, other=0):
    few = LINES // 4
    mine, _ = spots(other)
    for role in range(2):
        first = mine if role else 1 - mine
        for second in range(2):
            for z in range(4):
                parts = []
                if wide:
                    lanes = pl.ds(pl.multiple_of((first * 2 + second) * WIDTH, 128), WIDTH)
                    parts.append(full[z * LINES : (z + 1) * LINES, lanes])
                rows = pl.ds(pl.multiple_of(first * 2 * few, 8) + z * LINES + second * few, few)
                for n in range(narrow):
                    parts.append(full[rows, n * WIDTH : (n + 1) * WIDTH])
                if vectors is not None:
                    parts.append(jnp.where(first == 0, vectors[z], 0.0) if second == 0 else jnp.zeros((MORE, WIDTH), F32))
                part = jnp.concatenate(parts, axis=0)
                if came is not None:
                    part = part + came(role, second, z).astype(F32)
                target(role, second, z)[...] = part.astype(BF)


def in_product(ins, core, full, turned):
    low, pre = ins
    turned[...] = low.ref[...].T
    full[...] = dot(turned_rows(turned, core), pre.ref[...])
    return full.shape[1]


def in_send_kernel(ins, outs, full, turned):
    _, _, _, core = place()
    wide = in_product(ins, 1 - core, full, turned)
    cut(full, wide, 0, None, None, lambda role, second, z: outs[role].ref.at[second, z], 1)


def in_keep_kernel(ins, outs, full, turned):
    _, _, _, core = place()
    wide = in_product(ins[:2], core, full, turned)
    came = lambda role, second, z: ins[2 + role].ref[second, z]
    cut(full, wide, 0, None, came, lambda role, second, z: outs[role].ref.at[second, z])


def rest_product(ins, core, full, turned):
    tok, ctx, *grads = ins
    turned[...] = tok.ref[...].T
    left = turned_rows(turned, core)
    for n, grad in enumerate(grads):
        width = grad.ref.shape[1]
        if n == len(grads) - 1:
            turned[...] = ctx.ref[...].T
            left = turned_rows(turned, core)
        full[:, n * width : (n + 1) * width] = dot(left, grad.ref[...])


def rest_send_kernel(ins, outs, full, turned):
    _, _, _, core = place()
    rest_product(ins[:6], 1 - core, full, turned)
    vectors = vector_lines(ins[6:10], 1 - core)
    def target(role, second, z):
        array, at = unit(role, second, z)
        return outs[array].ref.at[at]

    cut(full, 0, 4, vectors, None, target, 1)


def rest_keep_kernel(ins, outs, full, turned):
    _, _, _, core = place()
    rest_product(ins[:6], core, full, turned)
    def came(role, second, z):
        array, at = unit(role, second, z)
        return ins[10 + array].ref[at]

    vectors = vector_lines(ins[6:10], core)
    cut(full, 0, 4, vectors, came, lambda role, second, z: (outs[2].ref.at[second] if role else outs[second].ref).at[z])


def plain(operands):
    return [(part, 0) for part in operands]


def unit(role, second, z):
    n = role * 8 + second * 4 + z
    return (0, n) if n < 6 else ((n - 1) // 5, (n - 1) % 5)


def cut_for_partner(body, name, ins, lines, scratch, cuts, after=()):
    dims = [(2, 4)] * 2 if cuts == 2 else [(6,), (5,), (5,)]
    return kernel(body, name, ins, [((*part, lines, WIDTH), BF, "", 0) for part in dims], scratch=scratch, after=after)


def cut_for_chips(body, name, ins, came, lines, scratch, cuts, after=()):
    outs = [((2, 4, lines, WIDTH), BF, "", 0)]
    outs = (outs if cuts == 1 else [((4, lines, WIDTH), BF, "", 0)] * 2) + outs
    return kernel(body, name, [*ins, *plain(came)], outs, scratch=scratch, after=after)


def halve_kernel(ins, outs):
    _, mine = spots()
    kept = ins[0].ref
    for n, second in enumerate((1 - mine, mine)):
        if len(ins) == 2:
            came = ins[1].ref[second]
        else:
            came = jnp.where(second == 0, ins[1].ref[...], ins[2].ref[...])
        value = (kept[second].astype(F32) + came.astype(F32)).astype(BF)
        if n:
            outs[-1].ref[...] = value
            continue
        size = value.shape[0] // (len(outs) - 1)
        for part, out in enumerate(outs[:-1]):
            out.ref[...] = value[part * size : (part + 1) * size]


def deal_kernel(ins, outs):
    _, _, z, core = place()
    kept, *came = [given.ref for given in ins]
    for n, far in enumerate((3, 1 + core, 2 - core, 0)):
        at = z ^ far
        if len(came) == 1:
            other = came[0][at]
        else:
            other = jnp.where(at < 2, came[0][at % 2], came[1][at % 2])
        outs[n // 2].ref[n % 2] = (kept[at].astype(F32) + other.astype(F32)).astype(BF)


def total_kernel(ins, outs):
    kept, came, last = [given.ref for given in ins]
    outs[0].ref[...] = (kept[1].astype(F32) + came[1].astype(F32) + last[...].astype(F32)).astype(BF)


def combine(body, name, operands, outs, after=(), scratch=()):
    return kernel(body, name, plain(operands), [(*out, "", 0) for out in outs], after=after, scratch=scratch)


def dp_sources(ins):
    first, second = spots()
    refs = [given.ref for given in ins]
    values = [ref[n] for ref in refs for n in range(2)] if len(refs) == 2 else [ref[...] for ref in refs]
    numbers = (2 * first + second, 2 * (1 - first) + second, 2 * first + 1 - second, 2 * (1 - first) + 1 - second)
    return [(value.astype(F32), number) for value, number in zip(values, numbers)]


def hid_final_kernel(ins, outs, full):
    size = full.shape[0] // 4
    for value, number in dp_sources(ins):
        full[pl.ds(pl.multiple_of(number * size, 16), size), :] = value
    outs[0].ref[...] = full[...].T


def in_final_kernel(ins, outs):
    for value, number in dp_sources(ins):
        outs[0].ref[:, pl.ds(pl.multiple_of(number * WIDTH, 128), WIDTH)] = value


def rest_final_kernel(questions, a, b, c, d, q, k, v, o, bq, bv, bo, bi, bh, g1, s1, g2, s2, loss, entropy):
    lines = jnp.zeros((MORE, LANES), F32)
    few = LINES // 4
    for value, number in dp_sources([Given(None, ref) for ref in (a, b, c, d)]):
        lines = lines + jnp.where(number == 0, value[LINES:, :LANES], 0.0)
        rows = pl.ds(pl.multiple_of(number * few, 8), few)
        for n, out in enumerate((q, k, v, o)):
            out[rows, :] = value[n * few : (n + 1) * few]
    for n, out in enumerate((bq, bv, bo, bh, g1, s1, g2, s2)):
        out[...] = lines[n, :LINES]
    bi[...] = jnp.concatenate([lines[8 + n : 9 + n, :LINES] for n in range(4)], axis=1).reshape(4 * LINES)
    nll, ent = jnp.sum(lines[12:13, :96]), jnp.sum(lines[12:13, 96:192])
    loss[0, 0] = (nll + ENTROPY_WEIGHT * ent) / questions
    entropy[0, 0] = ent / questions


def rest_final(pieces, questions, width):
    part, deep = width // 8, width // 2
    vectors = [shape((size,), F32) for size in (part, part, part, deep, part, part, part, part, part)]
    return pl.pallas_call(
        functools.partial(rest_final_kernel, questions),
        out_shape=[shape((part, width), F32)] * 4 + vectors + [shape((1, 1), F32)] * 2,
        in_specs=[whole()] * 4,
        out_specs=[whole()] * 13 + [whole(pltpu.SMEM)] * 2,
        compiler_params=params(12),
        cost_estimate=cost(0, MIB),
        name="rest_final",
    )(*pieces)


def halve(name, kept, *came, cuts=1, after=()):
    dims = kept.shape[1:]
    outs = [((dims[0] // cuts, *dims[1:]), BF)] * cuts + [(dims, BF)]
    return combine(halve_kernel, name, (kept, *came), outs, after=after)


def deal(name, halves, after=()):
    *send, kept = halves
    came = [exchange(part, over_plane(1)) for part in send]
    return combine(deal_kernel, name, (kept, *came), [((2, *kept.shape[1:]), BF)] * 2, after=after)


def on_this_slice(
    tokens, upstream, w_query, w_key, w_value, w_out, w_in, w_hid, b_query, b_value, b_out, b_in, b_hid,
    gain_one, shift_one, gain_two, shift_two, passages, slots, counts, gen_loglik,
):
    rows, width = tokens.shape
    deep = w_in.shape[1]
    questions = slots.shape[0] * lax.axis_size("dp")
    q_near, k_near, v_near, cls, vec_near, q, k, v, vec = project(
        (
            tokens, w_key, w_value, w_query, b_value, b_query, w_out, b_out, gain_one, shift_one, w_in, b_in, w_hid, b_hid,
            gain_two, shift_two,
        )
    )
    own = [cls] + [exchange(cls, over_z(n)) for n in (1, 2, 3)]
    p, ctx, n1, i1, low, n1_near, low_near = attend(q_near, k_near, v_near, tokens, w_out, vec_near)
    found = mark(passages, slots.T)
    mine = kernel(collect_kernel, "collect", plain(own), [((4 * cls.shape[0], width), BF, "", 0)], after=(low_near,))[0]
    record = search(mine, exchange(mine, over_core), passages, found)
    cuts = meet(record, exchange(record, over_core))
    records = [cuts[0]] + [exchange(cuts[n], over_z(n)) for n in (1, 2, 3)]
    act, slope, encoded, sum_two, back, first, sums = forward(low_near, n1_near, vec, w_in, w_hid, upstream, after=(cuts[0],))
    back, fix, lead_vec, hid_cut = lead(records, cls, counts, gen_loglik.T, first, sums, vec, back, act)
    hid_came = exchange(hid_cut, over_core)
    pre, slope_vec = slope_part(back, w_hid, slope)
    scratch = [pltpu.VMEM((4 * LINES, deep), F32), pltpu.VMEM((width, rows), BF)]
    in_cut = cut_for_partner(in_send_kernel, "in_send", plain((low, pre)), LINES, scratch, 2)
    in_came = [exchange(part, over_core) for part in in_cut]
    block = (width, deep // 8)
    hid_sent, hid_kept = kernel(
        hid_keep_kernel, "hid_keep", plain((back, act, hid_came)), [((2, *block), BF, "", 0)] * 2,
        scratch=[pltpu.VMEM((width, deep // 2), F32)], after=(in_cut[0],),
    )
    hid_came = exchange(hid_sent, over_z_by_core(0))
    attend_low, grad, descend_vec, one = descend(
        pre, w_in, fix, sum_two, n1, i1, vec, w_out, after=(hid_kept,)
    )
    into = cut_for_chips(
        in_keep_kernel, "in_keep", plain((low, pre)), in_came, LINES, scratch, 1, after=(attend_low,)
    )
    in_first = exchange(into[0], over_plane(0))
    dq, dk, dv, unattend_vec, input_grad = unattend(grad, p, q, k, v, one, w_query, w_key, w_value, after=(into[1],))
    operands = plain((tokens, ctx, dq, dk, dv, attend_low, lead_vec, slope_vec, descend_vec, unattend_vec))
    more = LINES + MORE
    rest_cut = cut_for_partner(rest_send_kernel, "rest_send", operands, more, scratch, 3)
    rest_came = [exchange(part, over_core) for part in rest_cut]
    hid_sum = combine(pair_kernel, "hid_pair", (hid_kept, hid_came), [(block, BF)], after=(rest_cut[0],))[0]
    hid_last = exchange(hid_sum, over_z_by_core(1))
    in_halves = halve("in_halve", into[1], in_first, after=(hid_sum,))
    rest = cut_for_chips(rest_keep_kernel, "rest_keep", operands, rest_came, more, scratch, 2, after=(in_halves[0],))
    rest_first = exchange(rest[0], over_plane(0)), exchange(rest[1], over_plane(0))
    in_parts = deal("in_deal", in_halves, after=(rest[2],))
    in_came = exchange(in_parts[0], over_z_by_core(0))
    rest_halves = halve("rest_halve", rest[2], *rest_first, cuts=2, after=(in_parts[0],))
    in_pair = combine(pair_kernel, "in_pair", (in_parts[1], in_came), [(in_came.shape[1:], BF)], after=(rest_halves[0],))[0]
    in_last = exchange(in_pair, over_z_by_core(1))
    size = ((width // 2, deep // 8), BF)
    hid_parts = combine(hid_deal_kernel, "hid_deal", (hid_kept, hid_came, hid_last), [size] * 2, after=(in_pair,))
    hid_first = exchange(hid_parts[0], over_plane(0))
    operands = (in_parts[1], in_came, in_last)
    in_sum = combine(total_kernel, "in_total", operands, [(in_pair.shape, BF)], after=(hid_parts[0],))[0]
    in_all = in_sum, exchange(in_sum, over_plane(0)), exchange(in_sum, over_plane(1)), exchange(in_sum, over_both)
    rest_parts = deal("rest_deal", rest_halves, after=(in_sum,))
    rest_came = exchange(rest_parts[0], over_z_by_core(0))
    size = ((width // 4, deep // 8), BF)
    hid_halves = combine(hid_halve_kernel, "hid_halve", (hid_parts[1], hid_first), [size] * 2, after=(rest_parts[0],))
    hid_second = exchange(hid_halves[0], over_plane(1))
    rest_pair = combine(pair_kernel, "rest_pair", (rest_parts[1], rest_came), [(rest_came.shape[1:], BF)], after=(hid_halves[0],))[0]
    grad_in = combine(in_final_kernel, "in_final", in_all, [((LINES, deep), F32)], after=(rest_pair,))[0]
    rest_last = exchange(rest_pair, over_z_by_core(1))
    done = pltpu.with_memory_space_constraint(grad_in, pltpu.HBM)
    mine = combine(sum_kernel, "hid_total", (hid_halves[1], hid_second), [size], after=(done,))[0]
    hid_all = mine, exchange(mine, over_plane(0)), exchange(mine, over_plane(1)), exchange(mine, over_both)
    operands = (rest_parts[1], rest_came, rest_last)
    mine = combine(total_kernel, "rest_total", operands, [(rest_pair.shape, BF)], after=(mine,))[0]
    last = mine, exchange(mine, over_plane(0)), exchange(mine, over_plane(1)), exchange(mine, over_both)
    grad_hid = combine(
        hid_final_kernel, "hid_final", hid_all, [((deep // 8, width), F32)], scratch=[pltpu.VMEM((width, deep // 8), F32)],
        after=(mine,),
    )[0]
    *rest, loss, entropy = rest_final(last, questions, width)
    return (
        encoded, input_grad, loss.reshape(()), entropy.reshape(()), *rest[:4], grad_in, grad_hid, *rest[4:],
    )


PRECISE = lax.Precision.HIGHEST


def shortened(array):

    def short(part):
        return part.astype(jnp.bfloat16) if part.dtype == jnp.float32 else part

    return jax.tree.map(short, array)


def product(left_side, right_side):
    return jnp.dot(left_side, right_side, preferred_element_type=jnp.float32)


def times_transpose(left_side, right_side):
    return lax.dot_general(
        left_side, right_side, (((1,), (1,)), ((), ())), preferred_element_type=jnp.float32
    )


def transpose_times(left_side, right_side):
    return lax.dot_general(
        left_side, right_side, (((0,), (0,)), ((), ())), preferred_element_type=jnp.float32
    )


def plain_norm_forward(values, gain_vector, offset):
    center = values - jnp.mean(values, axis=-1, keepdims=True)
    inverse = lax.rsqrt(jnp.mean(center * center, axis=-1, keepdims=True) + NORM_EPSILON)
    normed = center * inverse
    return (normed * gain_vector + offset, normed, inverse)


def plain_norm_backward(incoming, normed, inverse, gain_vector):
    scaled = incoming * gain_vector
    inner = (
        scaled
        - jnp.mean(scaled, axis=-1, keepdims=True)
        - normed * jnp.mean(scaled * normed, axis=-1, keepdims=True)
    )
    return (inverse * inner, jnp.sum(incoming * normed, axis=0), jnp.sum(incoming, axis=0))


def gelu_slope(values):
    cumulative = 0.5 * (1.0 + jax.scipy.special.erf(values * 0.7071067811865476))
    return (
        values * cumulative,
        cumulative + values * jnp.exp(-0.5 * values * values) * 0.3989422804014327,
    )


def on_any_slice(
    tokens,
    upstream,
    w_query,
    w_key,
    w_value,
    w_out,
    w_in,
    w_hid,
    b_query,
    b_value,
    b_out,
    b_in,
    b_hid,
    gain_one,
    shift_one,
    gain_two,
    shift_two,
    passages,
    slots,
    counts,
    gen_loglik,
):
    tok_rows, model_width = tokens.shape
    seq_count = tok_rows // SEQ
    heads_shape = (seq_count, SEQ, HEADS, HDIM)
    inputs = tokens.astype(jnp.float32)
    queries = (product(tokens, w_query) + b_query).astype(jnp.bfloat16).reshape(heads_shape)
    keys_all = product(tokens, w_key).astype(jnp.bfloat16).reshape(heads_shape)
    values_all = (product(tokens, w_value) + b_value).astype(jnp.bfloat16).reshape(heads_shape)
    scores = (
        jnp.einsum("bqhd,bkhd->bhqk", queries, keys_all, preferred_element_type=jnp.float32) * 0.125
    )
    peak = jnp.max(scores, axis=-1, keepdims=True)
    log_total = peak + jnp.log(jnp.sum(jnp.exp(scores - peak), axis=-1, keepdims=True))
    weights_low = jnp.exp(scores - log_total).astype(jnp.bfloat16)
    context = jnp.einsum(
        "bhqk,bkhd->bqhd", weights_low, values_all, preferred_element_type=jnp.float32
    )
    context = context.reshape(tok_rows, model_width).astype(jnp.bfloat16)
    attended = product(context, w_out) + b_out
    hidden_one, normed_one, inverse_one = plain_norm_forward(inputs + attended, gain_one, shift_one)
    hidden_low = hidden_one.astype(jnp.bfloat16)
    pre_act = product(hidden_low, w_in) + b_in
    activated, slope = gelu_slope(pre_act)
    act_low = activated.astype(jnp.bfloat16)
    branch = product(act_low, w_hid) + b_hid
    outputs, normed_two, inverse_two = plain_norm_forward(hidden_one + branch, gain_two, shift_two)
    cls_low = outputs[::SEQ].astype(jnp.bfloat16)
    index_scores = times_transpose(lax.all_gather(cls_low, "index", axis=0, tiled=True), passages)
    group_rows, local_rows = index_scores.shape
    first_row = lax.axis_index("index") * local_rows
    local_slots = slots - first_row
    onehot = (
        lax.broadcasted_iota(jnp.int32, (1, 1, local_rows), 2) == local_slots[:, :, None]
    ).astype(jnp.float32)
    picked_part = jnp.einsum("qr,qsr->qs", index_scores, onehot, precision=PRECISE)
    row_peak = jnp.max(index_scores, axis=1)
    peak_all = lax.pmax(row_peak, "index")
    total_part = jnp.sum(jnp.exp(index_scores - peak_all[:, None]), axis=1)
    total_all, picked = lax.psum((total_part, picked_part), "index")
    index_lse = peak_all + jnp.log(total_all)
    valid = lax.broadcasted_iota(jnp.int32, picked.shape, 1) < counts[:, None]
    joint = picked - index_lse[:, None] + gen_loglik
    masked = jnp.where(valid, joint, -1e30)
    best = jnp.max(masked, axis=1, keepdims=True)
    marginal = best[:, 0] + jnp.log(jnp.sum(jnp.exp(masked - best), axis=1))
    centered = jnp.where(valid, joint - marginal[:, None], 0.0)
    posterior = jnp.where(valid, jnp.exp(masked - marginal[:, None]), 0.0)
    entropy_rows = -jnp.sum(posterior * centered, axis=1)
    nll_total, entropy_total = lax.psum((jnp.sum(-marginal), jnp.sum(entropy_rows)), "dp")
    questions = group_rows * lax.axis_size("dp")
    loss = (nll_total + ENTROPY_WEIGHT * entropy_total) / questions
    entropy = entropy_total / questions
    picked_grad = jnp.where(
        valid, -posterior * (1.0 + ENTROPY_WEIGHT * (centered + entropy_rows[:, None])), 0.0
    )
    score_grad = jnp.exp(index_scores - index_lse[:, None]) + jnp.einsum(
        "qs,qsr->qr", picked_grad, onehot, precision=PRECISE
    )
    score_low = score_grad.astype(jnp.bfloat16)
    cls_grad = lax.psum_scatter(
        product(score_low, passages), "index", scatter_dimension=0, tiled=True
    )
    out_grad = (
        upstream.astype(jnp.float32).reshape(seq_count, SEQ, model_width).at[:, 0].add(cls_grad)
    )
    out_grad = out_grad.reshape(tok_rows, model_width)
    sum_two, grad_gain_two, grad_shift_two = plain_norm_backward(
        out_grad, normed_two, inverse_two, gain_two
    )
    branch_low = sum_two.astype(jnp.bfloat16)
    grad_b_hid = jnp.sum(branch_low.astype(jnp.float32), axis=0)
    grad_w_hid = transpose_times(act_low, branch_low)
    pre_low = (times_transpose(branch_low, w_hid) * slope).astype(jnp.bfloat16)
    grad_b_in = jnp.sum(pre_low.astype(jnp.float32), axis=0)
    grad_w_in = transpose_times(hidden_low, pre_low)
    sum_one, grad_gain_one, grad_shift_one = plain_norm_backward(
        sum_two + times_transpose(pre_low, w_in), normed_one, inverse_one, gain_one
    )
    attend_low = sum_one.astype(jnp.bfloat16)
    grad_b_out = jnp.sum(attend_low.astype(jnp.float32), axis=0)
    grad_w_out = transpose_times(context, attend_low)
    context_grad = times_transpose(attend_low, w_out).astype(jnp.bfloat16).reshape(heads_shape)
    scores_again = (
        jnp.einsum("bqhd,bkhd->bhqk", queries, keys_all, preferred_element_type=jnp.float32) * 0.125
    )
    weights_again = jnp.exp(scores_again - log_total)
    again_low = weights_again.astype(jnp.bfloat16)
    weight_grad = jnp.einsum(
        "bqhd,bkhd->bhqk", context_grad, values_all, preferred_element_type=jnp.float32
    )
    value_grad = jnp.einsum(
        "bhqk,bqhd->bkhd", again_low, context_grad, preferred_element_type=jnp.float32
    )
    value_grad = value_grad.reshape(tok_rows, model_width).astype(jnp.bfloat16)
    logit_grad = weights_again * (
        weight_grad - jnp.sum(weight_grad * weights_again, axis=-1, keepdims=True)
    )
    logit_low = logit_grad.astype(jnp.bfloat16)
    query_grad = (
        jnp.einsum("bhqk,bkhd->bqhd", logit_low, keys_all, preferred_element_type=jnp.float32)
        * 0.125
    )
    query_grad = query_grad.reshape(tok_rows, model_width).astype(jnp.bfloat16)
    key_grad = (
        jnp.einsum("bhqk,bqhd->bkhd", logit_low, queries, preferred_element_type=jnp.float32)
        * 0.125
    )
    key_grad = key_grad.reshape(tok_rows, model_width).astype(jnp.bfloat16)
    input_grad = (
        sum_one
        + times_transpose(query_grad, w_query)
        + times_transpose(key_grad, w_key)
        + times_transpose(value_grad, w_value)
    ).astype(jnp.bfloat16)
    grad_w_query = transpose_times(tokens, query_grad)
    grad_w_key = transpose_times(tokens, key_grad)
    grad_w_value = transpose_times(tokens, value_grad)
    grad_b_query = jnp.sum(query_grad.astype(jnp.float32), axis=0)
    grad_b_value = jnp.sum(value_grad.astype(jnp.float32), axis=0)
    shares = (
        lax.psum_scatter(grad_w_query, "index", scatter_dimension=0, tiled=True),
        lax.psum_scatter(grad_w_key, "index", scatter_dimension=0, tiled=True),
        lax.psum_scatter(grad_w_value, "index", scatter_dimension=0, tiled=True),
        lax.psum_scatter(grad_w_out, "index", scatter_dimension=0, tiled=True),
        lax.psum_scatter(grad_w_in, "index", scatter_dimension=0, tiled=True),
        lax.psum_scatter(grad_w_hid, "index", scatter_dimension=0, tiled=True),
        lax.psum_scatter(grad_b_query, "index", scatter_dimension=0, tiled=True),
        lax.psum_scatter(grad_b_value, "index", scatter_dimension=0, tiled=True),
        lax.psum_scatter(grad_b_out, "index", scatter_dimension=0, tiled=True),
        lax.psum_scatter(grad_b_in, "index", scatter_dimension=0, tiled=True),
        lax.psum_scatter(grad_b_hid, "index", scatter_dimension=0, tiled=True),
        lax.psum_scatter(grad_gain_one, "index", scatter_dimension=0, tiled=True),
        lax.psum_scatter(grad_shift_one, "index", scatter_dimension=0, tiled=True),
        lax.psum_scatter(grad_gain_two, "index", scatter_dimension=0, tiled=True),
        lax.psum_scatter(grad_shift_two, "index", scatter_dimension=0, tiled=True),
    )
    summed = jax.tree.map(
        lambda part: part.astype(jnp.float32), lax.psum(shortened(tuple(shares)), "dp")
    )
    return (outputs.astype(jnp.bfloat16), input_grad, loss, entropy) + tuple(summed)


def solution(mesh):
    here = (mesh.shape["dp"], mesh.shape["index"]) == (4, 8)
    return jax.shard_map(
        on_this_slice if here else on_any_slice,
        mesh=mesh,
        in_specs=(
            P(("dp", "index"), None),
            P(("dp", "index"), None),
            P(),
            P(),
            P(),
            P(),
            P(),
            P(),
            P(),
            P(),
            P(),
            P(),
            P(),
            P(),
            P(),
            P(),
            P(),
            P("index", None),
            P("dp", None),
            P("dp"),
            P("dp", None),
        ),
        out_specs=(
            P(("dp", "index"), None),
            P(("dp", "index"), None),
            P(),
            P(),
            P("index", None),
            P("index", None),
            P("index", None),
            P("index", None),
            P("index", None),
            P("index", None),
            P("index"),
            P("index"),
            P("index"),
            P("index"),
            P("index"),
            P("index"),
            P("index"),
            P("index"),
            P("index"),
        ),
        check_vma=False,
    )
```
